128 devices in a mesh: seq: 32 (over z, y_lo, x), win: 4 (over y_hi, core).
Axes of the slice: x: 4, y: 4 (y_hi: 2, y_lo: 2; y = y_hi * 2 + y_lo), z: 4, core: 2. Of those that a mesh axis runs over, the one named last changes fastest.
Arguments:
- tokens: bfloat16 [4, 4096, 768], P('win', 'seq'), may hold values from -6 to 6
- file_lengths: int32 [4, 8], P('win'), may hold values from 1 to 3969, 4032 in all within a row
- upstream: bfloat16 [4, 4096, 768], P('win', 'seq'), may hold values from -6 to 6
- pre_gain: bfloat16 [768], P(('seq', 'win')), may hold values from 0.5 to 1.5
- pre_shift: bfloat16 [768], P(('seq', 'win')), may hold values from -1.5 to 1.5
- query_weight: bfloat16 [768, 768], P(('seq', 'win')), may hold values from -0.21875 to 0.21875
- query_bias: bfloat16 [768], P(('seq', 'win')), may hold values from -1.5 to 1.5
- keyval_weight: bfloat16 [768, 128], P(('seq', 'win')), may hold values from -0.21875 to 0.21875
- value_bias: bfloat16 [64], replicated, may hold values from -0.099609375 to 0.099609375
- mixer_weight: bfloat16 [768, 768], P(('seq', 'win')), may hold values from -3.5 to 3.5
- mixer_bias: bfloat16 [768], P(('seq', 'win')), may hold values from -1.5 to 1.5
- mid_gain: bfloat16 [768], P(('seq', 'win')), may hold values from 0.5 to 1.5
- middle_norm_bias: bfloat16 [768], P(('seq', 'win')), may hold values from -1.5 to 1.5
- expand_weight: bfloat16 [768, 3072], P(('seq', 'win')), may hold values from -0.21875 to 0.21875
- expand_bias: bfloat16 [3072], P(('seq', 'win')), may hold values from -1.5 to 1.5
- shrink_weight: bfloat16 [3072, 768], P(('seq', 'win')), may hold values from -0.109375 to 0.109375
- shrink_bias: bfloat16 [768], P(('seq', 'win')), may hold values from -1.5 to 1.5
Outputs:
- result: float32 [4, 4096, 768], P('win', 'seq')
- tokens_grad: float32 [4, 4096, 768], P('win', 'seq')
- prenorm_gain_gradient: float32 [768], P(('seq', 'win'))
- prenorm_bias_gradient: float32 [768], P(('seq', 'win'))
- queryweight_grad: float32 [768, 768], P(('seq', 'win'))
- querybias_grad: float32 [768], P(('seq', 'win'))
- keyval_grad: float32 [768, 128], P(('seq', 'win'))
- valuebias_grad: float32 [64], replicated
- mixerweight_grad: float32 [768, 768], P(('seq', 'win'))
- mixerbias_grad: float32 [768], P(('seq', 'win'))
- midgain_grad: float32 [768], P(('seq', 'win'))
- midshift_grad: float32 [768], P(('seq', 'win'))
- expandweight_grad: float32 [768, 3072], P(('seq', 'win'))
- expandbias_grad: float32 [3072], P(('seq', 'win'))
- shrinkweight_grad: float32 [3072, 768], P(('seq', 'win'))
- shrinkbias_grad: float32 [768], P(('seq', 'win'))
The draws below stay inside these ranges and needn't reach their ends.
Inputs may be any that keep to these rules, and one draw needn't show every extreme that they name: `file_lengths`: in each window the 8 lengths sum to 4032, so that the window ends in padding, and the longest is exactly 3969.
All inputs are finite; a program needn't handle non-finite values.
Results may differ from the reference program's by a relative error of at most 0.014.
Values may be sent and summed in bfloat16 or wider, within the bound.
No kernel may reach another device: no remote copies, remote signals or barrier semaphores. Data moves between devices by JAX's collectives and lax.ppermute only.
A program may use at most 128 MiB of HBM per device.

```python
import math
import jax
import jax.numpy as jnp
import numpy as np
from jax import lax

D = 768
H = 12
HD = 64
FF = 3072
NDOC = 8
TOK_DEV = 128
WINDOWS = 4
WINDOW = 4096


def steps_of(key, dims, cuts, low, largest):
    factor_of, own = 1.0, jax.random.fold_in(key, 6)
    for axis_at, shards_of in cuts:
        steps = jnp.exp(jax.random.uniform(jax.random.fold_in(own, axis_at), (shards_of,), jnp.float32, low / len(cuts), largest / len(cuts)))
        factor_of = factor_of * jnp.repeat(steps, dims[axis_at] // shards_of).reshape([-1 if axis == axis_at else 1 for axis in range(len(dims))])
    return factor_of


def profile(amount, total, limit, lean):
    weights = [(1 << 20) // math.isqrt(rank ** lean) + 1 for rank in range(2, amount + 1)]
    surplus, counts = total - limit - (amount - 1), [1] * (amount - 1)
    while surplus > 0:
        movable = [i for i in range(amount - 1) if counts[i] < limit]
        mass, budget = sum([weights[i] for i in movable]), surplus
        for i in movable:
            extra = min(limit - counts[i], max(1, budget * weights[i] // mass), surplus)
            counts[i] = counts[i] + extra
            surplus = surplus - extra
    return np.array([limit] + counts)


def ragged(key, count, total, most, skew):
    if count == 2:
        one = jax.random.randint(key, (), max(1, total - most), min(most, total - 1) + 1)
        return jnp.stack([one, total - one])
    sizes = jnp.asarray(profile(count, total, most, skew), jnp.int32)
    twos = (count - 1) // 2
    source_of, taker = sizes[1:1 + 2 * twos:2], sizes[2:2 + 2 * twos:2]
    slack = jnp.minimum(source_of - 1, most - taker)
    shifted = jax.random.randint(jax.random.fold_in(key, 1), (twos,), 0, 1 << 20) % (slack + 1)
    sizes = sizes.at[1:1 + 2 * twos:2].set(source_of - shifted).at[2:2 + 2 * twos:2].set(taker + shifted)
    return sizes[jax.random.permutation(jax.random.fold_in(key, 2), count)]


def centred(key, dims, scale, reach, pieces=(), kind=jnp.bfloat16):
    values = jax.random.normal(key, dims, jnp.float32) * scale
    if len(pieces) > 0:
        values = steps_of(key, dims, pieces, -0.22, 0.18) * values
    return jnp.clip(values, min=-reach, max=reach).astype(kind)


def setup_inputs(seed: int = 0) -> dict:
    streams_of = jax.random.split(jax.random.key(seed), 18)
    tokens = centred(streams_of[0], (WINDOWS, WINDOW, D), 1.0, 6.0, ((0, 4), (1, 32)))
    file_lengths = jax.vmap(lambda own: ragged(own, NDOC, WINDOW - TOK_DEV // 2, WINDOW - TOK_DEV + 1, 2))(jax.random.split(streams_of[1], WINDOWS)).reshape((WINDOWS, NDOC)).astype(jnp.int32)
    upstream = centred(streams_of[2], (WINDOWS, WINDOW, D), 1.0, 6.0, ((0, 4), (1, 32)))
    pre_gain = jnp.clip(1.0 + 0.1 * jax.random.normal(streams_of[3], (D,), jnp.float32), 0.5, 1.5).astype(jnp.bfloat16)
    pre_shift = centred(streams_of[4], (D,), 0.3, 1.5, ((0, 128),))
    query_weight = centred(streams_of[5], (D, D), D ** -0.5, 0.21875, ((0, 128),))
    query_bias = centred(streams_of[6], (D,), 0.3, 1.5, ((0, 128),))
    keyval_weight = centred(streams_of[7], (D, 2 * HD), D ** -0.5, 0.21875, ((0, 128),))
    value_bias = centred(streams_of[8], (HD,), 0.02, 0.099609375)
    mixer_weight = centred(streams_of[9], (D, D), (max(1, 16 * D // WINDOW)) ** -0.5, 3.5, ((0, 128),))
    mixer_bias = centred(streams_of[10], (D,), 0.3, 1.5, ((0, 128),))
    mid_gain = jnp.clip(1.0 + 0.1 * jax.random.normal(streams_of[11], (D,), jnp.float32), 0.5, 1.5).astype(jnp.bfloat16)
    middle_norm_bias = centred(streams_of[12], (D,), 0.3, 1.5, ((0, 128),))
    expand_weight = centred(streams_of[13], (D, FF), D ** -0.5, 0.21875, ((0, 128),))
    expand_bias = centred(streams_of[14], (FF,), 0.3, 1.5, ((0, 128),))
    shrink_weight = centred(streams_of[15], (FF, D), FF ** -0.5, 0.109375, ((0, 128),))
    shrink_bias = centred(streams_of[16], (D,), 0.3, 1.5, ((0, 128),))
    return {"tokens": tokens, "file_lengths": file_lengths, "upstream": upstream, "pre_gain": pre_gain, "pre_shift": pre_shift, "query_weight": query_weight, "query_bias": query_bias, "keyval_weight": keyval_weight, "value_bias": value_bias, "mixer_weight": mixer_weight, "mixer_bias": mixer_bias, "mid_gain": mid_gain, "middle_norm_bias": middle_norm_bias, "expand_weight": expand_weight, "expand_bias": expand_bias, "shrink_weight": shrink_weight, "shrink_bias": shrink_bias}


@jax.custom_vjp
def low(v):
    return lax.optimization_barrier(v.astype(jnp.bfloat16)).astype(jnp.float32)

@jax.custom_vjp
def low_back(v):
    return v

def low_keep(v):
    return (low(v), None)

def low_pass(kept, grad):
    return (grad,)

def back_keep(v):
    return (v, None)

def back_low(kept, grad):
    return (low(grad),)
low.defvjp(low_keep, low_pass)
low_back.defvjp(back_keep, back_low)

def apply_layer_norm(value, gain, shift):
    mean = lax.optimization_barrier(jnp.mean(value, axis=-1, keepdims=True))
    centered = value - mean
    spread = lax.optimization_barrier(jnp.mean(centered * centered, axis=-1, keepdims=True))
    return centered * lax.rsqrt(spread + 1e-05) * gain + shift

def product(left, right):
    return jnp.dot(left, right, precision=lax.Precision.HIGHEST)

def file_index(positions, ends):
    return lax.optimization_barrier(jnp.sum((positions[:, None] >= ends[None, :]).astype(jnp.int32), axis=1)).astype(jnp.int32)

def open_keys(query_pos, query_file, key_pos, key_file):
    same = query_file[:, None] == key_file[None, :]
    before = key_pos[None, :] <= query_pos[:, None]
    inside = (query_file[:, None] < NDOC) | (key_pos[None, :] == query_pos[:, None])
    return same & before & inside

def block_forward(params, window_tokens, lengths):
    pre_gain, pre_shift, query_weight, query_bias, keyval_weight, value_bias, mixer_weight, mixer_bias, mid_gain, middle_norm_bias, expand_weight, expand_bias, shrink_weight, shrink_bias = params
    normed = low(apply_layer_norm(window_tokens, pre_gain, pre_shift))
    query = low(low_back(product(normed, query_weight) + query_bias))
    kv_shift = jnp.concatenate([jnp.zeros((HD,), jnp.float32), value_bias])
    keyval = low(low_back(product(normed, keyval_weight) + kv_shift))
    keys = keyval[:, :HD]
    values = keyval[:, HD:]
    qblock = min(512, WINDOW)
    positions = jnp.arange(WINDOW, dtype=jnp.int32)
    ends = jnp.cumsum(lengths).astype(jnp.int32)
    files = file_index(positions, ends)
    scale = 1.0 / math.sqrt(HD)

    def attend(items):
        query_rows, query_pos, query_file = items
        raw = low_back(jnp.einsum('thd,kd->thk', query_rows, keys, precision=lax.Precision.HIGHEST) * scale)
        mask = open_keys(query_pos, query_file, positions, files)
        masked = jnp.where(mask[:, None, :], raw, -jnp.inf)
        probs = low(jax.nn.softmax(masked, axis=-1))
        return jnp.einsum('thk,kd->thd', probs, values, precision=lax.Precision.HIGHEST)
    query_blocks = query.reshape(WINDOW // qblock, qblock, H, HD)
    attended = lax.map(jax.checkpoint(attend), (query_blocks, positions.reshape(-1, qblock), files.reshape(-1, qblock)))
    attended = low(low_back(attended.reshape(WINDOW, D)))
    hidden = window_tokens + low_back(product(attended, mixer_weight)) + mixer_bias
    normed_mid = low(apply_layer_norm(hidden, mid_gain, middle_norm_bias))
    preact = low_back(product(normed_mid, expand_weight) + expand_bias)
    activated = low(jax.nn.gelu(preact, approximate=True))
    return hidden + low_back(product(activated, shrink_weight)) + shrink_bias

def reference(tokens, file_lengths, upstream, pre_gain, pre_shift, query_weight, query_bias, keyval_weight, value_bias, mixer_weight, mixer_bias, mid_gain, middle_norm_bias, expand_weight, expand_bias, shrink_weight, shrink_bias):
    params = tuple((item.astype(jnp.float32) for item in (pre_gain, pre_shift, query_weight, query_bias, keyval_weight, value_bias, mixer_weight, mixer_bias, mid_gain, middle_norm_bias, expand_weight, expand_bias, shrink_weight, shrink_bias)))

    def one_window(carry, items):
        window_tokens, lengths, window_up = items
        output, backward = jax.vjp(lambda weights, inputs: block_forward(weights, inputs, lengths), params, window_tokens.astype(jnp.float32))
        weight_grads, input_grad = backward(window_up.astype(jnp.float32))
        carry = jax.tree.map(lambda first, second: first + second, carry, weight_grads)
        return (carry, (output, input_grad))
    start = jax.tree.map(jnp.zeros_like, params)
    grads, outputs = lax.scan(one_window, start, (tokens, file_lengths, upstream))
    result, tokens_grad = outputs
    return (result, tokens_grad, grads[0], grads[1], grads[2], grads[3], grads[4], grads[5], grads[6], grads[7], grads[8], grads[9], grads[10], grads[11], grads[12], grads[13])
```

```python
import functools
import math

import jax
import jax.numpy as jnp
from jax import lax
from jax.experimental import pallas as pl
from jax.experimental.pallas import tpu as pltpu
from jax.sharding import Mesh, PartitionSpec as P

bf16 = jnp.bfloat16
f32 = jnp.float32
D = 768
H = 12
HD = 64
T = 128
HT = 64
WINDOW = 4096
NSEQ = 32
ROWS = H * HT
BK = 256
GRP = 256
NEG = -1e30
EPS = 1e-5
SEQ = ("z", "yl", "x")
WIN = ("yh", "c")
CHIPS = ("z", "yl", "x", "yh")
SLICE = ("yl", "x", "yh")
Q0, KV0, O0, V0, AW = 0, 768, 896, 1664, 1792
VMEM = pl.BlockSpec(memory_space=pltpu.VMEM)
SMEM = pl.BlockSpec(memory_space=pltpu.SMEM)


def dot(a, b):
    return jnp.dot(a, b, preferred_element_type=f32)


def dot_nt(a, b):
    return lax.dot_general(a, b, (((1,), (1,)), ((), ())), preferred_element_type=f32)


def dot_tn(a, b):
    return lax.dot_general(a, b, (((0,), (0,)), ((), ())), preferred_element_type=f32)


def call(kernel, outs, args, specs, scratch=(), flops=0, nbytes=0, limit=40, aliases=None):
    return pl.pallas_call(
        kernel,
        out_shape=[jax.ShapeDtypeStruct(s, d) for s, d in outs],
        in_specs=specs,
        out_specs=[VMEM] * len(outs),
        scratch_shapes=list(scratch),
        input_output_aliases=aliases or {},
        compiler_params=pltpu.CompilerParams(vmem_limit_bytes=limit * 1024 * 1024),
        cost_estimate=pl.CostEstimate(flops=flops, bytes_accessed=nbytes, transcendentals=0),
    )(*args)


def normalize(v):
    mean = jnp.mean(v, axis=-1, keepdims=True)
    centered = v - mean
    spread = jnp.mean(centered * centered, axis=-1, keepdims=True)
    rstd = lax.rsqrt(spread + EPS)
    return centered * rstd, rstd


def norm_back(xhat, rstd, d_out, gain):
    d_hat = d_out * gain
    return rstd * (
        d_hat
        - jnp.mean(d_hat, axis=-1, keepdims=True)
        - xhat * jnp.mean(d_hat * xhat, axis=-1, keepdims=True)
    )


def first_kernel(x_ref, wm_ref, wo_ref, pad_ref, pe_ref, vb_ref, kv_ref, normed_ref, npad_ref, vec_ref):
    chunk_t = jnp.concatenate(
        [wm_ref[:, V0:].astype(f32).T, wo_ref[:, V0:].astype(f32).T], axis=1
    ).astype(bf16)
    vecs = dot_nt(chunk_t, pad_ref[...])
    ebs = dot_nt(chunk_t, pe_ref[...])
    which = lax.broadcasted_iota(jnp.int32, (1, D), 1) % 24 % 4
    eb = jnp.zeros((1, D), f32)
    for k in range(4):
        eb = eb + jnp.where(which == k, ebs[8 + k : 9 + k], 0.0)
    vec_ref[0:8] = vecs[0:8]
    vec_ref[8:16] = jnp.broadcast_to(eb, (8, D))
    xhat, _ = normalize(x_ref[...].astype(f32))
    normed = (xhat * vecs[0:1] + vecs[1:2]).astype(bf16)
    normed_ref[...] = normed
    npad = dot(normed, pad_ref[...])
    ones = lax.broadcasted_iota(jnp.int32, (1, 1024), 1) % 8 == 6
    npad = jnp.where(ones, 1.0, npad).astype(bf16)
    npad_ref[...] = npad
    kv = dot(npad[:, :512], wm_ref[:, KV0:O0]) + dot(npad[:, 512:], wo_ref[:, KV0:O0])
    kv = (kv + vb_ref[...]).astype(bf16)
    for i in range(NSEQ):
        kv_ref[i] = kv


def pack_cols(xt, g):
    return jnp.concatenate(
        [xt[h * HD : (h + 1) * HD, g * HT : (g + 1) * HT] for h in range(H)], axis=1
    )


def pack_rows(x, g):
    return jnp.concatenate(
        [x[g * HT : (g + 1) * HT, h * HD : (h + 1) * HD] for h in range(H)], axis=0
    )


def unpack(y):
    yt = y.T
    return jnp.concatenate([yt[h * HT : (h + 1) * HT] for h in range(H)], axis=1)


def query_kernel(normed_ref, wm_ref, wo_ref, pad_ref, vec_ref, wnat_ref, qt_ref, qr_ref):
    for lo in (0, 256, 512):
        rows = pl.ds(lo, 256)
        wnat_ref[rows, :] = (
            dot(pad_ref[rows, :512], wm_ref[:, :V0]) + dot(pad_ref[rows, 512:], wo_ref[:, :V0])
        ).astype(bf16)
    q = (dot(normed_ref[...], wnat_ref[:, Q0:KV0]) + vec_ref[2:3]).astype(bf16).astype(f32)
    q = q * (1.0 / math.sqrt(HD))
    qt = q.T
    for g in range(2):
        qt_ref[g, :HD, :] = pack_cols(qt, g).astype(bf16)
        qt_ref[g, HD:, :] = jnp.zeros((HD, ROWS), bf16)
        rows = pack_rows(q, g)
        qr_ref[g] = jnp.concatenate([rows, jnp.zeros((ROWS, HD), f32)], axis=1).astype(bf16)


def masked_scores(s, k0, info_ref, g, cols):
    j = k0 + lax.broadcasted_iota(jnp.int32, s.shape, 0)
    return (j >= info_ref[g, 1:2, cols]) & (j <= info_ref[g, 0:1, cols])


def over_blocks(scal_ref, g, block):
    b = g * 4
    lo, u0, u1, end = scal_ref[b], scal_ref[b + 1], scal_ref[b + 2], scal_ref[b + 3]

    def run(first, last, masked):
        def step(kb, carry):
            block(kb, masked)
            return carry

        lax.fori_loop(first, last, step, 0)

    run(lo, u0, True)
    run(u0, u1, False)
    run(u1, end, True)


def forward_kernel(
    qt_ref, kv_ref, info_ref, scal_ref, x_ref, wnat_ref, vec_ref,
    ot_ref, lse_ref, att_ref, hid_ref, mid_ref, kvs_ref, kvt_ref,
    m_ref, l_ref,
):
    for i in range(NSEQ):
        blk = jnp.concatenate([kv_ref[i, :HT], kv_ref[NSEQ - 1 - i, HT:]], axis=0)
        kvs_ref[pl.ds(i * T, T), :] = blk
        kvt_ref[:, pl.ds(i * T, T)] = blk.astype(f32).T.astype(bf16)
    m_ref[...] = jnp.full(m_ref.shape, NEG, f32)
    l_ref[...] = jnp.zeros(l_ref.shape, f32)
    ot_ref[...] = jnp.zeros(ot_ref.shape, f32)

    def group(g, carry):
        def block(kb, masked):
            k0 = pl.multiple_of(kb * BK, BK)
            kvb = kvs_ref[pl.ds(k0, BK), :]
            vt = kvt_ref[HD:, pl.ds(k0, BK)]
            for i in range(ROWS // GRP):
                cols = slice(i * GRP, (i + 1) * GRP)
                s = dot(kvb, qt_ref[g, :, cols])
                if masked:
                    s = jnp.where(masked_scores(s, k0, info_ref, g, cols), s, NEG)
                m_old = m_ref[g, :, cols]
                m_new = jnp.maximum(m_old, jnp.max(s, axis=0, keepdims=True))
                p = jnp.exp(s - m_new)
                alpha = jnp.exp(m_old - m_new)
                m_ref[g, :, cols] = m_new
                l_ref[g, :, cols] = l_ref[g, :, cols] * alpha + jnp.sum(p, axis=0, keepdims=True)
                ot_ref[g, :, cols] = ot_ref[g, :, cols] * alpha + dot(vt, p.astype(bf16))

        over_blocks(scal_ref, g, block)
        return carry

    lax.fori_loop(0, 2, group, 0)
    for g in range(2):
        o = ot_ref[g] / l_ref[g]
        ot_ref[g] = o
        lse_ref[g] = m_ref[g] + jnp.log(l_ref[g])
        att_ref[g * HT : (g + 1) * HT, :] = unpack(o).astype(bf16)
    hidden = x_ref[...].astype(f32) + dot(att_ref[...], wnat_ref[:, O0:V0]) + vec_ref[3:4]
    hid_ref[...] = hidden
    xhat, _ = normalize(hidden)
    mid_ref[...] = (xhat * vec_ref[4:5] + vec_ref[5:6]).astype(bf16)


def mlp_kernel(
    n0, n1, n2, n3, u0, u1, u2, u3, mm_ref, mo_ref, pm_ref, vec_ref,
    d0, d1, d2, d3, act_ref, dp_ref, we_ref, n_ref, u_ref,
):
    for k, (n, u) in enumerate(((n0, u0), (n1, u1), (n2, u2), (n3, u3))):
        n_ref[pl.ds(k * T, T), :] = n[...]
        u_ref[pl.ds(k * T, T), :] = u[...]
    for lo in (0, 384):
        cols = pl.ds(lo, 384)
        back = pl.ds(384 - lo, 384)
        we_ref[:, cols] = (
            dot(pm_ref[:, :384], mm_ref[:, cols]) + dot(pm_ref[:, 384:], mo_ref[:, back])
        ).astype(bf16)
    c0 = math.sqrt(2.0 / math.pi)
    for lo, half in ((0, mm_ref), (384, mo_ref)):
        cols = pl.ds(lo, 384)
        pre = dot(n_ref[...], we_ref[:, cols]) + vec_ref[8:9, cols]
        da = dot_nt(u_ref[...], half[:, D:])
        sq = pre * pre
        th = jnp.tanh(c0 * pre * (1.0 + 0.044715 * sq))
        up = 0.5 * (1.0 + th)
        act_ref[:, cols] = (pre * up).astype(bf16)
        slope = up + 0.5 * pre * (1.0 - th * th) * (c0 * (1.0 + 3 * 0.044715 * sq))
        dp_ref[:, cols] = (slope * da).astype(bf16)
    dm = dot_nt(dp_ref[...], we_ref[...])
    for k, d in enumerate((d0, d1, d2, d3)):
        d[...] = dm[k * T : (k + 1) * T].astype(bf16)


def mlp_grads_kernel(
    act_ref, dp_ref, n_ref, u_ref, mm_ref, mo_ref, pm_ref,
    r0, r1, r2, r3, gm_ref, go_ref, eb_ref,
):
    out = dot(act_ref[:, :384], mm_ref[:, D:]) + dot(act_ref[:, 384:], mo_ref[:, D:])
    for k, r in enumerate((r0, r1, r2, r3)):
        r[...] = out[k * T : (k + 1) * T].astype(bf16)
    np_mine = dot(n_ref[...], pm_ref[:, :384]).astype(bf16)
    np_other = dot(n_ref[...], pm_ref[:, 384:]).astype(bf16)
    gm_ref[:, :D] = dot_tn(np_mine, dp_ref[...]).astype(bf16)
    go_ref[:, :384] = dot_tn(np_other, dp_ref[:, 384:]).astype(bf16)
    go_ref[:, 384:D] = dot_tn(np_other, dp_ref[:, :384]).astype(bf16)
    gm_ref[:, D:] = dot_tn(act_ref[:, :384], u_ref[...]).astype(bf16)
    go_ref[:, D:] = dot_tn(act_ref[:, 384:], u_ref[...]).astype(bf16)
    eb_ref[...] = jnp.sum(dp_ref[...].astype(f32), axis=0, keepdims=True)


def backward_kernel(
    d0, d1, d2, d3, hid_ref, up_ref, vec_ref, wnat_ref, ot_ref, lse_ref,
    qt_ref, qr_ref, kvs_ref, kvt_ref, info_ref, scal_ref,
    dkv_ref, dq_ref, dhid_ref, dhl_ref, sums_ref,
    dot_ref, dor_ref, delta_ref, dkv_acc, dqt_ref,
):
    d_mid = (
        d0[...].astype(f32) + d1[...].astype(f32) + d2[...].astype(f32) + d3[...].astype(f32)
    )
    xhat, rstd = normalize(hid_ref[...])
    up = up_ref[...].astype(f32)
    d_hidden = up + norm_back(xhat, rstd, d_mid, vec_ref[4:5])
    dhid_ref[...] = d_hidden
    d_low = d_hidden.astype(bf16)
    dhl_ref[...] = d_low
    d_att = dot_nt(d_low, wnat_ref[:, O0:V0]).astype(bf16).astype(f32)
    sums_ref[...] = jnp.concatenate(
        [
            jnp.sum(d_hidden, axis=0, keepdims=True),
            jnp.sum(d_mid * xhat, axis=0, keepdims=True),
            jnp.sum(d_mid, axis=0, keepdims=True),
            jnp.sum(up, axis=0, keepdims=True),
            jnp.zeros((4, D), f32),
        ],
        axis=0,
    )
    d_att_t = d_att.T
    for g in range(2):
        cols = pack_cols(d_att_t, g)
        delta_ref[g] = jnp.sum(cols * ot_ref[g], axis=0, keepdims=True)
        dot_ref[g, :HD, :] = jnp.zeros((HD, ROWS), bf16)
        dot_ref[g, HD:, :] = cols.astype(bf16)
        rows = pack_rows(d_att, g)
        dor_ref[g] = jnp.concatenate([jnp.zeros((ROWS, HD), f32), rows], axis=1).astype(bf16)
    dkv_acc[...] = jnp.zeros(dkv_acc.shape, f32)
    dqt_ref[...] = jnp.zeros(dqt_ref.shape, f32)

    def group(g, carry):
        def block(kb, masked):
            k0 = pl.multiple_of(kb * BK, BK)
            kvb = kvs_ref[pl.ds(k0, BK), :]
            kt = kvt_ref[:HD, pl.ds(k0, BK)]
            acc = dkv_acc[pl.ds(k0, BK), :]
            for i in range(ROWS // GRP):
                cols = slice(i * GRP, (i + 1) * GRP)
                s = dot(kvb, qt_ref[g, :, cols])
                p = jnp.exp(s - lse_ref[g, :, cols])
                if masked:
                    p = jnp.where(masked_scores(s, k0, info_ref, g, cols), p, 0.0)
                dp = dot(kvb, dot_ref[g, :, cols])
                ds = (p * (dp - delta_ref[g, :, cols])).astype(bf16)
                acc = acc + dot(p.astype(bf16), dor_ref[g, cols, :]) + dot(ds, qr_ref[g, cols, :])
                dqt_ref[g, :, cols] += dot(kt, ds)
            dkv_acc[pl.ds(k0, BK), :] = acc

        over_blocks(scal_ref, g, block)
        return carry

    lax.fori_loop(0, 2, group, 0)
    for g in range(2):
        dq_ref[g * HT : (g + 1) * HT, :] = (unpack(dqt_ref[g]) * (1.0 / math.sqrt(HD))).astype(bf16)
    for i in range(NSEQ):
        dkv_ref[i, :HT, :] = dkv_acc[pl.ds(i * T, HT), :].astype(bf16)
        dkv_ref[NSEQ - 1 - i, HT:, :] = dkv_acc[pl.ds(i * T + HT, HT), :].astype(bf16)


def weight_grads_kernel(npad_ref, att_ref, pad_ref, dq_ref, dhl_ref, gm_ref, go_ref):
    apad = dot(att_ref[...], pad_ref[...]).astype(bf16)
    for lo, out in ((0, gm_ref), (512, go_ref)):
        out[:, Q0:KV0] = dot_tn(npad_ref[:, lo : lo + 512], dq_ref[...]).astype(bf16)
        out[:, O0:V0] = dot_tn(apad[:, lo : lo + 512], dhl_ref[...]).astype(bf16)


def last_kernel(
    got_ref, npad_ref, dq_ref, wnat_ref, pad_ref, pe_ref, x_ref, vec_ref, dhid_ref, sums_ref, eb_ref,
    gm_in, go_in, tg_ref, gm_ref, go_ref,
):
    total = got_ref[0].astype(f32)
    for i in range(1, NSEQ):
        total = total + got_ref[i].astype(f32)
    owned = total.astype(bf16)
    d_normed = dot_nt(dq_ref[...], wnat_ref[:, Q0:KV0]) + dot_nt(owned, wnat_ref[:, KV0:O0])
    xhat, rstd = normalize(x_ref[...].astype(f32))
    tg_ref[...] = dhid_ref[...] + norm_back(xhat, rstd, d_normed, vec_ref[0:1])
    rows = jnp.concatenate(
        [
            jnp.sum(d_normed * xhat, axis=0, keepdims=True),
            jnp.sum(d_normed, axis=0, keepdims=True),
            jnp.sum(dq_ref[...].astype(f32), axis=0, keepdims=True),
            sums_ref[0:1],
            sums_ref[1:2],
            sums_ref[2:3],
            sums_ref[3:4],
            jnp.zeros((1, D), f32),
        ],
        axis=0,
    ).astype(bf16)
    which = lax.broadcasted_iota(jnp.int32, (8, D), 1) % 24 % 4
    row = lax.broadcasted_iota(jnp.int32, (8, D), 0)
    ebs = jnp.where(which == row, jnp.broadcast_to(eb_ref[...], (8, D)), 0.0).astype(bf16)
    packed = jnp.concatenate(
        [dot(rows, pad_ref[...]), dot(ebs, pe_ref[...]), jnp.zeros((112, 1024), f32)], axis=0
    ).T
    for lo, out, given in ((0, gm_ref, gm_in), (512, go_ref, go_in)):
        out[:, KV0:O0] = dot_tn(npad_ref[:, lo : lo + 512], owned).astype(bf16)
        out[:, V0:] = packed[lo : lo + 512].astype(bf16)
        out[:, Q0:KV0] = given[:, Q0:KV0]
        out[:, O0:V0] = given[:, O0:V0]


def shift(value, axis, by):
    size = lax.axis_size(axis)
    return lax.ppermute(value, axis, [(i, (i + by) % size) for i in range(size)])


def gather(block, axes):
    count = math.prod(lax.axis_size(a) for a in axes)
    spread = jnp.broadcast_to(block[None], (count,) + block.shape)
    return lax.all_to_all(spread, axes, 0, 0, tiled=True)


def body(
    tokens,
    file_lengths,
    upstream,
    pre_gain,
    pre_shift,
    query_weight,
    query_bias,
    keyval_weight,
    value_bias,
    mixer_weight,
    mixer_bias,
    mid_gain,
    middle_norm_bias,
    expand_weight,
    expand_bias,
    shrink_weight,
    shrink_bias,
):
    z = lax.axis_index("z")
    c = lax.axis_index("c")
    seq = lax.axis_index(SEQ)
    mirror = [(i, NSEQ - 1 - i) for i in range(NSEQ)]

    vectors = jnp.stack(
        [pre_gain, pre_shift, query_bias, mixer_bias, mid_gain, middle_norm_bias, shrink_bias], axis=1
    )
    vectors = jnp.concatenate(
        [vectors, jnp.zeros((6, 1), bf16), expand_bias.reshape(6, 4), jnp.zeros((6, 116), bf16)], axis=1
    )
    block = jnp.concatenate([query_weight, keyval_weight, mixer_weight, vectors], axis=1)
    block = jnp.concatenate([block, jnp.zeros((2, AW), bf16)], axis=0)
    w_mine = gather(block, CHIPS).reshape(512, AW)
    w_other = shift(w_mine, "c", 1)

    both = jnp.concatenate([tokens[0], upstream[0]], axis=1)
    far = lax.ppermute(both[HT:], SEQ, mirror)
    x = jnp.concatenate([tokens[0, :HT], far[:, :D]], axis=0)
    up = jnp.concatenate([upstream[0, :HT], far[:, D:]], axis=0)
    ups = [up] + [shift(up, "z", k) for k in (1, 2, 3)]

    feat = jnp.arange(D, dtype=jnp.int32)[:, None]
    e = jnp.arange(1024, dtype=jnp.int32)[None, :]
    side = jnp.where(e // 512 == 0, c, 1 - c)
    chip, r = (e % 512) // 8, e % 8
    pad = ((r < 6) & (feat == (2 * chip + side) * 6 + r)).astype(bf16)
    unit_side = jnp.where(feat // 384 == 0, c, 1 - c)
    unit_rest, unit_i = (feat % 384) // 24, feat % 24
    pe = (
        (unit_side == side) & (z * 16 + unit_rest == chip) & (unit_i // 4 == r)
    ).astype(bf16)
    e = jnp.arange(D, dtype=jnp.int32)[None, :]
    side = jnp.where(e // 384 == 0, c, 1 - c)
    rest, zz, r = (e % 384) // 24, e % 24 // 6, e % 6
    pm = (feat == 6 * (zz * 32 + rest * 2 + side) + r).astype(bf16)
    pc = (feat == (rest * 2 + side) * 24 + e % 24).astype(bf16)

    lengths = file_lengths[0]
    ends = jnp.cumsum(lengths)
    local = jnp.arange(HT, dtype=jnp.int32)
    pos = jnp.stack([seq * T + local, (NSEQ - 1 - seq) * T + HT + local])
    past = pos[:, :, None] >= ends
    start = jnp.where(
        jnp.all(past, axis=-1), pos, jnp.sum(jnp.where(past, lengths, 0), axis=-1)
    )
    info = jnp.tile(jnp.stack([pos, start], axis=1), (1, 1, H))
    base = pos[:, 0]
    lo = jnp.min(start, axis=1) // BK
    end = (base + HT - 1) // BK + 1
    u0 = jnp.clip((jnp.max(start, axis=1) + BK - 1) // BK, lo, end)
    u1 = jnp.clip((base + 1) // BK, u0, end)
    scal = jnp.stack([lo, u0, u1, end], axis=1).reshape(8).astype(jnp.int32)

    quarters = jnp.einsum(
        "rqn,nf->qrf", expand_weight.reshape(6, 4, D), pc, preferred_element_type=f32
    ).astype(bf16)
    rows24 = jnp.zeros((4, 6, D), bf16)
    for k in range(4):
        piece = lax.dynamic_index_in_dim(quarters, (z + k) % 4, 0, keepdims=True)
        if k:
            piece = shift(piece, "z", k)
        rows24 = lax.dynamic_update_slice_in_dim(rows24, piece, (z - k) % 4, 0)
    mlp_block = jnp.concatenate([rows24.reshape(24, D), shrink_weight], axis=1)

    vb = jnp.concatenate([jnp.zeros((HD,), f32), value_bias.astype(f32)])[None]
    kv_out, normed, npad, vec = call(
        first_kernel,
        [((NSEQ, T, 2 * HD), bf16), ((T, D), bf16), ((T, 1024), bf16), ((16, D), f32)],
        (x, w_mine, w_other, pad, pe, vb),
        [VMEM] * 6,
        flops=2 * T * 1024 * 3072,
        nbytes=8_000_000,
    )
    kv_all = lax.all_to_all(kv_out, SEQ, 0, 0, tiled=True)
    wnat, qt, qr = call(
        query_kernel,
        [((D, V0), bf16), ((2, 2 * HD, ROWS), bf16), ((2, ROWS, 2 * HD), bf16)],
        (normed, w_mine, w_other, pad, vec),
        [VMEM] * 5,
        flops=2 * D * 1024 * V0,
        nbytes=8_000_000,
    )
    kv_all, mlp_block = lax.optimization_barrier((kv_all, mlp_block))
    m_mine = gather(mlp_block, SLICE).reshape(384, 2 * D)
    m_other = shift(m_mine, "c", 1)

    ot, lse, att, hidden, mid, kvs, kvt = call(
        forward_kernel,
        [
            ((2, HD, ROWS), f32),
            ((2, 1, ROWS), f32),
            ((T, D), bf16),
            ((T, D), f32),
            ((T, D), bf16),
            ((WINDOW, 2 * HD), bf16),
            ((2 * HD, WINDOW), bf16),
        ],
        (qt, kv_all, info, scal, x, wnat, vec),
        [VMEM, VMEM, VMEM, SMEM, VMEM, VMEM, VMEM],
        scratch=[pltpu.VMEM((2, 1, ROWS), f32), pltpu.VMEM((2, 1, ROWS), f32)],
        flops=8_000_000_000,
        nbytes=10_000_000,
    )
    mids = [mid] + [shift(mid, "z", k) for k in (1, 2, 3)]
    d0, d1, d2, d3, act, dp, _, n_all, u_all = call(
        mlp_kernel,
        [((T, D), bf16)] * 4
        + [((4 * T, D), bf16), ((4 * T, D), bf16), ((D, D), bf16), ((4 * T, D), bf16), ((4 * T, D), bf16)],
        (*mids, *ups, m_mine, m_other, pm, vec),
        [VMEM] * 12,
        flops=2 * 4 * T * D * D * 4,
        nbytes=12_000_000,
    )
    back = [d0] + [shift(d, "z", -k) for k, d in ((1, d1), (2, d2), (3, d3))]
    r0, r1, r2, r3, gm_mlp, go_mlp, eb = call(
        mlp_grads_kernel,
        [((T, D), bf16)] * 4 + [((384, 2 * D), bf16), ((384, 2 * D), bf16), ((1, D), f32)],
        (act, dp, n_all, u_all, m_mine, m_other, pm),
        [VMEM] * 7,
        flops=2 * 4 * T * D * D * 4,
        nbytes=12_000_000,
    )
    outs = [r0] + [shift(r, "z", -k) for k, r in ((1, r1), (2, r2), (3, r3))]
    result = hidden + sum(o.astype(f32) for o in outs) + vec[6:7]
    g_mlp = gm_mlp + shift(go_mlp, "c", 1)
    got_mlp = lax.all_to_all(g_mlp.reshape(16, 24, 2 * D), SLICE, 0, 0, tiled=True)

    dkv, dq, d_hidden, dh_low, sums = call(
        backward_kernel,
        [((NSEQ, T, 2 * HD), bf16), ((T, D), bf16), ((T, D), f32), ((T, D), bf16), ((8, D), f32)],
        (*back, hidden, up, vec, wnat, ot, lse, qt, qr, kvs, kvt, info, scal),
        [VMEM] * 15 + [SMEM],
        scratch=[
            pltpu.VMEM((2, 2 * HD, ROWS), bf16),
            pltpu.VMEM((2, ROWS, 2 * HD), bf16),
            pltpu.VMEM((2, 1, ROWS), f32),
            pltpu.VMEM((WINDOW, 2 * HD), f32),
            pltpu.VMEM((2, HD, ROWS), f32),
        ],
        flops=20_000_000_000,
        nbytes=15_000_000,
    )
    got = lax.all_to_all(dkv, SEQ, 0, 0, tiled=True)
    gm, go = call(
        weight_grads_kernel,
        [((512, AW), bf16), ((512, AW), bf16)],
        (npad, att, pad, dq, dh_low),
        [VMEM] * 5,
        flops=2 * T * 1024 * 1536,
        nbytes=6_000_000,
    )
    tokens_grad, gm, go = call(
        last_kernel,
        [((T, D), f32), ((512, AW), bf16), ((512, AW), bf16)],
        (got, npad, dq, wnat, pad, pe, x, vec, d_hidden, sums, eb, gm, go),
        [VMEM] * 13,
        flops=2 * T * 1024 * 1024,
        nbytes=8_000_000,
    )
    g_att = gm + shift(go, "c", 1)
    got_att = lax.all_to_all(g_att.reshape(64, 8, AW), CHIPS, 0, 0, tiled=True)
    final = jnp.sum(got_att.astype(f32), axis=0)

    far = lax.ppermute(jnp.stack([result[HT:], tokens_grad[HT:]]), SEQ, mirror)
    result = jnp.concatenate([result[:HT], far[0]], axis=0)
    tokens_grad = jnp.concatenate([tokens_grad[:HT], far[1]], axis=0)

    mlp_rows = jnp.sum(got_mlp.astype(f32), axis=0)
    mine = jnp.einsum(
        "rf,nf->rn", mlp_rows[:, :D], pc.astype(f32), precision=lax.Precision.HIGHEST
    ).reshape(4, 6, D)
    expand_grad = jnp.zeros((6, 4 * D), f32)
    for k in range(4):
        piece = lax.dynamic_index_in_dim(mine, (z + k) % 4, 0, keepdims=False)
        if k:
            piece = shift(piece, "z", k)
        expand_grad = lax.dynamic_update_slice_in_dim(expand_grad, piece, ((z - k) % 4) * D, 1)

    vecs = final[:6, V0:]
    return (
        result[None],
        tokens_grad[None],
        vecs[:, 0],
        vecs[:, 1],
        final[:6, Q0:KV0],
        vecs[:, 2],
        final[:6, KV0:O0],
        final[6, KV0 + HD : O0],
        final[:6, O0:V0],
        vecs[:, 3],
        vecs[:, 4],
        vecs[:, 5],
        expand_grad,
        vecs[:, 8:12].reshape(24),
        mlp_rows[:, D:],
        vecs[:, 6],
    )


def solution(mesh):
    grid = Mesh(mesh.devices.reshape(4, 2, 4, 2, 2), SEQ + WIN)
    every = SEQ + WIN
    rows, flat = P(every, None), P(every)
    tokens = P(WIN, SEQ, None)
    return jax.shard_map(
        body,
        mesh=grid,
        in_specs=(
            tokens, P(WIN, None), tokens, flat, flat, rows, flat, rows, P(), rows, flat, flat, flat, rows, flat, rows, flat,
        ),
        out_specs=(
            tokens, tokens, flat, flat, rows, flat, rows, P(), rows, flat, flat, flat, rows, flat, rows, flat,
        ),
        check_vma=False,
    )
```

```python
import functools
import math

import jax
import jax.numpy as jnp
from jax import lax
from jax.experimental import pallas as pl
from jax.experimental.pallas import tpu as pltpu
from jax.sharding import Mesh, PartitionSpec as P

bf16 = jnp.bfloat16
f32 = jnp.float32
D = 768
H = 12
HD = 64
T = 128
HT = 64
WINDOW = 4096
NSEQ = 32
ROWS = H * HT
BK = 256
GRP = 256
NEG = -1e30
EPS = 1e-5
SEQ = ("z", "yl", "x")
WIN = ("yh", "c")
ALL = SEQ + WIN
CHIPS = ("z", "yl", "x", "yh")
Y = ("yl", "yh")
D2 = 2 * D
QT = D // 4
KV0, V0, Q0, O0, AW = 0, 128, 256, 1024, 1792
LW = 640
HBM = pl.BlockSpec(memory_space=pltpu.HBM)
SMEM = pl.BlockSpec(memory_space=pltpu.SMEM)


class Incoming:
    def __init__(self, source, ref, sem):
        self.ref, self.copy = ref, pltpu.make_async_copy(source, ref, sem)
        self.copy.start()

    def ready(self):
        if self.copy is not None:
            self.copy.wait()
            self.copy = None
        return self.ref

    def __getitem__(self, index):
        return self.ready()[index]


class Outgoing:
    def __init__(self, ref, target, sem):
        self.ref, self.copy, self.sent = ref, pltpu.make_async_copy(ref, target, sem), False

    def send(self):
        if not self.sent:
            self.copy.start()
            self.sent = True

    def __getitem__(self, index):
        return self.ref[index]

    def __setitem__(self, index, value):
        self.ref[index] = value


def call(kernel, outs, args, scalars=(), scratch=(), limit=32):
    parts = [a if isinstance(a, tuple) else (a, None, None) for a in args]
    arrays = [p[0] for p in parts]
    n, m, k = len(arrays), len(outs), len(scalars)

    def shape(array, lo, hi):
        return array.shape if lo is None else array.shape[:-1] + (hi - lo,)

    def run(*refs):
        ins, small, results = refs[:n], refs[n : n + k], refs[n + k : n + k + m]
        rest = refs[n + k + m :]
        bufs, out_bufs, (in_sem, out_sem), extra = rest[:n], rest[n : n + m], rest[n + m : n + m + 2], rest[n + m + 2 :]
        coming = [
            Incoming(r if p[1] is None else r.at[:, pl.ds(p[1], p[2] - p[1])], b, in_sem.at[i])
            for i, (r, p, b) in enumerate(zip(ins, parts, bufs, strict=True))
        ]
        going = [
            Outgoing(b, r, out_sem.at[i]) for i, (r, b) in enumerate(zip(results, out_bufs, strict=True))
        ]
        kernel(*coming, *small, *going, *extra)
        for c in coming:
            c.ready()
        for g in going:
            g.send()
        for g in going:
            g.copy.wait()

    return pl.pallas_call(
        run,
        out_shape=[pltpu.HBM(s, d) for s, d in outs],
        in_specs=[HBM] * n + [SMEM] * k,
        out_specs=[HBM] * m,
        scratch_shapes=[pltpu.VMEM(shape(*p), p[0].dtype) for p in parts]
        + [pltpu.VMEM(s, d) for s, d in outs]
        + [pltpu.SemaphoreType.DMA((n,)), pltpu.SemaphoreType.DMA((m,))]
        + list(scratch),
        compiler_params=pltpu.CompilerParams(vmem_limit_bytes=limit * 1024 * 1024),
    )(*(pltpu.with_memory_space_constraint(a, pltpu.HBM) for a in arrays), *scalars)


def dot(a, b):
    return jnp.dot(a, b, preferred_element_type=f32)


def dot_nt(a, b):
    return lax.dot_general(a, b, (((1,), (1,)), ((), ())), preferred_element_type=f32)


def dot_tn(a, b):
    return lax.dot_general(a, b, (((0,), (0,)), ((), ())), preferred_element_type=f32)


def normalize(v):
    mean = jnp.mean(v, axis=-1, keepdims=True)
    centered = v - mean
    spread = jnp.mean(centered * centered, axis=-1, keepdims=True)
    rstd = lax.rsqrt(spread + EPS)
    return centered * rstd, rstd


def norm_back(xhat, rstd, d_out, gain):
    d_hat = d_out * gain
    return rstd * (
        d_hat
        - jnp.mean(d_hat, axis=-1, keepdims=True)
        - xhat * jnp.mean(d_hat * xhat, axis=-1, keepdims=True)
    )


def first_kernel(
    x_ref, wm_ref, wo_ref, pad_ref, pe_ref, vb_ref,
    kv_ref, normed_ref, wkv_ref, vec_ref,
):
    xhat, _ = normalize(x_ref[...].astype(f32))
    chunk_t = jnp.concatenate(
        [wm_ref[:, V0:Q0].astype(f32).T, wo_ref[:, V0:Q0].astype(f32).T], axis=1
    ).astype(bf16)
    vecs = dot_nt(chunk_t, pad_ref[...])
    normed = (xhat * vecs[0:1] + vecs[1:2]).astype(bf16)
    normed_ref[...] = normed
    wkv = dot(pad_ref[:, :512], wm_ref[:, KV0:V0]) + dot(pad_ref[:, 512:], wo_ref[:, KV0:V0])
    wkv = wkv.astype(bf16)
    wkv_ref[...] = wkv
    kv = (dot(normed, wkv) + vb_ref[...]).astype(bf16)
    for i in range(NSEQ):
        kv_ref[i] = kv
    kv_ref.send()
    ebs = dot_nt(chunk_t, pe_ref[...])
    which = lax.broadcasted_iota(jnp.int32, (1, D), 1) % 24 // 6
    eb = jnp.zeros((1, D), f32)
    for k in range(4):
        eb = eb + jnp.where(which == k, ebs[8 + k : 9 + k], 0.0)
    vec_ref[0:8] = vecs[0:8]
    vec_ref[8:16] = jnp.broadcast_to(eb, (8, D))


def pack_cols(xt, g):
    return jnp.concatenate(
        [xt[h * HD : (h + 1) * HD, g * HT : (g + 1) * HT] for h in range(H)], axis=1
    )


def pack_rows(x, g):
    return jnp.concatenate(
        [x[g * HT : (g + 1) * HT, h * HD : (h + 1) * HD] for h in range(H)], axis=0
    )


def unpack(y):
    yt = y.T
    return jnp.concatenate([yt[h * HT : (h + 1) * HT] for h in range(H)], axis=1)


def widen(x):
    return jnp.concatenate([x, jnp.zeros((x.shape[0], 256 - x.shape[1]), x.dtype)], axis=1)


def query_kernel(normed_ref, wm_ref, wo_ref, pad_ref, vec_ref, qt_ref, qr_ref, wq_ref, wnat_ref):
    for out, lo in ((wq_ref, 0), (wnat_ref, D)):
        cols = pl.ds(lo, D)
        for row in (0, 256, 512):
            rows = pl.ds(row, 256)
            out[rows, :] = (
                dot(pad_ref[rows, :512], wm_ref[:, cols]) + dot(pad_ref[rows, 512:], wo_ref[:, cols])
            ).astype(bf16)
        out.send()
    q = (dot(normed_ref[...], wq_ref[...]) + vec_ref[2:3]).astype(bf16).astype(f32)
    q = q * (1.0 / math.sqrt(HD))
    qt = q.T
    for g in range(2):
        qt_ref[g, :HD, :] = pack_cols(qt, g).astype(bf16)
        qt_ref[g, HD:, :] = jnp.zeros((HD, ROWS), bf16)
        rows = pack_rows(q, g)
        qr_ref[g] = jnp.concatenate([rows, jnp.zeros((ROWS, HD), f32)], axis=1).astype(bf16)


def masked_scores(s, k0, info_ref, g, cols):
    j = k0 + lax.broadcasted_iota(jnp.int32, s.shape, 0)
    return (j >= info_ref[g, 1:2, cols]) & (j <= info_ref[g, 0:1, cols])


def over_blocks(scal_ref, g, block, carry):
    b = g * 4
    lo, u0, u1, end = scal_ref[b], scal_ref[b + 1], scal_ref[b + 2], scal_ref[b + 3]
    for first, last, masked in ((lo, u0, True), (u0, u1, False), (u1, end, True)):
        carry = lax.fori_loop(
            first, last, lambda kb, value, masked=masked: block(kb, value, masked), carry
        )
    return carry


def forward_kernel(
    kv_ref, qt_ref, info_ref, x_ref, wnat_ref, vec_ref, scal_ref,
    ot_ref, lse_ref, att_ref, hid_ref, mid_ref, kvs_ref, kvt_ref,
):
    kv_ref.ready()
    eye = (
        lax.broadcasted_iota(jnp.int32, (T, T), 0) == lax.broadcasted_iota(jnp.int32, (T, T), 1)
    ).astype(bf16)
    for i in range(NSEQ):
        blk = jnp.concatenate([kv_ref[i, :HT], kv_ref[NSEQ - 1 - i, HT:]], axis=0)
        kvs_ref[pl.ds(i * T, T), :] = blk
    for i in range(NSEQ // 4):
        rows = pl.ds(i * 4 * T, 4 * T)
        kvt_ref[:, rows] = dot_nt(eye, kvs_ref[rows, :]).astype(bf16)
    kvs_ref.send()
    kvt_ref.send()
    ot_ref[...] = jnp.zeros((2, HD, ROWS), f32)
    qt_ref.ready()
    info_ref.ready()
    parts = [slice(i * GRP, (i + 1) * GRP) for i in range(ROWS // GRP)]

    for g in range(2):

        def block(kb, carry, masked, g=g):
            k0 = pl.multiple_of(kb * BK, BK)
            kvb = kvs_ref[pl.ds(k0, BK), :]
            vt = kvt_ref[HD:, pl.ds(k0, BK)]
            scores = [dot(kvb, qt_ref[g, :, cols]) for cols in parts]
            new, products = [], []
            for s, cols, (m_old, l_old) in zip(scores, parts, carry, strict=True):
                if masked:
                    s = jnp.where(masked_scores(s, k0, info_ref, g, cols), s, NEG)
                m_new = jnp.maximum(m_old, jnp.max(s, axis=0, keepdims=True))
                p = jnp.exp(s - m_new)
                alpha = jnp.exp(m_old - m_new)
                new.append((m_new, l_old * alpha + jnp.sum(p, axis=0, keepdims=True)))
                products.append((alpha, dot(vt, p.astype(bf16))))
            for cols, (alpha, product) in zip(parts, products, strict=True):
                ot_ref[g, :, cols] = ot_ref[g, :, cols] * alpha + product
            return tuple(new)

        start = tuple((jnp.full((1, GRP), NEG, f32), jnp.zeros((1, GRP), f32)) for _ in parts)
        done = over_blocks(scal_ref, g, block, start)
        for cols, (m, l) in zip(parts, done, strict=True):
            ot_ref[g, :, cols] = ot_ref[g, :, cols] / l
            lse_ref[g, :, cols] = m + jnp.log(l)
        att_ref[g * HT : (g + 1) * HT, :] = unpack(ot_ref[g]).astype(bf16)
    ot_ref.send()
    hidden = x_ref[...].astype(f32) + dot(att_ref[...], wnat_ref[...]) + vec_ref[3:4]
    hid_ref[...] = hidden
    xhat, _ = normalize(hidden)
    mid_ref[...] = (xhat * vec_ref[4:5] + vec_ref[5:6]).astype(bf16)


def weights_kernel(mm_ref, mo_ref, pm_ref, pu_ref, we_ref, ws_ref):
    for out, perm, lo in ((we_ref, pm_ref, 0), (ws_ref, pu_ref, D)):
        cols = pl.ds(lo, D)
        out[...] = (
            dot(perm[:, :384], mm_ref[:, cols]) + dot(perm[:, 384:], mo_ref[:, cols])
        ).astype(bf16)
        out.send()


def mlp_kernel(
    we_ref, ws_ref, vec_ref, n0, n1, n2, n3, u0, u1, u2, u3, c_ref,
    d0, d1, d2, d3, keep_ref, send_ref, act_ref, eb_ref, dp_ref, n_ref, u_ref,
):
    for k, (n, u) in enumerate(((n0, u0), (n1, u1), (n2, u2), (n3, u3))):
        n_ref[pl.ds(k * T, T), :] = n[...]
        u_ref[pl.ds(k * T, T), :] = u[...]
    first = c_ref[0] == 0
    c0 = math.sqrt(2.0 / math.pi)
    for lo in (0, 384):
        cols = pl.ds(lo, 384)
        pre = dot(n_ref[...], we_ref[:, cols]) + vec_ref[8:9, cols]
        da = dot_nt(u_ref[...], ws_ref[cols, :])
        sq = pre * pre
        th = jnp.tanh(c0 * pre * (1.0 + 0.044715 * sq))
        up = 0.5 * (1.0 + th)
        act_ref[:, cols] = (pre * up).astype(bf16)
        slope = up + 0.5 * pre * (1.0 - th * th) * (c0 * (1.0 + 3 * 0.044715 * sq))
        dp_ref[:, cols] = (slope * da).astype(bf16)
    act_ref.send()
    dm = dot_nt(dp_ref[...], we_ref[...])
    for k, d in enumerate((d0, d1, d2, d3)):
        d[...] = dm[k * T : (k + 1) * T].astype(bf16)
        d.send()
    here, there = (keep_ref, send_ref), (send_ref, keep_ref)
    for when, (a, b) in ((first, here), (jnp.logical_not(first), there)):

        @pl.when(when)
        def _(a=a, b=b):
            a[:, :D] = n_ref[...]
            a[:, D:] = dp_ref[...]
            b[:, :D] = act_ref[...]
            b[:, D:] = u_ref[...]

    send_ref.send()
    keep_ref.send()
    eb_ref[...] = jnp.sum(dp_ref[...].astype(f32), axis=0, keepdims=True)


def result_kernel(act_ref, ws_ref, att_ref, r0, p1, p2, p3):
    for p in (p1, p2, p3):
        p[:, D:] = att_ref[...]
    out = dot(act_ref[...], ws_ref[...])
    for k, r in enumerate((r0, p3, p2, p1)):
        r[:, :D] = out[k * T : (k + 1) * T].astype(bf16)


def mlp_grads_kernel(keep_ref, perm_ref, got_ref, g0, g1, g2, g3):
    rows = [dot_nt(perm_ref[...], ref[:, :D]).astype(bf16) for ref in (keep_ref, got_ref)]
    for k, g in enumerate((g0, g1, g2, g3)):
        at = slice(k * 192, (k + 1) * 192)
        g[...] = (dot(rows[0][at], keep_ref[:, D:]) + dot(rows[1][at], got_ref[:, D:])).astype(bf16)
        g.send()


def backward_kernel(
    hid_ref, d0, d1, d2, d3, up_ref, vec_ref, wnat_ref, ot_ref, qt_ref, kvs_ref, kvt_ref, qr_ref, lse_ref, info_ref,
    scal_ref, dkv_ref, dq_ref, q0, q1, q2, q3, dhid_ref, sums_ref,
    dot_ref, dor_ref, delta_ref, dkv_acc, dqt_ref, dqh_ref,
):
    xhat, rstd = normalize(hid_ref[...])
    d_mid = (
        d0[...].astype(f32) + d1[...].astype(f32) + d2[...].astype(f32) + d3[...].astype(f32)
    )
    up = up_ref[...].astype(f32)
    d_hidden = up + norm_back(xhat, rstd, d_mid, vec_ref[4:5])
    dhid_ref[...] = d_hidden
    dhid_ref.send()
    d_low = d_hidden.astype(bf16)
    d_att = dot_nt(d_low, wnat_ref[...]).astype(bf16).astype(f32)
    for k in range(4):
        dqh_ref[k, :, 256:] = widen(d_low[:, k * QT : (k + 1) * QT].astype(f32))
    sums_ref[...] = jnp.concatenate(
        [
            jnp.sum(d_hidden, axis=0, keepdims=True),
            jnp.sum(d_mid * xhat, axis=0, keepdims=True),
            jnp.sum(d_mid, axis=0, keepdims=True),
            jnp.sum(up, axis=0, keepdims=True),
            jnp.zeros((4, D), f32),
        ],
        axis=0,
    )
    d_att_t = d_att.T
    for g in range(2):
        cols = pack_cols(d_att_t, g)
        delta_ref[g] = jnp.sum(cols * ot_ref[g], axis=0, keepdims=True)
        dot_ref[g, :HD, :] = jnp.zeros((HD, ROWS), bf16)
        dot_ref[g, HD:, :] = cols.astype(bf16)
        rows = pack_rows(d_att, g)
        dor_ref[g] = jnp.concatenate([jnp.zeros((ROWS, HD), f32), rows], axis=1).astype(bf16)
    dkv_acc[...] = jnp.zeros(dkv_acc.shape, f32)
    dqt_ref[...] = jnp.zeros(dqt_ref.shape, f32)
    for ref in (qt_ref, kvs_ref, kvt_ref, qr_ref, lse_ref, info_ref):
        ref.ready()
    parts = [slice(i * GRP, (i + 1) * GRP) for i in range(ROWS // GRP)]

    for g in range(2):

        def block(kb, carry, masked, g=g):
            k0 = pl.multiple_of(kb * BK, BK)
            kvb = kvs_ref[pl.ds(k0, BK), :]
            kt = kvt_ref[:HD, pl.ds(k0, BK)]
            acc = dkv_acc[pl.ds(k0, BK), :]
            pairs = [(dot(kvb, qt_ref[g, :, cols]), dot(kvb, dot_ref[g, :, cols])) for cols in parts]
            parts_out = []
            for (s, dp), cols in zip(pairs, parts, strict=True):
                p = jnp.exp(s - lse_ref[g, :, cols])
                if masked:
                    p = jnp.where(masked_scores(s, k0, info_ref, g, cols), p, 0.0)
                ds = (p * (dp - delta_ref[g, :, cols])).astype(bf16)
                parts_out.append((p.astype(bf16), ds))
            products = []
            for (p, ds), cols in zip(parts_out, parts, strict=True):
                acc = acc + dot(p, dor_ref[g, cols, :]) + dot(ds, qr_ref[g, cols, :])
                products.append(dot(kt, ds))
            dkv_acc[pl.ds(k0, BK), :] = acc
            for product, cols in zip(products, parts, strict=True):
                dqt_ref[g, :, cols] += product
            return carry

        over_blocks(scal_ref, g, block, 0)
    for i in range(NSEQ):
        dkv_ref[i, :HT, :] = dkv_acc[pl.ds(i * T, HT), :].astype(bf16)
        dkv_ref[NSEQ - 1 - i, HT:, :] = dkv_acc[pl.ds(i * T + HT, HT), :].astype(bf16)
    dkv_ref.send()
    at = scal_ref[8]
    for g in range(2):
        dq = (unpack(dqt_ref[g]) * (1.0 / math.sqrt(HD))).astype(bf16)
        rows = slice(g * HT, (g + 1) * HT)
        dq_ref[rows, :] = dq
        for k in range(4):
            dqh_ref[k, rows, :256] = widen(dq[:, k * QT : (k + 1) * QT].astype(f32))
    for k, q in enumerate((q0, q1, q2, q3)):
        q[...] = dqh_ref[(at + k) % 4].astype(bf16)


def weight_grads_kernel(
    q0, q1, q2, q3, normed_ref, x1, x2, x3, a0, p1, p2, p3, vec_ref, pad_ref,
    g_ref, left_ref, qh_ref,
):
    for k, x in enumerate((None, x1, x2, x3)):
        rows = pl.ds(k * T, T)
        if x is None:
            left_ref[rows, :] = normed_ref[...]
        else:
            xhat, _ = normalize(x[...].astype(f32))
            left_ref[rows, :] = (xhat * vec_ref[0:1] + vec_ref[1:2]).astype(bf16)
    npad = dot(left_ref[...], pad_ref[...]).astype(bf16)
    for k, q in enumerate((q0, q1, q2, q3)):
        qh_ref[pl.ds(k * T, T), :] = q[...]
    dwq = dot_tn(npad, qh_ref[:, :256])
    for k, a in enumerate((a0, p1, p2, p3)):
        left_ref[pl.ds(k * T, T), :] = a[...]
    dwo = dot_tn(dot(left_ref[...], pad_ref[...]).astype(bf16), qh_ref[:, 256:])
    g_ref[...] = jnp.concatenate([dwq[:, :QT], dwo[:, :QT]], axis=1).astype(bf16)


def last_kernel(
    x_ref, vec_ref, dq_ref, wq_ref, wkv_ref, got_ref, dhid_ref, sums_ref, eb_ref, normed_ref, pad_ref, pe_ref, given_ref,
    tg_ref, g_ref,
):
    xhat, rstd = normalize(x_ref[...].astype(f32))
    total = got_ref[0].astype(f32)
    for i in range(1, NSEQ):
        total = total + got_ref[i].astype(f32)
    owned = total.astype(bf16)
    d_normed = dot_nt(dq_ref[...], wq_ref[...]) + dot_nt(owned, wkv_ref[...])
    tg_ref[...] = dhid_ref[...] + norm_back(xhat, rstd, d_normed, vec_ref[0:1])
    tg_ref.send()
    rows = jnp.concatenate(
        [
            jnp.sum(d_normed * xhat, axis=0, keepdims=True),
            jnp.sum(d_normed, axis=0, keepdims=True),
            jnp.sum(dq_ref[...].astype(f32), axis=0, keepdims=True),
            sums_ref[0:1],
            sums_ref[1:2],
            sums_ref[2:3],
            sums_ref[3:4],
            jnp.zeros((1, D), f32),
        ],
        axis=0,
    ).astype(bf16)
    which = lax.broadcasted_iota(jnp.int32, (8, D), 1) % 24 // 6
    row = lax.broadcasted_iota(jnp.int32, (8, D), 0)
    ebs = jnp.where(which == row, jnp.broadcast_to(eb_ref[...], (8, D)), 0.0).astype(bf16)
    packed = jnp.concatenate(
        [dot(rows, pad_ref[...]), dot(ebs, pe_ref[...]), jnp.zeros((112, 1024), f32)], axis=0
    ).T
    ones = lax.broadcasted_iota(jnp.int32, (1, 1024), 1) % 8 == 6
    npad = jnp.where(ones, 1.0, dot(normed_ref[...], pad_ref[...])).astype(bf16)
    g_ref[:, :T] = dot_tn(npad, owned).astype(bf16)
    g_ref[:, T : 2 * T] = packed.astype(bf16)
    g_ref[:, 2 * T :] = given_ref[...]


def shift(value, axis, by):
    if axis == Y:
        ring = (0, 2, 1, 3)
        pairs = [(ring[i], ring[(i + by) % 4]) for i in range(4)]
    else:
        size = lax.axis_size(axis)
        pairs = [(i, (i + by) % size) for i in range(size)]
    return lax.ppermute(value, axis, pairs)


def after(value, *others):
    return lax.optimization_barrier((value, *others))[0]


def spread(block, axis):
    return [block] + [shift(block, axis, k) for k in (1, 2, 3)]


def collect(parts, axis):
    got = [parts[0]] + [shift(parts[k], axis, -k) for k in (1, 2, 3)]
    return [g.astype(f32) for g in got]


def quarter(values, k, dtype):
    rows = values[0].shape[0] // 4
    total = values[0][k * rows : (k + 1) * rows].astype(f32)
    for v in values[1:]:
        total = total + v[k * rows : (k + 1) * rows].astype(f32)
    return total.astype(dtype)


def body(
    tokens,
    file_lengths,
    upstream,
    pre_gain,
    pre_shift,
    query_weight,
    query_bias,
    keyval_weight,
    value_bias,
    mixer_weight,
    mixer_bias,
    mid_gain,
    middle_norm_bias,
    expand_weight,
    expand_bias,
    shrink_weight,
    shrink_bias,
):
    z, yl, xx, yh, c = (lax.axis_index(a) for a in ALL)
    y = yh * 2 + yl
    seq = lax.axis_index(SEQ)
    mirror = [(i, NSEQ - 1 - i) for i in range(NSEQ)]

    at = jnp.stack([z]).astype(jnp.int32)

    vectors = jnp.concatenate(
        [
            v.reshape(1, 6)
            for v in (
                pre_gain, pre_shift, query_bias, mixer_bias, mid_gain, middle_norm_bias, shrink_bias,
                jnp.zeros((6,), bf16),
            )
        ]
        + [expand_bias.reshape(4, 6)],
        axis=0,
    )
    vectors = jnp.pad(vectors.T, ((0, 0), (0, 116)))
    block = jnp.concatenate([keyval_weight, vectors, query_weight, mixer_weight], axis=1)
    block = jnp.broadcast_to(jnp.pad(block, ((0, 2), (0, 0)))[None], (64, 8, AW))
    w_mine = lax.all_to_all(block, CHIPS, 0, 0, tiled=True).reshape(512, AW)

    both = jnp.concatenate([tokens[0], upstream[0]], axis=1)
    far = lax.ppermute(both[HT:], SEQ, mirror)
    xu = jnp.concatenate([both[:HT], far], axis=0)

    rows24 = jnp.zeros((4, 6, D), bf16)
    columns = expand_weight.reshape(6, 4, D)
    for k in range(4):
        piece = lax.dynamic_index_in_dim(columns, (z + k) % 4, 1, keepdims=False)[None]
        if k:
            piece = shift(piece, "z", k)
        rows24 = lax.dynamic_update_slice_in_dim(rows24, piece, (z - k) % 4, 0)
    m_mine = jnp.concatenate([rows24.reshape(24, D), shrink_weight], axis=1)

    feat = jnp.arange(D, dtype=jnp.int32)[:, None]
    e = jnp.arange(1024, dtype=jnp.int32)[None, :]
    chip, r = e % 512 // 8, e % 8
    dev = 2 * chip + jnp.where(e < 512, c, 1 - c)
    pad = ((r < 6) & (feat == dev * 6 + r)).astype(bf16)
    pe = ((z * 32 + feat // 24 == dev) & (feat % 24 % 6 == r)).astype(bf16)

    def device(half, ky, kx):
        y_of, side = (y - ky) % 4, jnp.where(half == 0, c, 1 - c)
        return y_of % 2 * 16 + (xx - kx) % 4 * 4 + y_of // 2 * 2 + side

    of = jnp.arange(D, dtype=jnp.int32)[None, :]
    rest = device(of // 384, of % 384 // 96, of % 96 // 24)
    pm = (feat == (of % 24 // 6 * 32 + rest) * 6 + of % 6).astype(bf16)
    pu = (feat == rest * 24 + of % 24).astype(bf16)
    rest = device((feat % 48 // 24 + c) % 2, feat // 192, feat % 192 // 48)
    perm = (
        of == jnp.where(c == 0, (feat % 24 // 6 * 32 + rest) * 6 + feat % 6, rest * 24 + feat % 24)
    ).astype(bf16)

    lengths = file_lengths[0]
    ends = jnp.cumsum(lengths)
    local = jnp.arange(HT, dtype=jnp.int32)
    pos = jnp.stack([seq * T + local, (NSEQ - 1 - seq) * T + HT + local])
    past = pos[:, :, None] >= ends
    start = jnp.where(
        jnp.all(past, axis=-1), pos, jnp.sum(jnp.where(past, lengths, 0), axis=-1)
    )
    info = jnp.tile(jnp.stack([pos, start], axis=1), (1, 1, H))
    base = pos[:, 0]
    lo = jnp.min(start, axis=1) // BK
    end = (base + HT - 1) // BK + 1
    u0 = jnp.clip((jnp.max(start, axis=1) + BK - 1) // BK, lo, end)
    u1 = jnp.clip((base + 1) // BK, u0, end)
    scal = jnp.stack([lo, u0, u1, end], axis=1).reshape(8).astype(jnp.int32)
    scal = jnp.concatenate([scal, at])

    vb = jnp.concatenate([jnp.zeros((HD,), f32), value_bias.astype(f32)])[None]
    w_mine, m_mine, xu, pad, pe, pm, pu, perm, info, scal, vb = lax.optimization_barrier(
        (w_mine, m_mine, xu, pad, pe, pm, pu, perm, info, scal, vb)
    )
    w_other = shift(w_mine, "c", 1)
    kv_out, normed, wkv, vec = call(
        first_kernel,
        [((NSEQ, T, 2 * HD), bf16), ((T, D), bf16), ((D, 2 * HD), bf16), ((16, D), f32)],
        ((xu, 0, D), (w_mine, 0, Q0), (w_other, 0, Q0), pad, pe, vb),
    )
    kv_all = lax.all_to_all(kv_out, SEQ, 0, 0, tiled=True)
    m_mine = after(m_mine, kv_out)
    m_mine = jnp.stack(spread(m_mine, "x"))
    qt, qr, wq, wnat = call(
        query_kernel,
        [((2, 2 * HD, ROWS), bf16), ((2, ROWS, 2 * HD), bf16), ((D, D), bf16), ((D, D), bf16)],
        (normed, (w_mine, Q0, AW), (w_other, Q0, AW), pad, vec),
    )
    kv_all, m_mine, wnat, qt, xu = lax.optimization_barrier((kv_all, m_mine, wnat, qt, xu))
    m_mine = spread(m_mine, Y)
    xus = spread(xu, "z")

    ot, lse, att, hidden, mid, kvs, kvt = call(
        forward_kernel,
        [
            ((2, HD, ROWS), f32),
            ((2, 1, ROWS), f32),
            ((T, D), bf16),
            ((T, D), f32),
            ((T, D), bf16),
            ((WINDOW, 2 * HD), bf16),
            ((2 * HD, WINDOW), bf16),
        ],
        (kv_all, qt, info, (xu, 0, D), wnat, vec),
        [scal],
    )
    m_mine, xus, mid, feat = lax.optimization_barrier((m_mine, xus, mid, feat))
    dev = e // 8
    pad = ((r < 6) & (feat == dev * 6 + r)).astype(bf16)
    pe = ((z * 32 + feat // 24 == dev) & (feat % 24 % 6 == r)).astype(bf16)
    mids = spread(mid, "z")
    m_mine = jnp.stack(m_mine).reshape(384, D2)
    m_other = shift(m_mine, "c", 1)
    we, ws = call(weights_kernel, [((D, D), bf16)] * 2, (m_mine, m_other, pm, pu))
    mids, pad, pe = lax.optimization_barrier((mids, pad, pe))
    *ds, keep, send, act, eb = call(
        mlp_kernel,
        [((T, D), bf16)] * 4 + [((4 * T, D2), bf16)] * 2 + [((4 * T, D), bf16), ((1, D), f32)],
        (we, ws, vec, *mids, *((u, D, D2) for u in xus)),
        [jnp.stack([c]).astype(jnp.int32)],
        scratch=[pltpu.VMEM((4 * T, D), bf16)] * 3,
    )
    back = [ds[0]] + [shift(ds[k], "z", -k) for k in (1, 2, 3)]
    got = shift(send, "c", 1)
    r0, *pays = call(
        result_kernel, [((T, D), bf16)] + [((T, D2), bf16)] * 3, (act, ws, att)
    )
    g_mlp = call(mlp_grads_kernel, [((192, D), bf16)] * 4, (keep, perm, got))
    back, g_mlp, pays = lax.optimization_barrier((back, g_mlp, pays))
    g_mlp = [g_mlp[0]] + [shift(g_mlp[k], Y, -k) for k in (1, 2, 3)]
    pays = [shift(p, "z", k) for k, p in zip((1, 2, 3), pays, strict=True)]

    dkv, dq, *qhs, d_hidden, sums = call(
        backward_kernel,
        [((NSEQ, T, 2 * HD), bf16), ((T, D), bf16)]
        + [((T, 512), bf16)] * 4
        + [((T, D), f32), ((8, D), f32)],
        (hidden, *back, (xu, D, D2), vec, wnat, ot, qt, kvs, kvt, qr, lse, info),
        [scal],
        scratch=[
            pltpu.VMEM((2, 2 * HD, ROWS), bf16),
            pltpu.VMEM((2, ROWS, 2 * HD), bf16),
            pltpu.VMEM((2, 1, ROWS), f32),
            pltpu.VMEM((WINDOW, 2 * HD), f32),
            pltpu.VMEM((2, HD, ROWS), f32),
            pltpu.VMEM((4, T, 512), f32),
        ],
    )
    dkv, g_mlp, pays = lax.optimization_barrier((dkv, g_mlp, pays))
    got = lax.all_to_all(dkv, SEQ, 0, 0, tiled=True)
    qhs = [qhs[0]] + [shift(qhs[k], "z", k) for k in (1, 2, 3)]
    (given,) = call(
        weight_grads_kernel,
        [((1024, 2 * QT), bf16)],
        (*qhs, normed, *((u, 0, D) for u in xus[1:]), att, *((p, D, D2) for p in pays), vec, pad),
        scratch=[pltpu.VMEM((4 * T, D), bf16), pltpu.VMEM((4 * T, 512), bf16)],
    )
    g_mlp = [quarter(g_mlp, k, bf16) for k in range(4)]
    got, *g_mlp = lax.optimization_barrier((got, *g_mlp))
    tokens_grad, last = call(
        last_kernel,
        [((T, D), f32), ((1024, LW), bf16)],
        ((xu, 0, D), vec, dq, wq, wkv, got, d_hidden, sums, eb, normed, pad, pe, given),
    )
    g_mlp = collect(g_mlp, "x")
    g_mlp, pays, r0 = lax.optimization_barrier((g_mlp, pays, r0, last))[:3]
    both = sum(g_mlp).reshape(2, 24, D)
    keep = lax.dynamic_index_in_dim(both, c, 0, keepdims=False)
    got = shift(lax.dynamic_index_in_dim(both, 1 - c, 0, keepdims=False), "c", 1)
    mine = jnp.where(c == 0, keep, got).reshape(4, 6, D)
    shrink_grad = jnp.where(c == 0, got, keep)
    expand_grad = jnp.zeros((6, 4 * D), f32)
    for k in range(4):
        piece = lax.dynamic_index_in_dim(mine, (z + k) % 4, 0, keepdims=False)
        if k:
            piece = shift(piece, "z", k)
        expand_grad = lax.dynamic_update_slice_in_dim(expand_grad, piece, ((z - k) % 4) * D, 1)
    result = hidden + r0.astype(f32) + sum(p[:, :D].astype(f32) for p in pays) + vec[6:7]
    result = jnp.concatenate([result[:HT], lax.ppermute(result[HT:], SEQ, mirror)], axis=0)
    last = lax.all_to_all(last.reshape(128, 8, LW), ALL, 0, 0, tiled=True)
    last = jnp.sum(last.reshape(4, 32, 8, LW).astype(f32), axis=1)
    quarters = jnp.transpose(last[:, :6, 2 * T :], (1, 0, 2)).reshape(6, 4, 2, QT)
    last = jnp.sum(last[:, :, : 2 * T], axis=0)
    tokens_grad = jnp.concatenate(
        [tokens_grad[:HT], lax.ppermute(tokens_grad[HT:], SEQ, mirror)], axis=0
    )

    vecs = last[:6, T : 2 * T]
    return (
        result[None],
        tokens_grad[None],
        vecs[:, 0],
        vecs[:, 1],
        quarters[:, :, 0].reshape(6, D),
        vecs[:, 2],
        last[:6, :T],
        last[6, HD:T],
        quarters[:, :, 1].reshape(6, D),
        vecs[:, 3],
        vecs[:, 4],
        vecs[:, 5],
        expand_grad,
        vecs[:, 8:12].T.reshape(24),
        shrink_grad,
        vecs[:, 6],
    )


def solution(mesh):
    grid = Mesh(mesh.devices.reshape(4, 2, 4, 2, 2), SEQ + WIN)
    every = SEQ + WIN
    rows, flat = P(every, None), P(every)
    tokens = P(WIN, SEQ, None)
    return jax.shard_map(
        body,
        mesh=grid,
        in_specs=(
            tokens, P(WIN, None), tokens, flat, flat, rows, flat, rows, P(), rows, flat, flat, flat, rows, flat, rows, flat,
        ),
        out_specs=(
            tokens, tokens, flat, flat, rows, flat, rows, P(), rows, flat, flat, flat, rows, flat, rows, flat,
        ),
        check_vma=False,
    )
```

```python
import functools
import math

import jax
import jax.numpy as jnp
from jax import lax
from jax.experimental import pallas as pl
from jax.experimental.pallas import tpu as pltpu
from jax.sharding import Mesh, PartitionSpec as P

bf16 = jnp.bfloat16
f32 = jnp.float32
D = 768
H = 12
HD = 64
T = 128
HT = 64
WINDOW = 4096
NSEQ = 32
ROWS = H * HT
BK = 256
GRP = 256
NEG = -1e30
EPS = 1e-5
SEQ = ("z", "yl", "x")
WIN = ("yh", "c")
ALL = SEQ + WIN
CHIPS = ("z", "yl", "x", "yh")
SLICE = ("yl", "x", "yh")
D2 = 2 * D
KV0, V0, Q0, O0, AW = 0, 128, 256, 1024, 1792
HBM = pl.BlockSpec(memory_space=pltpu.HBM)
SMEM = pl.BlockSpec(memory_space=pltpu.SMEM)
ANY = pl.BlockSpec(memory_space=pl.ANY)


class Anywhere:
    def __init__(self, array):
        self.array = array


class Incoming:
    def __init__(self, source, ref, sem):
        self.ref, self.copy = ref, pltpu.make_async_copy(source, ref, sem)
        self.copy.start()

    def ready(self):
        if self.copy is not None:
            self.copy.wait()
            self.copy = None
        return self.ref

    def __getitem__(self, index):
        return self.ready()[index]


class Outgoing:
    def __init__(self, ref, target, sem):
        self.ref, self.copy, self.sent = ref, pltpu.make_async_copy(ref, target, sem), False

    def send(self):
        if not self.sent:
            self.copy.start()
            self.sent = True

    def __getitem__(self, index):
        return self.ref[index]

    def __setitem__(self, index, value):
        self.ref[index] = value


def call(kernel, outs, args, scalars=(), scratch=(), limit=32):
    loose = [isinstance(a, Anywhere) for a in args]
    parts = [a.array if isinstance(a, Anywhere) else a for a in args]
    parts = [a if isinstance(a, tuple) else (a, None, None) for a in parts]
    arrays = [
        p[0] if free else pltpu.with_memory_space_constraint(p[0], pltpu.HBM)
        for p, free in zip(parts, loose, strict=True)
    ]
    n, m, k = len(arrays), len(outs), len(scalars)

    def shape(array, lo, hi):
        return array.shape if lo is None else array.shape[:-1] + (hi - lo,)

    def run(*refs):
        ins, small, results = refs[:n], refs[n : n + k], refs[n + k : n + k + m]
        rest = refs[n + k + m :]
        bufs, out_bufs, (in_sem, out_sem), extra = rest[:n], rest[n : n + m], rest[n + m : n + m + 2], rest[n + m + 2 :]
        coming = [
            Incoming(r if p[1] is None else r.at[:, pl.ds(p[1], p[2] - p[1])], b, in_sem.at[i])
            for i, (r, p, b) in enumerate(zip(ins, parts, bufs, strict=True))
        ]
        going = [
            Outgoing(b, r, out_sem.at[i]) for i, (r, b) in enumerate(zip(results, out_bufs, strict=True))
        ]
        kernel(*coming, *small, *going, *extra)
        for c in coming:
            c.ready()
        for g in going:
            g.send()
        for g in going:
            g.copy.wait()

    return pl.pallas_call(
        run,
        out_shape=[pltpu.HBM(s, d) for s, d in outs],
        in_specs=[ANY if free else HBM for free in loose] + [SMEM] * k,
        out_specs=[HBM] * m,
        scratch_shapes=[pltpu.VMEM(shape(*p), p[0].dtype) for p in parts]
        + [pltpu.VMEM(s, d) for s, d in outs]
        + [pltpu.SemaphoreType.DMA((n,)), pltpu.SemaphoreType.DMA((m,))]
        + list(scratch),
        compiler_params=pltpu.CompilerParams(vmem_limit_bytes=limit * 1024 * 1024),
    )(*arrays, *scalars)


def dot(a, b):
    return jnp.dot(a, b, preferred_element_type=f32)


def dot_nt(a, b):
    return lax.dot_general(a, b, (((1,), (1,)), ((), ())), preferred_element_type=f32)


def dot_tn(a, b):
    return lax.dot_general(a, b, (((0,), (0,)), ((), ())), preferred_element_type=f32)


def normalize(v):
    mean = jnp.mean(v, axis=-1, keepdims=True)
    centered = v - mean
    spread = jnp.mean(centered * centered, axis=-1, keepdims=True)
    rstd = lax.rsqrt(spread + EPS)
    return centered * rstd, rstd


def norm_back(xhat, rstd, d_out, gain):
    d_hat = d_out * gain
    return rstd * (
        d_hat
        - jnp.mean(d_hat, axis=-1, keepdims=True)
        - xhat * jnp.mean(d_hat * xhat, axis=-1, keepdims=True)
    )


def first_kernel(
    x_ref, wm_ref, wo_ref, pad_ref, pe_ref, vb_ref,
    kv_ref, normed_ref, wkv_ref, vec_ref,
):
    xhat, _ = normalize(x_ref[...].astype(f32))
    chunk_t = jnp.concatenate(
        [wm_ref[:, V0:Q0].astype(f32).T, wo_ref[:, V0:Q0].astype(f32).T], axis=1
    ).astype(bf16)
    vecs = dot_nt(chunk_t, pad_ref[...])
    normed = (xhat * vecs[0:1] + vecs[1:2]).astype(bf16)
    normed_ref[...] = normed
    wkv = dot(pad_ref[:, :512], wm_ref[:, KV0:V0]) + dot(pad_ref[:, 512:], wo_ref[:, KV0:V0])
    wkv = wkv.astype(bf16)
    wkv_ref[...] = wkv
    kv = (dot(normed, wkv) + vb_ref[...]).astype(bf16)
    for i in range(NSEQ):
        kv_ref[i] = kv
    kv_ref.send()
    ebs = dot_nt(chunk_t, pe_ref[...])
    which = lax.broadcasted_iota(jnp.int32, (1, D), 1) % 24 // 6
    eb = jnp.zeros((1, D), f32)
    for k in range(4):
        eb = eb + jnp.where(which == k, ebs[8 + k : 9 + k], 0.0)
    vec_ref[0:8] = vecs[0:8]
    vec_ref[8:16] = jnp.broadcast_to(eb, (8, D))


def pack_cols(xt, g):
    return jnp.concatenate(
        [xt[h * HD : (h + 1) * HD, g * HT : (g + 1) * HT] for h in range(H)], axis=1
    )


def pack_rows(x, g):
    return jnp.concatenate(
        [x[g * HT : (g + 1) * HT, h * HD : (h + 1) * HD] for h in range(H)], axis=0
    )


def unpack(y):
    yt = y.T
    return jnp.concatenate([yt[h * HT : (h + 1) * HT] for h in range(H)], axis=1)


def query_kernel(normed_ref, wm_ref, wo_ref, pad_ref, vec_ref, qt_ref, qr_ref, wq_ref, wnat_ref):
    for out, lo in ((wq_ref, 0), (wnat_ref, D)):
        cols = pl.ds(lo, D)
        for row in (0, 256, 512):
            rows = pl.ds(row, 256)
            out[rows, :] = (
                dot(pad_ref[rows, :512], wm_ref[:, cols]) + dot(pad_ref[rows, 512:], wo_ref[:, cols])
            ).astype(bf16)
        out.send()
    q = (dot(normed_ref[...], wq_ref[...]) + vec_ref[2:3]).astype(bf16).astype(f32)
    q = q * (1.0 / math.sqrt(HD))
    qt = q.T
    for g in range(2):
        qt_ref[g, :HD, :] = pack_cols(qt, g).astype(bf16)
        qt_ref[g, HD:, :] = jnp.zeros((HD, ROWS), bf16)
        rows = pack_rows(q, g)
        qr_ref[g] = jnp.concatenate([rows, jnp.zeros((ROWS, HD), f32)], axis=1).astype(bf16)


def masked_scores(s, k0, info_ref, g, cols):
    j = k0 + lax.broadcasted_iota(jnp.int32, s.shape, 0)
    return (j >= info_ref[g, 1:2, cols]) & (j <= info_ref[g, 0:1, cols])


def over_blocks(scal_ref, g, block, carry):
    b = g * 4
    lo, u0, u1, end = scal_ref[b], scal_ref[b + 1], scal_ref[b + 2], scal_ref[b + 3]
    for first, last, masked in ((lo, u0, True), (u0, u1, False), (u1, end, True)):
        carry = lax.fori_loop(
            first, last, lambda kb, value, masked=masked: block(kb, value, masked), carry
        )
    return carry


def forward_kernel(
    kv_ref, qt_ref, info_ref, x_ref, wnat_ref, vec_ref, scal_ref,
    ot_ref, lse_ref, att_ref, hid_ref, mid_ref, kvs_ref, kvt_ref,
):
    kv_ref.ready()
    eye = (
        lax.broadcasted_iota(jnp.int32, (T, T), 0) == lax.broadcasted_iota(jnp.int32, (T, T), 1)
    ).astype(bf16)
    for i in range(NSEQ):
        blk = jnp.concatenate([kv_ref[i, :HT], kv_ref[NSEQ - 1 - i, HT:]], axis=0)
        kvs_ref[pl.ds(i * T, T), :] = blk
    for i in range(NSEQ // 4):
        rows = pl.ds(i * 4 * T, 4 * T)
        kvt_ref[:, rows] = dot_nt(eye, kvs_ref[rows, :]).astype(bf16)
    kvs_ref.send()
    kvt_ref.send()
    ot_ref[...] = jnp.zeros((2, HD, ROWS), f32)
    qt_ref.ready()
    info_ref.ready()
    parts = [slice(i * GRP, (i + 1) * GRP) for i in range(ROWS // GRP)]

    for g in range(2):

        def block(kb, carry, masked, g=g):
            k0 = pl.multiple_of(kb * BK, BK)
            kvb = kvs_ref[pl.ds(k0, BK), :]
            vt = kvt_ref[HD:, pl.ds(k0, BK)]
            scores = [dot(kvb, qt_ref[g, :, cols]) for cols in parts]
            new, products = [], []
            for s, cols, (m_old, l_old) in zip(scores, parts, carry, strict=True):
                if masked:
                    s = jnp.where(masked_scores(s, k0, info_ref, g, cols), s, NEG)
                m_new = jnp.maximum(m_old, jnp.max(s, axis=0, keepdims=True))
                p = jnp.exp(s - m_new)
                alpha = jnp.exp(m_old - m_new)
                new.append((m_new, l_old * alpha + jnp.sum(p, axis=0, keepdims=True)))
                products.append((alpha, dot(vt, p.astype(bf16))))
            for cols, (alpha, product) in zip(parts, products, strict=True):
                ot_ref[g, :, cols] = ot_ref[g, :, cols] * alpha + product
            return tuple(new)

        start = tuple((jnp.full((1, GRP), NEG, f32), jnp.zeros((1, GRP), f32)) for _ in parts)
        done = over_blocks(scal_ref, g, block, start)
        for cols, (m, l) in zip(parts, done, strict=True):
            ot_ref[g, :, cols] = ot_ref[g, :, cols] / l
            lse_ref[g, :, cols] = m + jnp.log(l)
        att_ref[g * HT : (g + 1) * HT, :] = unpack(ot_ref[g]).astype(bf16)
    ot_ref.send()
    hidden = x_ref[...].astype(f32) + dot(att_ref[...], wnat_ref[...]) + vec_ref[3:4]
    hid_ref[...] = hidden
    xhat, _ = normalize(hidden)
    mid_ref[...] = (xhat * vec_ref[4:5] + vec_ref[5:6]).astype(bf16)


def weights_kernel(mm_ref, mo_ref, pm_ref, pu_ref, we_ref, ws_ref):
    for out, perm, lo in ((we_ref, pm_ref, 0), (ws_ref, pu_ref, D)):
        cols = pl.ds(lo, D)
        out[...] = (
            dot(perm[:, :384], mm_ref[:, cols]) + dot(perm[:, 384:], mo_ref[:, cols])
        ).astype(bf16)
        out.send()


def mlp_kernel(
    we_ref, ws_ref, vec_ref, u0, u1, u2, u3, n0, n1, n2, n3, c_ref,
    d0, d1, d2, d3, keep_ref, send_ref, act_ref, eb_ref, dp_ref, n_ref, u_ref,
):
    for k, (n, u) in enumerate(((n0, u0), (n1, u1), (n2, u2), (n3, u3))):
        u_ref[pl.ds(k * T, T), :] = u[...]
        n_ref[pl.ds(k * T, T), :] = n[...]
    first = c_ref[0] == 0
    c0 = math.sqrt(2.0 / math.pi)
    for lo in (0, 384):
        cols = pl.ds(lo, 384)
        pre = dot(n_ref[...], we_ref[:, cols]) + vec_ref[8:9, cols]
        da = dot_nt(u_ref[...], ws_ref[cols, :])
        sq = pre * pre
        th = jnp.tanh(c0 * pre * (1.0 + 0.044715 * sq))
        up = 0.5 * (1.0 + th)
        act_ref[:, cols] = (pre * up).astype(bf16)
        slope = up + 0.5 * pre * (1.0 - th * th) * (c0 * (1.0 + 3 * 0.044715 * sq))
        dp_ref[:, cols] = (slope * da).astype(bf16)
    act_ref.send()
    dm = dot_nt(dp_ref[...], we_ref[...])
    for k, d in enumerate((d0, d1, d2, d3)):
        d[...] = dm[k * T : (k + 1) * T].astype(bf16)
        d.send()
    here, there = (keep_ref, send_ref), (send_ref, keep_ref)
    for when, (a, b) in ((first, here), (jnp.logical_not(first), there)):

        @pl.when(when)
        def _(a=a, b=b):
            a[:, :D] = n_ref[...]
            a[:, D:] = dp_ref[...]
            b[:, :D] = act_ref[...]
            b[:, D:] = u_ref[...]

    send_ref.send()
    keep_ref.send()
    eb_ref[...] = jnp.sum(dp_ref[...].astype(f32), axis=0, keepdims=True)


def result_kernel(act_ref, ws_ref, r0, r1, r2, r3):
    for k, r in enumerate((r0, r1, r2, r3)):
        r[...] = dot(act_ref[k * T : (k + 1) * T, :], ws_ref[...]).astype(bf16)


def mlp_grads_kernel(perm_ref, left_ref, right_ref, left2_ref, right2_ref, g_ref):
    rows = dot_nt(perm_ref[...], left_ref[...]).astype(bf16)
    own = dot(rows, right_ref[...])
    rows = dot_nt(perm_ref[...], left2_ref[...]).astype(bf16)
    g_ref[...] = (own + dot(rows, right2_ref[...])).astype(bf16)


def backward_kernel(
    hid_ref, d0, d1, d2, d3, up_ref, vec_ref, wnat_ref, ot_ref, qt_ref, kvs_ref, kvt_ref, qr_ref, lse_ref, info_ref,
    scal_ref, dkv_ref, dq_ref, dhid_ref, dhl_ref, sums_ref,
    dot_ref, dor_ref, delta_ref, dkv_acc, dqt_ref,
):
    xhat, rstd = normalize(hid_ref[...])
    d_mid = (
        d0[...].astype(f32) + d1[...].astype(f32) + d2[...].astype(f32) + d3[...].astype(f32)
    )
    up = up_ref[...].astype(f32)
    d_hidden = up + norm_back(xhat, rstd, d_mid, vec_ref[4:5])
    dhid_ref[...] = d_hidden
    dhid_ref.send()
    d_low = d_hidden.astype(bf16)
    d_att = dot_nt(d_low, wnat_ref[...]).astype(bf16).astype(f32)
    dhl_ref[...] = d_low
    dhl_ref.send()
    sums_ref[...] = jnp.concatenate(
        [
            jnp.sum(d_hidden, axis=0, keepdims=True),
            jnp.sum(d_mid * xhat, axis=0, keepdims=True),
            jnp.sum(d_mid, axis=0, keepdims=True),
            jnp.sum(up, axis=0, keepdims=True),
            jnp.zeros((4, D), f32),
        ],
        axis=0,
    )
    d_att_t = d_att.T
    for g in range(2):
        cols = pack_cols(d_att_t, g)
        delta_ref[g] = jnp.sum(cols * ot_ref[g], axis=0, keepdims=True)
        dot_ref[g, :HD, :] = jnp.zeros((HD, ROWS), bf16)
        dot_ref[g, HD:, :] = cols.astype(bf16)
        rows = pack_rows(d_att, g)
        dor_ref[g] = jnp.concatenate([jnp.zeros((ROWS, HD), f32), rows], axis=1).astype(bf16)
    dkv_acc[...] = jnp.zeros(dkv_acc.shape, f32)
    dqt_ref[...] = jnp.zeros(dqt_ref.shape, f32)
    for ref in (qt_ref, kvs_ref, kvt_ref, qr_ref, lse_ref, info_ref):
        ref.ready()
    parts = [slice(i * GRP, (i + 1) * GRP) for i in range(ROWS // GRP)]

    for g in range(2):

        def block(kb, carry, masked, g=g):
            k0 = pl.multiple_of(kb * BK, BK)
            kvb = kvs_ref[pl.ds(k0, BK), :]
            kt = kvt_ref[:HD, pl.ds(k0, BK)]
            acc = dkv_acc[pl.ds(k0, BK), :]
            pairs = [(dot(kvb, qt_ref[g, :, cols]), dot(kvb, dot_ref[g, :, cols])) for cols in parts]
            parts_out = []
            for (s, dp), cols in zip(pairs, parts, strict=True):
                p = jnp.exp(s - lse_ref[g, :, cols])
                if masked:
                    p = jnp.where(masked_scores(s, k0, info_ref, g, cols), p, 0.0)
                ds = (p * (dp - delta_ref[g, :, cols])).astype(bf16)
                parts_out.append((p.astype(bf16), ds))
            products = []
            for (p, ds), cols in zip(parts_out, parts, strict=True):
                acc = acc + dot(p, dor_ref[g, cols, :]) + dot(ds, qr_ref[g, cols, :])
                products.append(dot(kt, ds))
            dkv_acc[pl.ds(k0, BK), :] = acc
            for product, cols in zip(products, parts, strict=True):
                dqt_ref[g, :, cols] += product
            return carry

        over_blocks(scal_ref, g, block, 0)
    for i in range(NSEQ):
        dkv_ref[i, :HT, :] = dkv_acc[pl.ds(i * T, HT), :].astype(bf16)
        dkv_ref[NSEQ - 1 - i, HT:, :] = dkv_acc[pl.ds(i * T + HT, HT), :].astype(bf16)
    dkv_ref.send()
    for g in range(2):
        dq_ref[g * HT : (g + 1) * HT, :] = (unpack(dqt_ref[g]) * (1.0 / math.sqrt(HD))).astype(bf16)


def weight_grads_kernel(pad_ref, left_ref, right_ref, gm_ref, go_ref):
    for lo, out in ((512, go_ref), (0, gm_ref)):
        rows = dot(left_ref[...], pad_ref[:, lo : lo + 512]).astype(bf16)
        out[...] = dot_tn(rows, right_ref[...]).astype(bf16)
        out.send()


def last_kernel(
    x_ref, vec_ref, dq_ref, wq_ref, wkv_ref, got_ref, dhid_ref, sums_ref, eb_ref, normed_ref, pad_ref, pe_ref,
    tg_ref, gm_ref, go_ref,
):
    xhat, rstd = normalize(x_ref[...].astype(f32))
    total = got_ref[0].astype(f32)
    for i in range(1, NSEQ):
        total = total + got_ref[i].astype(f32)
    owned = total.astype(bf16)
    d_normed = dot_nt(dq_ref[...], wq_ref[...]) + dot_nt(owned, wkv_ref[...])
    tg_ref[...] = dhid_ref[...] + norm_back(xhat, rstd, d_normed, vec_ref[0:1])
    tg_ref.send()
    rows = jnp.concatenate(
        [
            jnp.sum(d_normed * xhat, axis=0, keepdims=True),
            jnp.sum(d_normed, axis=0, keepdims=True),
            jnp.sum(dq_ref[...].astype(f32), axis=0, keepdims=True),
            sums_ref[0:1],
            sums_ref[1:2],
            sums_ref[2:3],
            sums_ref[3:4],
            jnp.zeros((1, D), f32),
        ],
        axis=0,
    ).astype(bf16)
    which = lax.broadcasted_iota(jnp.int32, (8, D), 1) % 24 // 6
    row = lax.broadcasted_iota(jnp.int32, (8, D), 0)
    ebs = jnp.where(which == row, jnp.broadcast_to(eb_ref[...], (8, D)), 0.0).astype(bf16)
    packed = jnp.concatenate(
        [dot(rows, pad_ref[...]), dot(ebs, pe_ref[...]), jnp.zeros((112, 1024), f32)], axis=0
    ).T
    ones = lax.broadcasted_iota(jnp.int32, (1, 1024), 1) % 8 == 6
    npad = jnp.where(ones, 1.0, dot(normed_ref[...], pad_ref[...])).astype(bf16)
    kv = dot_tn(npad, owned).astype(bf16)
    for lo, out in ((512, go_ref), (0, gm_ref)):
        out[:, :T] = kv[lo : lo + 512]
        out[:, T:] = packed[lo : lo + 512].astype(bf16)
        out.send()


def shift(value, axis, by):
    size = lax.axis_size(axis)
    return lax.ppermute(value, axis, [(i, (i + by) % size) for i in range(size)])


def after(value, *others):
    return lax.optimization_barrier((value, *others))[0]


def spread(block, axis):
    return [block] + [shift(block, axis, k) for k in (1, 2, 3)]


def gather(block, axes):
    count = math.prod(lax.axis_size(a) for a in axes)
    block = jnp.broadcast_to(block[None], (count,) + block.shape)
    return lax.all_to_all(block, axes, 0, 0, tiled=True)


def collect(parts, axis):
    return [parts[0]] + [shift(parts[k], axis, -k) for k in (1, 2, 3)]


def body(
    tokens,
    file_lengths,
    upstream,
    pre_gain,
    pre_shift,
    query_weight,
    query_bias,
    keyval_weight,
    value_bias,
    mixer_weight,
    mixer_bias,
    mid_gain,
    middle_norm_bias,
    expand_weight,
    expand_bias,
    shrink_weight,
    shrink_bias,
):
    z, c = lax.axis_index("z"), lax.axis_index("c")
    seq = lax.axis_index(SEQ)
    mirror = [(i, NSEQ - 1 - i) for i in range(NSEQ)]


    def mirrored(rows):
        far = lax.ppermute(rows[HT:].astype(bf16), SEQ, mirror)
        return jnp.concatenate([rows[:HT], far.astype(f32)], axis=0)

    vectors = jnp.concatenate(
        [
            v.reshape(1, 6)
            for v in (
                pre_gain, pre_shift, query_bias, mixer_bias, mid_gain, middle_norm_bias, shrink_bias,
                jnp.zeros((6,), bf16),
            )
        ]
        + [expand_bias.reshape(4, 6)],
        axis=0,
    )
    vectors = jnp.pad(vectors.T, ((0, 0), (0, 116)))
    block = jnp.concatenate([keyval_weight, vectors, query_weight, mixer_weight], axis=1)
    block = jnp.pad(block, ((0, 2), (0, 0)))
    w_mine = gather(block, CHIPS).reshape(512, AW)

    tokens, upstream, expand_weight = lax.optimization_barrier(
        (tokens, upstream, expand_weight, block)
    )[:3]
    both = jnp.concatenate([tokens[0], upstream[0]], axis=1)
    far = lax.ppermute(both[HT:], SEQ, mirror)
    xu = jnp.concatenate([both[:HT], far], axis=0)

    columns, rows24 = expand_weight.reshape(6, 4, D), jnp.zeros((4, 6, D), bf16)
    for k in range(4):
        piece = lax.dynamic_index_in_dim(columns, (z + k) % 4, 1, keepdims=False)[None]
        if k:
            piece = shift(piece, "z", k)
        rows24 = lax.dynamic_update_slice_in_dim(rows24, piece, (z - k) % 4, 0)
    m_mine = jnp.concatenate([rows24.reshape(24, D), shrink_weight], axis=1)

    feat = jnp.arange(D, dtype=jnp.int32)[:, None]
    e = jnp.arange(1024, dtype=jnp.int32)[None, :]
    chip, r = e % 512 // 8, e % 8
    dev = 2 * chip + jnp.where(e < 512, c, 1 - c)
    pad = ((r < 6) & (feat == dev * 6 + r)).astype(bf16)
    pe = ((z * 32 + feat // 24 == dev) & (feat % 24 % 6 == r)).astype(bf16)

    of = jnp.arange(D, dtype=jnp.int32)[None, :]
    rest = of % 384 // 24 * 2 + jnp.where(of < 384, c, 1 - c)
    pm = (feat == (of % 24 // 6 * 32 + rest) * 6 + of % 6).astype(bf16)
    pu = (feat == rest * 24 + of % 24).astype(bf16)
    rest = feat // 24
    perm = (
        of == jnp.where(c == 0, (feat % 24 // 6 * 32 + rest) * 6 + feat % 6, rest * 24 + feat % 24)
    ).astype(bf16)

    lengths = file_lengths[0]
    ends = jnp.cumsum(lengths)
    local = jnp.arange(HT, dtype=jnp.int32)
    pos = jnp.stack([seq * T + local, (NSEQ - 1 - seq) * T + HT + local])
    past = pos[:, :, None] >= ends
    start = jnp.where(
        jnp.all(past, axis=-1), pos, jnp.sum(jnp.where(past, lengths, 0), axis=-1)
    )
    info = jnp.tile(jnp.stack([pos, start], axis=1), (1, 1, H))
    base = pos[:, 0]
    lo = jnp.min(start, axis=1) // BK
    end = (base + HT - 1) // BK + 1
    u0 = jnp.clip((jnp.max(start, axis=1) + BK - 1) // BK, lo, end)
    u1 = jnp.clip((base + 1) // BK, u0, end)
    scal = jnp.stack([lo, u0, u1, end], axis=1).reshape(8).astype(jnp.int32)

    vb = jnp.concatenate([jnp.zeros((HD,), f32), value_bias.astype(f32)])[None]
    w_mine, m_mine, xu, pad, pe, pm, pu, perm, info, scal, vb = lax.optimization_barrier(
        (w_mine, m_mine, xu, pad, pe, pm, pu, perm, info, scal, vb)
    )
    w_kv = [w_mine[:, :Q0]]
    w_kv.append(shift(w_kv[0], "c", 1))
    kv_out, normed, wkv, vec = call(
        first_kernel,
        [((NSEQ, T, 2 * HD), bf16), ((T, D), bf16), ((D, 2 * HD), bf16), ((16, D), f32)],
        ((xu, 0, D), Anywhere(w_kv[0]), Anywhere(w_kv[1]), pad, pe, vb),
    )
    kv_all = lax.all_to_all(kv_out, SEQ, 0, 0, tiled=True)
    w_qo = [after(w_mine, kv_out)[:, Q0:]]
    w_qo.append(shift(w_qo[0], "c", 1))
    qt, qr, wq, wnat = call(
        query_kernel,
        [((2, 2 * HD, ROWS), bf16), ((2, ROWS, 2 * HD), bf16), ((D, D), bf16), ((D, D), bf16)],
        (normed, Anywhere(w_qo[0]), Anywhere(w_qo[1]), pad, vec),
    )
    kv_all, wnat, qt, m_mine, xu = lax.optimization_barrier((kv_all, wnat, qt, m_mine, xu))
    m_mine = gather(m_mine, SLICE).reshape(384, D2)
    ups = spread(xu[:, D:], "z")

    ot, lse, att, hidden, mid, kvs, kvt = call(
        forward_kernel,
        [
            ((2, HD, ROWS), f32),
            ((2, 1, ROWS), f32),
            ((T, D), bf16),
            ((T, D), f32),
            ((T, D), bf16),
            ((WINDOW, 2 * HD), bf16),
            ((2 * HD, WINDOW), bf16),
        ],
        (kv_all, qt, info, (xu, 0, D), wnat, vec),
        [scal],
    )
    m_mine, mid, ups = lax.optimization_barrier((m_mine, mid, ups))
    m_other = shift(m_mine, "c", 1)
    mids = spread(mid, "z")
    we, ws = call(
        weights_kernel, [((D, D), bf16)] * 2, (Anywhere(m_mine), Anywhere(m_other), pm, pu)
    )
    *ds, keep, send, act, eb = call(
        mlp_kernel,
        [((T, D), bf16)] * 4 + [((4 * T, D2), bf16)] * 2 + [((4 * T, D), bf16), ((1, D), f32)],
        (we, ws, vec, *ups, *mids),
        [jnp.stack([c]).astype(jnp.int32)],
        scratch=[pltpu.VMEM((4 * T, D), bf16)] * 3,
    )
    back = [ds[0]] + [shift(ds[k], "z", -k) for k in (1, 2, 3)]
    got = shift(send, "c", 1)
    (g_mlp,) = call(
        mlp_grads_kernel,
        [((D, D), bf16)],
        (perm, (keep, 0, D), (keep, D, D2), Anywhere((got, 0, D)), Anywhere((got, D, D2))),
    )
    back, g_mlp = lax.optimization_barrier((back, g_mlp))
    g_mlp = lax.all_to_all(g_mlp.reshape(16, 48, D), SLICE, 0, 0, tiled=True)

    dkv, dq, d_hidden, dh_low, sums = call(
        backward_kernel,
        [((NSEQ, T, 2 * HD), bf16), ((T, D), bf16), ((T, D), f32), ((T, D), bf16), ((8, D), f32)],
        (hidden, *back, (xu, D, D2), vec, wnat, ot, qt, kvs, kvt, qr, lse, info),
        [scal],
        scratch=[
            pltpu.VMEM((2, 2 * HD, ROWS), bf16),
            pltpu.VMEM((2, ROWS, 2 * HD), bf16),
            pltpu.VMEM((2, 1, ROWS), f32),
            pltpu.VMEM((WINDOW, 2 * HD), f32),
            pltpu.VMEM((2, HD, ROWS), f32),
        ],
    )
    dkv, dq, dh_low, g_mlp = lax.optimization_barrier((dkv, dq, dh_low, g_mlp))
    got = lax.all_to_all(dkv, SEQ, 0, 0, tiled=True)
    mine, other = [], []
    for left, right in ((normed, dq), (att, dh_low)):
        a, b = call(weight_grads_kernel, [((512, D), bf16)] * 2, (pad, left, right))
        mine.append(a)
        other.append(shift(b, "c", 1))
    both = jnp.sum(g_mlp.astype(f32), axis=0).reshape(2, 24, D)
    keep = lax.dynamic_index_in_dim(both, c, 0, keepdims=False)
    far = shift(lax.dynamic_index_in_dim(both, 1 - c, 0, keepdims=False), "c", 1)
    rows = jnp.where(c == 0, keep, far).reshape(4, 6, D)
    shrink_grad = jnp.where(c == 0, far, keep)
    pieces = [lax.dynamic_index_in_dim(rows, (z + k) % 4, 0, keepdims=False) for k in range(4)]
    pieces = [pieces[0]] + [shift(pieces[k], "z", k) for k in (1, 2, 3)]
    act = after(act, shrink_grad)
    outs = collect(call(result_kernel, [((T, D), bf16)] * 4, (act, ws)), "z")
    got, pieces = lax.optimization_barrier((got, pieces))
    tokens_grad, g_kv, kv_other = call(
        last_kernel,
        [((T, D), f32), ((512, Q0), bf16), ((512, Q0), bf16)],
        ((xu, 0, D), vec, dq, wq, wkv, Anywhere(got), d_hidden, sums, eb, normed, pad, pe),
    )
    tokens_grad = mirrored(tokens_grad)
    result = mirrored(hidden + sum(o.astype(f32) for o in outs) + vec[6:7])
    kv_other = shift(kv_other, "c", 1)
    result, kv_other = lax.optimization_barrier((result, kv_other))
    g_all = jnp.concatenate([g_kv + kv_other] + [a + b for a, b in zip(mine, other, strict=True)], axis=1)
    last = lax.all_to_all(g_all.reshape(64, 8, AW), CHIPS, 0, 0, tiled=True)
    last = jnp.sum(last.astype(f32), axis=0)
    expand_grad = jnp.zeros((6, 4 * D), f32)
    for k in range(4):
        expand_grad = lax.dynamic_update_slice_in_dim(expand_grad, pieces[k], ((z - k) % 4) * D, 1)

    vecs = last[:6, V0:Q0]
    return (
        result[None],
        tokens_grad[None],
        vecs[:, 0],
        vecs[:, 1],
        last[:6, Q0:O0],
        vecs[:, 2],
        last[:6, :V0],
        last[6, HD:V0],
        last[:6, O0:],
        vecs[:, 3],
        vecs[:, 4],
        vecs[:, 5],
        expand_grad,
        vecs[:, 8:12].T.reshape(24),
        shrink_grad,
        vecs[:, 6],
    )


def solution(mesh):
    grid = Mesh(mesh.devices.reshape(4, 2, 4, 2, 2), SEQ + WIN)
    every = SEQ + WIN
    rows, flat = P(every, None), P(every)
    tokens = P(WIN, SEQ, None)
    return jax.shard_map(
        body,
        mesh=grid,
        in_specs=(
            tokens, P(WIN, None), tokens, flat, flat, rows, flat, rows, P(), rows, flat, flat, flat, rows, flat, rows, flat,
        ),
        out_specs=(
            tokens, tokens, flat, flat, rows, flat, rows, P(), rows, flat, flat, flat, rows, flat, rows, flat,
        ),
        check_vma=False,
    )
```

```python
import functools
import math

import jax
import jax.numpy as jnp
from jax import lax
from jax.experimental import pallas as pl
from jax.experimental.pallas import tpu as pltpu
from jax.sharding import Mesh, PartitionSpec as P

bf16 = jnp.bfloat16
f32 = jnp.float32
D = 768
H = 12
HD = 64
T = 128
HT = 64
WINDOW = 4096
NSEQ = 32
ROWS = H * HT
BK_FORWARD = 512
BK = 256
VROWS = 80
GRP = 256
NEG = -1e30
EPS = 1e-5
SEQ = ("z", "yl", "x")
WIN = ("yh", "c")
ALL = SEQ + WIN
CHIPS = ("z", "yl", "x", "yh")
SLICE = ("yl", "x", "yh")
D2 = 2 * D
KV0, V0, Q0, O0, AW = 0, 128, 256, 1024, 1792
HBM = pl.BlockSpec(memory_space=pltpu.HBM)
SMEM = pl.BlockSpec(memory_space=pltpu.SMEM)
ANY = pl.BlockSpec(memory_space=pl.ANY)


class Anywhere:
    def __init__(self, array):
        self.array = array


class Incoming:
    def __init__(self, source, ref, sem):
        self.ref, self.copy = ref, pltpu.make_async_copy(source, ref, sem)
        self.copy.start()

    def ready(self):
        if self.copy is not None:
            self.copy.wait()
            self.copy = None
        return self.ref

    def __getitem__(self, index):
        return self.ready()[index]


class Outgoing:
    def __init__(self, ref, target, sem):
        self.ref, self.copy, self.sent = ref, pltpu.make_async_copy(ref, target, sem), False

    def send(self):
        if not self.sent:
            self.copy.start()
            self.sent = True

    def __getitem__(self, index):
        return self.ref[index]

    def __setitem__(self, index, value):
        self.ref[index] = value


def call(kernel, outs, args, scalars=(), scratch=(), limit=32):
    loose = [isinstance(a, Anywhere) for a in args]
    parts = [a.array if isinstance(a, Anywhere) else a for a in args]
    parts = [a if isinstance(a, tuple) else (a, None, None) for a in parts]
    arrays = [
        p[0] if free else pltpu.with_memory_space_constraint(p[0], pltpu.HBM)
        for p, free in zip(parts, loose, strict=True)
    ]
    n, m, k = len(arrays), len(outs), len(scalars)

    def shape(array, lo, hi):
        return array.shape if lo is None else array.shape[:-1] + (hi - lo,)

    def run(*refs):
        ins, small, results = refs[:n], refs[n : n + k], refs[n + k : n + k + m]
        rest = refs[n + k + m :]
        bufs, out_bufs, (in_sem, out_sem), extra = rest[:n], rest[n : n + m], rest[n + m : n + m + 2], rest[n + m + 2 :]
        coming = [
            Incoming(r if p[1] is None else r.at[:, pl.ds(p[1], p[2] - p[1])], b, in_sem.at[i])
            for i, (r, p, b) in enumerate(zip(ins, parts, bufs, strict=True))
        ]
        going = [
            Outgoing(b, r, out_sem.at[i]) for i, (r, b) in enumerate(zip(results, out_bufs, strict=True))
        ]
        kernel(*coming, *small, *going, *extra)
        for c in coming:
            c.ready()
        for g in going:
            g.send()
        for g in going:
            g.copy.wait()

    return pl.pallas_call(
        run,
        out_shape=[pltpu.HBM(s, d) for s, d in outs],
        in_specs=[ANY if free else HBM for free in loose] + [SMEM] * k,
        out_specs=[HBM] * m,
        scratch_shapes=[pltpu.VMEM(shape(*p), p[0].dtype) for p in parts]
        + [pltpu.VMEM(s, d) for s, d in outs]
        + [pltpu.SemaphoreType.DMA((n,)), pltpu.SemaphoreType.DMA((m,))]
        + list(scratch),
        compiler_params=pltpu.CompilerParams(vmem_limit_bytes=limit * 1024 * 1024),
    )(*arrays, *scalars)


def dot(a, b):
    return jnp.dot(a, b, preferred_element_type=f32)


def dot_nt(a, b):
    return lax.dot_general(a, b, (((1,), (1,)), ((), ())), preferred_element_type=f32)


def dot_tn(a, b):
    return lax.dot_general(a, b, (((0,), (0,)), ((), ())), preferred_element_type=f32)


def normalize(v):
    mean = jnp.mean(v, axis=-1, keepdims=True)
    centered = v - mean
    spread = jnp.mean(centered * centered, axis=-1, keepdims=True)
    rstd = lax.rsqrt(spread + EPS)
    return centered * rstd, rstd


def norm_back(xhat, rstd, d_out, gain):
    d_hat = d_out * gain
    return rstd * (
        d_hat
        - jnp.mean(d_hat, axis=-1, keepdims=True)
        - xhat * jnp.mean(d_hat * xhat, axis=-1, keepdims=True)
    )


def first_kernel(
    x_ref, wm_ref, wo_ref, pad_ref, pe_ref, vb_ref,
    kv_ref, normed_ref, wkv_ref, vec_ref,
):
    xhat, _ = normalize(x_ref[...].astype(f32))
    chunk_t = jnp.concatenate(
        [wm_ref[:, V0:Q0].astype(f32).T, wo_ref[:, V0:Q0].astype(f32).T], axis=1
    ).astype(bf16)
    vecs = dot_nt(chunk_t, pad_ref[...])
    normed = (xhat * vecs[0:1] + vecs[1:2]).astype(bf16)
    normed_ref[...] = normed
    wkv = dot(pad_ref[:, :512], wm_ref[:, KV0:V0]) + dot(pad_ref[:, 512:], wo_ref[:, KV0:V0])
    wkv = wkv.astype(bf16)
    wkv_ref[...] = wkv
    kv = (dot(normed, wkv) + vb_ref[...]).astype(bf16)
    for i in range(NSEQ):
        kv_ref[i] = kv
    kv_ref.send()
    ebs = dot_nt(chunk_t, pe_ref[...])
    which = lax.broadcasted_iota(jnp.int32, (1, D), 1) % 24 // 6
    eb = jnp.zeros((1, D), f32)
    for k in range(4):
        eb = eb + jnp.where(which == k, ebs[8 + k : 9 + k], 0.0)
    vec_ref[0:8] = vecs[0:8]
    vec_ref[8:16] = jnp.broadcast_to(eb, (8, D))


def pack_cols(xt, g):
    return jnp.concatenate(
        [xt[h * HD : (h + 1) * HD, g * HT : (g + 1) * HT] for h in range(H)], axis=1
    )


def pack_rows(x, g):
    return jnp.concatenate(
        [x[g * HT : (g + 1) * HT, h * HD : (h + 1) * HD] for h in range(H)], axis=0
    )


def unpack(y):
    yt = y.T
    return jnp.concatenate([yt[h * HT : (h + 1) * HT] for h in range(H)], axis=1)


def query_kernel(
    normed_ref, wm_ref, wo_ref, pad_ref, vec_ref, qt_ref, qr_ref, wq_ref, wnat_ref, npt_ref
):
    for out, lo in ((wq_ref, 0), (wnat_ref, D)):
        cols = pl.ds(lo, D)
        for row in (0, 256, 512):
            rows = pl.ds(row, 256)
            out[rows, :] = (
                dot(pad_ref[rows, :512], wm_ref[:, cols]) + dot(pad_ref[rows, 512:], wo_ref[:, cols])
            ).astype(bf16)
        out.send()
    q = (dot(normed_ref[...], wq_ref[...]) + vec_ref[2:3]).astype(bf16).astype(f32)
    qt = (q * (math.log2(math.e) / math.sqrt(HD))).T
    q = q * (1.0 / math.sqrt(HD))
    for g in range(2):
        cols = pack_cols(qt, g)
        high = cols.astype(bf16)
        zeros = jnp.zeros((HD, ROWS), bf16)
        qt_ref[g] = jnp.concatenate([high, zeros, (cols - high.astype(f32)).astype(bf16), zeros], axis=0)
        rows = pack_rows(q, g)
        qr_ref[g] = jnp.concatenate([rows, jnp.zeros((ROWS, HD), f32)], axis=1).astype(bf16)
    ones = lax.broadcasted_iota(jnp.int32, (1024, 1), 0) % 8 == 6
    npt_ref[...] = jnp.where(ones, 1.0, dot(normed_ref[...], pad_ref[...]).T).astype(bf16)


def three_parts(row):
    first = row.astype(bf16)
    rest = row - first.astype(f32)
    second = rest.astype(bf16)
    third = (rest - second.astype(f32)).astype(bf16)
    at = lax.broadcasted_iota(jnp.int32, (16, row.shape[1]), 0)
    out = jnp.where(at == 0, first.astype(f32), 0.0)
    out = jnp.where(at == 1, second.astype(f32), out)
    return jnp.where(at == 2, third.astype(f32), out).astype(bf16)


def open_keys(s, k0, info_ref, g, cols):
    j = k0 + lax.broadcasted_iota(jnp.int32, s.shape, 0)
    return (j >= info_ref[g, 1:2, cols]) & (j <= info_ref[g, 0:1, cols])


def over_blocks(scal_ref, b, block, carry):
    lo, u0, u1, end = scal_ref[b], scal_ref[b + 1], scal_ref[b + 2], scal_ref[b + 3]
    for first, last, masked in ((lo, u0, True), (u0, u1, False), (u1, end, True)):
        carry = lax.fori_loop(
            first, last, lambda kb, value, masked=masked: block(kb, value, masked), carry
        )
    return carry


def forward_kernel(
    kv_ref, qt_ref, info_ref, x_ref, wnat_ref, vec_ref, scal_ref,
    ot_ref, lse_ref, att_ref, hid_ref, mid_ref, keys_ref, kvt_ref, acc_ref,
):
    kv_ref.ready()
    lane = lax.broadcasted_iota(jnp.int32, (T, T), 1)
    for i in range(NSEQ):
        blk = jnp.concatenate([kv_ref[i, :HT], kv_ref[NSEQ - 1 - i, HT:]], axis=0)
        rows = pl.ds(i * T, T)
        keys_ref[rows, :T] = blk
        keys_ref[rows, T:] = jnp.where(lane < HD, blk.astype(f32), 1.0).astype(bf16)
    keys_ref.send()
    at = lax.broadcasted_iota(jnp.int32, (VROWS + HD, T), 0)
    lane = lax.broadcasted_iota(jnp.int32, (VROWS + HD, T), 1)
    pick = (lane == jnp.where(at < HD, at + HD, at - VROWS)).astype(bf16)
    at = lax.broadcasted_iota(jnp.int32, (VROWS + HD, 1), 0)
    ones = (at >= HD) & (at < VROWS)
    for i in range(NSEQ // 4):
        rows = pl.ds(i * 4 * T, 4 * T)
        kvt_ref[:, rows] = jnp.where(ones, 1.0, dot_nt(pick, keys_ref[rows, :T])).astype(bf16)
    kvt_ref.send()
    acc_ref[...] = jnp.zeros(acc_ref.shape, f32)
    qt_ref.ready()
    info_ref.ready()
    parts = [slice(i * GRP, (i + 1) * GRP) for i in range(ROWS // GRP)]

    for g in range(2):

        def block(kb, carry, masked, g=g):
            k0 = pl.multiple_of(kb * BK_FORWARD, BK_FORWARD)
            keys = keys_ref[pl.ds(k0, BK_FORWARD), :]
            vt = kvt_ref[:VROWS, pl.ds(k0, BK_FORWARD)]
            scores = [dot(keys, qt_ref[g, :, cols]) for cols in parts]
            new, products = [], []
            for s, cols, m_old in zip(scores, parts, carry, strict=True):
                if masked:
                    s = jnp.where(open_keys(s, k0, info_ref, g, cols), s, NEG)
                m_new = jnp.maximum(m_old, jnp.max(s, axis=0, keepdims=True))
                p = jnp.exp2(s - m_new)
                new.append(m_new)
                products.append((jnp.exp2(m_old - m_new), dot(vt, p.astype(bf16))))
            for cols, (alpha, product) in zip(parts, products, strict=True):
                acc_ref[g, :, cols] = acc_ref[g, :, cols] * alpha + product
            return tuple(new)

        start = tuple(jnp.full((1, GRP), NEG, f32) for _ in parts)
        done = over_blocks(scal_ref, g * 4, block, start)
        for cols, m in zip(parts, done, strict=True):
            total = acc_ref[g, HD : HD + 1, cols]
            ot_ref[g, :, cols] = acc_ref[g, :HD, cols] / total
            lse_ref[g, :, cols] = m + jnp.log2(total)
        att_ref[g * HT : (g + 1) * HT, :] = unpack(ot_ref[g]).astype(bf16)
    ot_ref.send()
    att_ref.send()
    hidden = x_ref[...].astype(f32) + dot(att_ref[...], wnat_ref[...]) + vec_ref[3:4]
    hid_ref[...] = hidden
    xhat, _ = normalize(hidden)
    mid_ref[...] = (xhat * vec_ref[4:5] + vec_ref[5:6]).astype(bf16)


def weights_kernel(att_ref, pad_ref, mm_ref, pm_ref, pu_ref, mo_ref, we_ref, ws_ref, apt_ref):
    apt_ref[...] = dot(att_ref[...], pad_ref[...]).T.astype(bf16)
    apt_ref.send()
    for out, perm, lo in ((we_ref, pm_ref, 0), (ws_ref, pu_ref, D)):
        cols = pl.ds(lo, D)
        out[...] = (
            dot(perm[:, :384], mm_ref[:, cols]) + dot(perm[:, 384:], mo_ref[:, cols])
        ).astype(bf16)
        out.send()


def mlp_kernel(
    we_ref, ws_ref, vec_ref, u0, u1, u2, u3, n0, n1, n2, n3, c_ref,
    d0, d1, d2, d3, keep_ref, send_ref, act_ref, eb_ref, dp_ref, n_ref, u_ref,
):
    for k, (n, u) in enumerate(((n0, u0), (n1, u1), (n2, u2), (n3, u3))):
        u_ref[pl.ds(k * T, T), :] = u[...]
        n_ref[pl.ds(k * T, T), :] = n[...]
    first = c_ref[0] == 0
    c0 = math.sqrt(2.0 / math.pi)
    for lo in (0, 384):
        cols = pl.ds(lo, 384)
        pre = dot(n_ref[...], we_ref[:, cols]) + vec_ref[8:9, cols]
        da = dot_nt(u_ref[...], ws_ref[cols, :])
        sq = pre * pre
        th = jnp.tanh(c0 * pre * (1.0 + 0.044715 * sq))
        up = 0.5 * (1.0 + th)
        act_ref[:, cols] = (pre * up).astype(bf16)
        slope = up + 0.5 * pre * (1.0 - th * th) * (c0 * (1.0 + 3 * 0.044715 * sq))
        dp_ref[:, cols] = (slope * da).astype(bf16)
    act_ref.send()
    dm = dot_nt(dp_ref[...], we_ref[...])
    for k, d in enumerate((d0, d1, d2, d3)):
        d[...] = dm[k * T : (k + 1) * T].astype(bf16)
        d.send()
    here, there = (keep_ref, send_ref), (send_ref, keep_ref)
    for when, (a, b) in ((first, here), (jnp.logical_not(first), there)):

        @pl.when(when)
        def _(a=a, b=b):
            a[:, :D] = n_ref[...]
            a[:, D:] = dp_ref[...]
            b[:, :D] = act_ref[...]
            b[:, D:] = u_ref[...]

    send_ref.send()
    keep_ref.send()
    eb_ref[...] = jnp.sum(dp_ref[...].astype(f32), axis=0, keepdims=True)


def result_kernel(act_ref, ws_ref, piece_ref, r0, p1, p2, p3):
    for k, r in enumerate((r0, p3, p2, p1)):
        r[:T, :] = dot(act_ref[k * T : (k + 1) * T, :], ws_ref[...]).astype(bf16)
    for k, p in enumerate((p1, p2, p3)):
        p[T:, :] = piece_ref[k]


def mlp_grads_kernel(perm_ref, left_ref, right_ref, left2_ref, right2_ref, g_ref):
    rows = dot_nt(perm_ref[...], left_ref[...]).astype(bf16)
    own = dot(rows, right_ref[...])
    rows = dot_nt(perm_ref[...], left2_ref[...]).astype(bf16)
    g_ref[...] = (own + dot(rows, right2_ref[...])).astype(bf16)


def backward_kernel(
    hid_ref, d0, d1, d2, d3, up_ref, vec_ref, wnat_ref, ot_ref, qt_ref, lse_ref, keys_ref, kvt_ref, qr_ref, info_ref,
    scal_ref, dkv_ref, dq_ref, dhid_ref, dhl_ref, sums_ref,
    rs_ref, rd_ref, dor_ref, dkv_acc, dqt_ref,
):
    xhat, rstd = normalize(hid_ref[...])
    d_mid = (
        d0[...].astype(f32) + d1[...].astype(f32) + d2[...].astype(f32) + d3[...].astype(f32)
    )
    up = up_ref[...].astype(f32)
    d_hidden = up + norm_back(xhat, rstd, d_mid, vec_ref[4:5])
    dhid_ref[...] = d_hidden
    dhid_ref.send()
    d_low = d_hidden.astype(bf16)
    d_att = dot_nt(d_low, wnat_ref[...]).astype(bf16).astype(f32)
    dhl_ref[...] = d_low
    dhl_ref.send()
    sums_ref[...] = jnp.concatenate(
        [
            jnp.sum(d_hidden, axis=0, keepdims=True),
            jnp.sum(d_mid * xhat, axis=0, keepdims=True),
            jnp.sum(d_mid, axis=0, keepdims=True),
            jnp.sum(up, axis=0, keepdims=True),
            jnp.zeros((4, D), f32),
        ],
        axis=0,
    )
    d_att_t = d_att.T
    for g in range(2):
        cols = pack_cols(d_att_t, g)
        delta = jnp.sum(cols * ot_ref[g], axis=0, keepdims=True)
        rd_ref[g] = jnp.zeros((4 * HD, ROWS), bf16)
        rd_ref[g, HD : 2 * HD, :] = cols.astype(bf16)
        rd_ref[g, 3 * HD : 3 * HD + 16, :] = three_parts(-delta)
        rs_ref[g] = qt_ref[g]
        rs_ref[g, 3 * HD : 3 * HD + 16, :] = three_parts(-lse_ref[g])
        rows = pack_rows(d_att, g)
        dor_ref[g] = jnp.concatenate([jnp.zeros((ROWS, HD), f32), rows], axis=1).astype(bf16)
    dkv_acc[...] = jnp.zeros(dkv_acc.shape, f32)
    dqt_ref[...] = jnp.zeros(dqt_ref.shape, f32)
    for ref in (keys_ref, kvt_ref, qr_ref, info_ref):
        ref.ready()
    parts = [slice(i * GRP, (i + 1) * GRP) for i in range(ROWS // GRP)]

    for g in range(2):

        def block(kb, carry, masked, g=g):
            k0 = pl.multiple_of(kb * BK, BK)
            keys = keys_ref[pl.ds(k0, BK), :]
            kt = kvt_ref[VROWS:, pl.ds(k0, BK)]
            acc = dkv_acc[pl.ds(k0, BK), :]
            pairs = [(dot(keys, rs_ref[g, :, cols]), dot(keys, rd_ref[g, :, cols])) for cols in parts]
            terms = []
            for (s, dp), cols in zip(pairs, parts, strict=True):
                p = jnp.exp2(s)
                if masked:
                    p = jnp.where(open_keys(s, k0, info_ref, g, cols), p, 0.0)
                terms.append((p.astype(bf16), (p * dp).astype(bf16)))
            products = []
            for (p, ds), cols in zip(terms, parts, strict=True):
                acc = acc + dot(p, dor_ref[g, cols, :]) + dot(ds, qr_ref[g, cols, :])
                products.append(dot(kt, ds))
            dkv_acc[pl.ds(k0, BK), :] = acc
            for product, cols in zip(products, parts, strict=True):
                dqt_ref[g, :, cols] += product
            return carry

        over_blocks(scal_ref, 8 + g * 4, block, 0)
    for i in range(NSEQ):
        dkv_ref[i, :HT, :] = dkv_acc[pl.ds(i * T, HT), :].astype(bf16)
        dkv_ref[NSEQ - 1 - i, HT:, :] = dkv_acc[pl.ds(i * T + HT, HT), :].astype(bf16)
    dkv_ref.send()
    for g in range(2):
        dq_ref[g * HT : (g + 1) * HT, :] = (unpack(dqt_ref[g]) * (1.0 / math.sqrt(HD))).astype(bf16)


def weight_grads_kernel(npt_ref, dq_ref, apt_ref, dhl_ref, qm_ref, qo_ref, om_ref, oo_ref):
    for left, right, mine, other in ((npt_ref, dq_ref, qm_ref, qo_ref), (apt_ref, dhl_ref, om_ref, oo_ref)):
        for lo, out in ((512, other), (0, mine)):
            out[...] = dot(left[lo : lo + 512, :], right[...]).astype(bf16)
            out.send()


def last_kernel(
    x_ref, vec_ref, dq_ref, wq_ref, wkv_ref, got_ref, dhid_ref, sums_ref, eb_ref, npt_ref, pad_ref, pe_ref,
    tg_ref, gm_ref, go_ref,
):
    xhat, rstd = normalize(x_ref[...].astype(f32))
    total = got_ref[0].astype(f32)
    for i in range(1, NSEQ):
        total = total + got_ref[i].astype(f32)
    owned = total.astype(bf16)
    d_normed = dot_nt(dq_ref[...], wq_ref[...]) + dot_nt(owned, wkv_ref[...])
    tg_ref[...] = dhid_ref[...] + norm_back(xhat, rstd, d_normed, vec_ref[0:1])
    tg_ref.send()
    rows = jnp.concatenate(
        [
            jnp.sum(d_normed * xhat, axis=0, keepdims=True),
            jnp.sum(d_normed, axis=0, keepdims=True),
            jnp.sum(dq_ref[...].astype(f32), axis=0, keepdims=True),
            sums_ref[0:1],
            sums_ref[1:2],
            sums_ref[2:3],
            sums_ref[3:4],
            jnp.zeros((1, D), f32),
        ],
        axis=0,
    ).astype(bf16)
    which = lax.broadcasted_iota(jnp.int32, (8, D), 1) % 24 // 6
    row = lax.broadcasted_iota(jnp.int32, (8, D), 0)
    ebs = jnp.where(which == row, jnp.broadcast_to(eb_ref[...], (8, D)), 0.0).astype(bf16)
    packed = jnp.concatenate(
        [dot(rows, pad_ref[...]), dot(ebs, pe_ref[...]), jnp.zeros((112, 1024), f32)], axis=0
    ).T
    kv = dot(npt_ref[...], owned).astype(bf16)
    for lo, out in ((512, go_ref), (0, gm_ref)):
        out[:, :T] = kv[lo : lo + 512]
        out[:, T:] = packed[lo : lo + 512].astype(bf16)
        out.send()


def shift(value, axis, by):
    size = lax.axis_size(axis)
    return lax.ppermute(value, axis, [(i, (i + by) % size) for i in range(size)])


def after(value, *others):
    return lax.optimization_barrier((value, *others))[0]


def spread(block, axis):
    return [block] + [shift(block, axis, k) for k in (1, 2, 3)]


def repeated(block, axes):
    count = math.prod(lax.axis_size(a) for a in axes)
    return jnp.broadcast_to(block[None], (count,) + block.shape)


def body(
    tokens,
    file_lengths,
    upstream,
    pre_gain,
    pre_shift,
    query_weight,
    query_bias,
    keyval_weight,
    value_bias,
    mixer_weight,
    mixer_bias,
    mid_gain,
    middle_norm_bias,
    expand_weight,
    expand_bias,
    shrink_weight,
    shrink_bias,
):
    z, c = lax.axis_index("z"), lax.axis_index("c")
    seq = lax.axis_index(SEQ)
    mirror = [(i, NSEQ - 1 - i) for i in range(NSEQ)]


    vectors = jnp.concatenate(
        [
            v.reshape(1, 6)
            for v in (
                pre_gain, pre_shift, query_bias, mixer_bias, mid_gain, middle_norm_bias, shrink_bias,
                jnp.zeros((6,), bf16),
            )
        ]
        + [expand_bias.reshape(4, 6)],
        axis=0,
    )
    vectors = jnp.pad(vectors.T, ((0, 0), (0, 116)))
    block = jnp.concatenate([keyval_weight, vectors, query_weight, mixer_weight], axis=1)
    block = jnp.pad(block, ((0, 2), (0, 0)))
    block = repeated(block, CHIPS)

    tokens, upstream, expand_weight = lax.optimization_barrier(
        (tokens, upstream, expand_weight, block)
    )[:3]
    w_mine = lax.all_to_all(block, CHIPS, 0, 0, tiled=True).reshape(512, AW)
    both = jnp.concatenate([tokens[0], upstream[0]], axis=1)
    far = lax.ppermute(both[HT:], SEQ, mirror)
    xu = jnp.concatenate([both[:HT], far], axis=0)

    columns, rows24 = expand_weight.reshape(6, 4, D), jnp.zeros((4, 6, D), bf16)
    for k in range(4):
        piece = lax.dynamic_index_in_dim(columns, (z + k) % 4, 1, keepdims=False)[None]
        if k:
            piece = shift(piece, "z", k)
        rows24 = lax.dynamic_update_slice_in_dim(rows24, piece, (z - k) % 4, 0)
    m_mine = jnp.concatenate([rows24.reshape(24, D), shrink_weight], axis=1)

    feat = jnp.arange(D, dtype=jnp.int32)[:, None]
    e = jnp.arange(1024, dtype=jnp.int32)[None, :]
    chip, r = e % 512 // 8, e % 8
    dev = 2 * chip + jnp.where(e < 512, c, 1 - c)
    pad = ((r < 6) & (feat == dev * 6 + r)).astype(bf16)
    pe = ((z * 32 + feat // 24 == dev) & (feat % 24 % 6 == r)).astype(bf16)

    of = jnp.arange(D, dtype=jnp.int32)[None, :]
    rest = of % 384 // 24 * 2 + jnp.where(of < 384, c, 1 - c)
    pm = (feat == (of % 24 // 6 * 32 + rest) * 6 + of % 6).astype(bf16)
    pu = (feat == rest * 24 + of % 24).astype(bf16)
    rest = feat // 24
    perm = (
        of == jnp.where(c == 0, (feat % 24 // 6 * 32 + rest) * 6 + feat % 6, rest * 24 + feat % 24)
    ).astype(bf16)

    lengths = file_lengths[0]
    ends = jnp.cumsum(lengths)
    local = jnp.arange(HT, dtype=jnp.int32)
    pos = jnp.stack([seq * T + local, (NSEQ - 1 - seq) * T + HT + local])
    past = pos[:, :, None] >= ends
    start = jnp.where(
        jnp.all(past, axis=-1), pos, jnp.sum(jnp.where(past, lengths, 0), axis=-1)
    )
    info = jnp.tile(jnp.stack([pos, start], axis=1), (1, 1, H))
    base = pos[:, 0]
    scal = []
    for size in (BK_FORWARD, BK):
        lo = jnp.min(start, axis=1) // size
        end = (base + HT - 1) // size + 1
        u0 = jnp.clip((jnp.max(start, axis=1) + size - 1) // size, lo, end)
        u1 = jnp.clip((base + 1) // size, u0, end)
        scal.append(jnp.stack([lo, u0, u1, end], axis=1))
    scal = jnp.stack(scal).reshape(16).astype(jnp.int32)

    vb = jnp.concatenate([jnp.zeros((HD,), f32), value_bias.astype(f32)])[None]
    w_mine, m_mine, xu, pad, pe, pm, pu, perm, info, scal, vb = lax.optimization_barrier(
        (w_mine, m_mine, xu, pad, pe, pm, pu, perm, info, scal, vb)
    )
    w_kv = [w_mine[:, :Q0]]
    w_kv.append(shift(w_kv[0], "c", 1))
    kv_out, normed, wkv, vec = call(
        first_kernel,
        [((NSEQ, T, 2 * HD), bf16), ((T, D), bf16), ((D, 2 * HD), bf16), ((16, D), f32)],
        ((xu, 0, D), Anywhere(w_kv[0]), Anywhere(w_kv[1]), pad, pe, vb),
    )
    kv_all = lax.all_to_all(kv_out, SEQ, 0, 0, tiled=True)
    w_qo = [after(w_mine, kv_out)[:, Q0:]]
    w_qo.append(shift(w_qo[0], "c", 1))
    m_all = repeated(after(m_mine, kv_out), SLICE)
    normed = after(normed, m_all)
    qt, qr, wq, wnat, npt = call(
        query_kernel,
        [
            ((2, 4 * HD, ROWS), bf16),
            ((2, ROWS, 2 * HD), bf16),
            ((D, D), bf16),
            ((D, D), bf16),
            ((1024, T), bf16),
        ],
        (normed, Anywhere(w_qo[0]), Anywhere(w_qo[1]), pad, vec),
    )
    kv_all, wnat, qt, m_all, xu = lax.optimization_barrier((kv_all, wnat, qt, m_all, xu))
    m_all = lax.all_to_all(m_all, SLICE, 0, 0, tiled=True).reshape(384, D2)
    ups = spread(xu[:, D:], "z")

    ot, lse, att, hidden, mid, keys, kvt = call(
        forward_kernel,
        [
            ((2, HD, ROWS), f32),
            ((2, 1, ROWS), f32),
            ((T, D), bf16),
            ((T, D), f32),
            ((T, D), bf16),
            ((WINDOW, 4 * HD), bf16),
            ((VROWS + HD, WINDOW), bf16),
        ],
        (kv_all, qt, info, (xu, 0, D), wnat, vec),
        [scal],
        scratch=[pltpu.VMEM((2, VROWS, ROWS), f32)],
    )
    m_all, mid, ups = lax.optimization_barrier((m_all, mid, ups))
    m_other = shift(m_all, "c", 1)
    mids = spread(mid, "z")
    we, ws, apt = call(
        weights_kernel,
        [((D, D), bf16), ((D, D), bf16), ((1024, T), bf16)],
        (att, pad, Anywhere(m_all), pm, pu, Anywhere(m_other)),
    )
    *ds, keep, send, act, eb = call(
        mlp_kernel,
        [((T, D), bf16)] * 4 + [((4 * T, D2), bf16)] * 2 + [((4 * T, D), bf16), ((1, D), f32)],
        (we, ws, vec, *ups, *mids),
        [jnp.stack([c]).astype(jnp.int32)],
        scratch=[pltpu.VMEM((4 * T, D), bf16)] * 3,
    )
    back = [ds[0]] + [shift(ds[k], "z", -k) for k in (1, 2, 3)]
    got = shift(send, "c", 1)
    (g_mlp,) = call(
        mlp_grads_kernel,
        [((D, D), bf16)],
        (perm, (keep, 0, D), (keep, D, D2), Anywhere((got, 0, D)), Anywhere((got, D, D2))),
    )
    back, g_mlp = lax.optimization_barrier((back, g_mlp))
    g_mlp = lax.all_to_all(g_mlp.reshape(16, 48, D), SLICE, 0, 0, tiled=True)

    dkv, dq, d_hidden, dh_low, sums = call(
        backward_kernel,
        [((NSEQ, T, 2 * HD), bf16), ((T, D), bf16), ((T, D), f32), ((T, D), bf16), ((8, D), f32)],
        (hidden, *back, (xu, D, D2), vec, wnat, ot, qt, lse, keys, kvt, qr, info),
        [scal],
        scratch=[
            pltpu.VMEM((2, 4 * HD, ROWS), bf16),
            pltpu.VMEM((2, 4 * HD, ROWS), bf16),
            pltpu.VMEM((2, ROWS, 2 * HD), bf16),
            pltpu.VMEM((WINDOW, 2 * HD), f32),
            pltpu.VMEM((2, HD, ROWS), f32),
        ],
    )
    dkv, dq, dh_low, g_mlp = lax.optimization_barrier((dkv, dq, dh_low, g_mlp))
    got = lax.all_to_all(dkv, SEQ, 0, 0, tiled=True)
    qm, qo, om, oo = call(weight_grads_kernel, [((512, D), bf16)] * 4, (npt, dq, apt, dh_low))
    qo, oo = shift(qo, "c", 1), shift(oo, "c", 1)
    both = jnp.sum(g_mlp.astype(f32), axis=0).reshape(2, 24, D)
    keep = lax.dynamic_index_in_dim(both, c, 0, keepdims=False)
    far = shift(lax.dynamic_index_in_dim(both, 1 - c, 0, keepdims=False), "c", 1)
    rows = jnp.where(c == 0, keep, far).reshape(4, 6, D)
    shrink_grad = jnp.where(c == 0, far, keep)
    rows = jnp.stack([lax.dynamic_index_in_dim(rows, (z + k) % 4, 0, keepdims=False) for k in range(4)])
    pieces = jnp.pad(rows[1:], ((0, 0), (0, 10), (0, 0))).astype(bf16)
    r0, *outs = call(
        result_kernel, [((T, D), bf16)] + [((T + 16, D), bf16)] * 3, (after(act, qm), ws, pieces)
    )
    got = after(got, r0)
    outs = [shift(o, "z", k) for k, o in zip((1, 2, 3), outs, strict=True)]
    tokens_grad, g_kv, kv_other = call(
        last_kernel,
        [((T, D), f32), ((512, Q0), bf16), ((512, Q0), bf16)],
        ((xu, 0, D), vec, dq, wq, wkv, Anywhere(got), d_hidden, sums, eb, npt, pad, pe),
    )
    result = hidden + r0.astype(f32) + sum(o[:T].astype(f32) for o in outs) + vec[6:7]
    far = jnp.concatenate([result[HT:], tokens_grad[HT:]], axis=1).astype(bf16)
    far = lax.ppermute(far, SEQ, mirror).astype(f32)
    result = jnp.concatenate([result[:HT], far[:, :D]], axis=0)
    tokens_grad = jnp.concatenate([tokens_grad[:HT], far[:, D:]], axis=0)
    expand_grad = jnp.zeros((6, 4 * D), f32)
    for k in range(4):
        piece = outs[k - 1][T : T + 6].astype(f32) if k else rows[0]
        expand_grad = lax.dynamic_update_slice_in_dim(expand_grad, piece, ((z - k) % 4) * D, 1)
    g_all = jnp.concatenate([g_kv + shift(kv_other, "c", 1), qm + qo, om + oo], axis=1)
    last = lax.all_to_all(g_all.reshape(64, 8, AW), CHIPS, 0, 0, tiled=True)
    last = jnp.sum(last.astype(f32), axis=0)

    vecs = last[:6, V0:Q0]
    return (
        result[None],
        tokens_grad[None],
        vecs[:, 0],
        vecs[:, 1],
        last[:6, Q0:O0],
        vecs[:, 2],
        last[:6, :V0],
        last[6, HD:V0],
        last[:6, O0:],
        vecs[:, 3],
        vecs[:, 4],
        vecs[:, 5],
        expand_grad,
        vecs[:, 8:12].T.reshape(24),
        shrink_grad,
        vecs[:, 6],
    )


def solution(mesh):
    grid = Mesh(mesh.devices.reshape(4, 2, 4, 2, 2), SEQ + WIN)
    every = SEQ + WIN
    rows, flat = P(every, None), P(every)
    tokens = P(WIN, SEQ, None)
    return jax.shard_map(
        body,
        mesh=grid,
        in_specs=(
            tokens, P(WIN, None), tokens, flat, flat, rows, flat, rows, P(), rows, flat, flat, flat, rows, flat, rows, flat,
        ),
        out_specs=(
            tokens, tokens, flat, flat, rows, flat, rows, P(), rows, flat, flat, flat, rows, flat, rows, flat,
        ),
        check_vma=False,
    )
```

```python
import functools
import math

import jax
import jax.numpy as jnp
from jax import lax
from jax.experimental import pallas as pl
from jax.experimental.pallas import tpu as pltpu
from jax.sharding import Mesh, PartitionSpec as P

bf16 = jnp.bfloat16
f32 = jnp.float32
D = 768
H = 12
HD = 64
T = 128
HT = 64
WINDOW = 4096
NSEQ = 32
ROWS = H * HT
BK_FORWARD = 512
BK = 256
VROWS = 80
GRP = 256
NEG = -1e30
EPS = 1e-5
SEQ = ("z", "yl", "x")
WIN = ("yh", "c")
ALL = SEQ + WIN
CHIPS = ("z", "yl", "x", "yh")
SLICE = ("yl", "x", "yh")
D2 = 2 * D
Q0, O0, AW = 128, 896, 1280
HALF = D // 2
HBM = pl.BlockSpec(memory_space=pltpu.HBM)
ANY = pl.BlockSpec(memory_space=pl.ANY)
VMEM = pl.BlockSpec(memory_space=pltpu.VMEM)


class Anywhere:
    def __init__(self, array):
        self.array = array


class Inside(Anywhere):
    pass


class Incoming:
    def __init__(self, source, ref, sem):
        self.ref, self.copy = ref, pltpu.make_async_copy(source, ref, sem)
        self.copy.start()

    def ready(self):
        if self.copy is not None:
            self.copy.wait()
            self.copy = None
        return self.ref

    def __getitem__(self, index):
        return self.ready()[index]


class Outgoing:
    def __init__(self, ref, target, sem):
        self.ref, self.copy, self.sent = ref, pltpu.make_async_copy(ref, target, sem), False

    def send(self):
        if not self.sent:
            self.copy.start()
            self.sent = True

    def __getitem__(self, index):
        return self.ref[index]

    def __setitem__(self, index, value):
        self.ref[index] = value


class Plain:
    def __init__(self, ref):
        self.ref = ref

    def ready(self):
        return self.ref

    def send(self):
        pass

    def __getitem__(self, index):
        return self.ref[index]

    def __setitem__(self, index, value):
        self.ref[index] = value


def call(kernel, outs, args, scalars=(), scratch=(), limit=20):
    kinds = [type(a) if isinstance(a, Anywhere) else None for a in args]
    parts = [a.array if isinstance(a, Anywhere) else a for a in args]
    parts = [a if isinstance(a, tuple) else (a, None, None) for a in parts]
    spaces = {None: pltpu.HBM, Inside: pltpu.VMEM}
    arrays = [
        p[0] if kind is Anywhere else pltpu.with_memory_space_constraint(p[0], spaces[kind])
        for p, kind in zip(parts, kinds, strict=True)
    ]
    inner = [len(o) == 3 for o in outs]
    n, m, k = len(arrays), len(outs), len(scalars)

    def shape(array, lo, hi):
        return array.shape if lo is None else array.shape[:-1] + (hi - lo,)

    moved = [i for i, kind in enumerate(kinds) if kind is not Inside]
    left = [i for i, here in enumerate(inner) if not here]

    def run(*refs):
        ins, small, results = refs[:n], refs[n : n + k], refs[n + k : n + k + m]
        rest = list(refs[n + k + m :])
        bufs = dict(zip(moved, rest, strict=False))
        out_bufs = dict(zip(left, rest[len(moved) :], strict=False))
        small_bufs = rest[len(moved) + len(left) :][:k]
        in_sem, out_sem, *extra = rest[len(moved) + len(left) + k :]
        small = [Incoming(r, b, in_sem.at[n + i]) for i, (r, b) in enumerate(zip(small, small_bufs, strict=True))]
        coming = []
        for i, (r, p) in enumerate(zip(ins, parts, strict=True)):
            if i in bufs:
                source = r if p[1] is None else r.at[..., pl.ds(p[1], p[2] - p[1])]
                coming.append(Incoming(source, bufs[i], in_sem.at[i]))
            else:
                coming.append(Plain(r))
        going = [
            Outgoing(out_bufs[i], r, out_sem.at[i]) if i in out_bufs else Plain(r)
            for i, r in enumerate(results)
        ]
        kernel(*coming, *small, *going, *extra)
        for c in coming + small:
            c.ready()
        for g in going:
            g.send()
        for g in going:
            if isinstance(g, Outgoing):
                g.copy.wait()

    specs = {None: HBM, Anywhere: ANY, Inside: VMEM}
    return pl.pallas_call(
        run,
        out_shape=[(pltpu.VMEM if here else pltpu.HBM)(*o[:2]) for o, here in zip(outs, inner, strict=True)],
        in_specs=[specs[kind] for kind in kinds] + [HBM] * k,
        out_specs=[VMEM if here else HBM for here in inner],
        scratch_shapes=[pltpu.VMEM(shape(*parts[i]), parts[i][0].dtype) for i in moved]
        + [pltpu.VMEM(*outs[i]) for i in left]
        + [pltpu.SMEM(a.shape, a.dtype) for a in scalars]
        + [pltpu.SemaphoreType.DMA((n + k,)), pltpu.SemaphoreType.DMA((m,))]
        + list(scratch),
        compiler_params=pltpu.CompilerParams(vmem_limit_bytes=limit * 1024 * 1024),
    )(*arrays, *(pltpu.with_memory_space_constraint(a, pltpu.HBM) for a in scalars))


def dot(a, b):
    return jnp.dot(a, b, preferred_element_type=f32)


def dot_nt(a, b):
    return lax.dot_general(a, b, (((1,), (1,)), ((), ())), preferred_element_type=f32)


def dot_tn(a, b):
    return lax.dot_general(a, b, (((0,), (0,)), ((), ())), preferred_element_type=f32)


def normalize(v):
    mean = jnp.mean(v, axis=-1, keepdims=True)
    centered = v - mean
    spread = jnp.mean(centered * centered, axis=-1, keepdims=True)
    rstd = lax.rsqrt(spread + EPS)
    return centered * rstd, rstd


def norm_back(xhat, rstd, d_out, gain):
    d_hat = d_out * gain
    return rstd * (
        d_hat
        - jnp.mean(d_hat, axis=-1, keepdims=True)
        - xhat * jnp.mean(d_hat * xhat, axis=-1, keepdims=True)
    )


def hot(target, group=1):
    return (lax.broadcasted_iota(jnp.int32, (D, 1), 0) // group == target).astype(bf16)


def hot_rows(target, group=1):
    return (lax.broadcasted_iota(jnp.int32, (1, D), 1) // group == target).astype(bf16)


def vector_places():
    lane = lax.broadcasted_iota(jnp.int32, (T, 1), 0)
    feat = lax.broadcasted_iota(jnp.int32, (1, D), 1)
    return (lane % 6 == feat % 6) & (lane < 48), lane == 48 + feat % 24


def first_kernel(x_ref, wm_ref, wo_ref, tgt_ref, vb_ref, kv_ref, normed_ref, wkv_ref, vec_ref, chunk_ref):
    xhat, _ = normalize(x_ref[...].astype(f32))
    chunk = jnp.concatenate([wm_ref[...].astype(f32).T, wo_ref[...].astype(f32).T], axis=1).astype(bf16)
    places, _ = vector_places()
    found = jnp.where(places, dot_nt(chunk, hot(tgt_ref[4:5, :], 6)), 0.0).astype(bf16)
    lane = lax.broadcasted_iota(jnp.int32, (16, T), 1)
    row = lax.broadcasted_iota(jnp.int32, (16, T), 0)
    vecs = dot(((lane // 6 == row) & (lane < 48)).astype(bf16), found)
    normed = (xhat * vecs[0:1] + vecs[1:2]).astype(bf16)
    wkv = dot(hot(tgt_ref[0:1, :512]), wm_ref[...]) + dot(hot(tgt_ref[0:1, 512:]), wo_ref[...])
    wkv = wkv.astype(bf16)
    kv = (dot(normed, wkv) + vb_ref[...]).astype(bf16)
    for i in range(NSEQ):
        kv_ref[i] = kv
    kv_ref.send()
    normed_ref[...] = normed
    wkv_ref[...] = wkv
    vec_ref[...] = vecs[0:8]
    chunk_ref[...] = chunk


def pack_cols(xt, g):
    return jnp.concatenate(
        [xt[h * HD : (h + 1) * HD, g * HT : (g + 1) * HT] for h in range(H)], axis=1
    )


def pack_rows(x, g):
    return jnp.concatenate(
        [x[g * HT : (g + 1) * HT, h * HD : (h + 1) * HD] for h in range(H)], axis=0
    )


def unpack(y):
    yt = y.T
    return jnp.concatenate([yt[h * HT : (h + 1) * HT] for h in range(H)], axis=1)


def query_kernel(
    normed_ref, wm_ref, wo_ref, tgt_ref, cols_ref, vec_ref, chunk_ref,
    qt_ref, qr_ref, wq_ref, wnat_ref, npt_ref, eb_ref,
):
    halves = ((wm_ref, slice(0, 512)), (wo_ref, slice(512, 1024)))
    picks = [hot(tgt_ref[0:1, at]) for _, at in halves]
    wq_ref[...] = sum(dot(p, w[:, :D]) for p, (w, _) in zip(picks, halves, strict=True)).astype(bf16)
    wq_ref.send()
    wnat_ref[:, :HALF] = sum(dot(p, w[:, D:]) for p, (w, _) in zip(picks, halves, strict=True)).astype(bf16)
    total = jnp.zeros((D, HALF), f32)
    for k in range(3):
        for w, at in halves:
            total = total + dot(hot(tgt_ref[1 + k : 2 + k, at]), w[:, k * HALF : (k + 1) * HALF])
    wnat_ref[:, HALF:] = total.astype(bf16)
    wnat_ref.send()
    q = (dot(normed_ref[...], wq_ref[...]) + vec_ref[2:3]).astype(bf16).astype(f32)
    qt = (q * (math.log2(math.e) / math.sqrt(HD))).T
    q = q * (1.0 / math.sqrt(HD))
    for g in range(2):
        cols = pack_cols(qt, g)
        high = cols.astype(bf16)
        qt_ref[g, :HD, :] = high
        qt_ref[g, HD:, :] = (cols - high.astype(f32)).astype(bf16)
        rows = pack_rows(q, g)
        qr_ref[g] = jnp.concatenate([rows, jnp.zeros((ROWS, HD), f32)], axis=1).astype(bf16)
    npt_ref[...] = dot_nt(hot_rows(cols_ref[:, 0:1]), normed_ref[...]).astype(bf16)
    _, places = vector_places()
    found = jnp.where(places, dot_nt(chunk_ref[...], hot(tgt_ref[5:6, :], 24)), 0.0)
    eb_ref[...] = jnp.broadcast_to(jnp.sum(found, axis=0, keepdims=True), (8, D))


def three_parts(row):
    first = row.astype(bf16)
    rest = row - first.astype(f32)
    second = rest.astype(bf16)
    third = (rest - second.astype(f32)).astype(bf16)
    at = lax.broadcasted_iota(jnp.int32, (16, row.shape[1]), 0)
    out = jnp.where(at == 0, first.astype(f32), 0.0)
    out = jnp.where(at == 1, second.astype(f32), out)
    return jnp.where(at == 2, third.astype(f32), out).astype(bf16)


def open_keys(s, k0, info_ref, g, cols):
    j = k0 + lax.broadcasted_iota(jnp.int32, s.shape, 0)
    return (j >= info_ref[g, 1:2, cols]) & (j <= info_ref[g, 0:1, cols])


def over_blocks(scal_ref, b, block, carry):
    lo, u0, u1, end = scal_ref[b], scal_ref[b + 1], scal_ref[b + 2], scal_ref[b + 3]
    for first, last, masked in ((lo, u0, True), (u0, u1, False), (u1, end, True)):
        carry = lax.fori_loop(
            first, last, lambda kb, value, masked=masked: block(kb, value, masked), carry
        )
    return carry


def spread_keys(kvs_ref, keys_ref):
    keys_ref[:, :T] = kvs_ref[...]
    lane = lax.broadcasted_iota(jnp.int32, (T, T), 1)
    for i in range(NSEQ):
        rows = pl.ds(i * T, T)
        keys_ref[rows, T:] = jnp.where(lane < HD, kvs_ref[rows, :].astype(f32), 1.0).astype(bf16)


def spread_query(qt_ref, rs_ref, g):
    rs_ref[g] = jnp.zeros((4 * HD, ROWS), bf16)
    rs_ref[g, :HD, :] = qt_ref[g, :HD, :]
    rs_ref[g, 2 * HD : 3 * HD, :] = qt_ref[g, HD:, :]


def forward_kernel(
    kv_ref, qt_ref, info_ref, x_ref, wnat_ref, vec_ref, scal_ref,
    ot_ref, lse_ref, att_ref, hid_ref, mid_ref, kvs_ref, kt_ref, keys_ref, vt_ref, rs_ref, acc_ref,
):
    for i in range(NSEQ):
        kvs_ref[pl.ds(i * T, T), :] = jnp.concatenate(
            [kv_ref[i, :HT], kv_ref[NSEQ - 1 - i, HT:]], axis=0
        )
    kvs_ref.send()
    spread_keys(kvs_ref, keys_ref)
    at = lax.broadcasted_iota(jnp.int32, (T, T), 0)
    lane = lax.broadcasted_iota(jnp.int32, (T, T), 1)
    pick = (lane == (at + HD) % T).astype(bf16)
    for i in range(NSEQ // 4):
        rows = pl.ds(i * 4 * T, 4 * T)
        turned = dot_nt(pick, kvs_ref[rows, :]).astype(bf16)
        vt_ref[:HD, rows] = turned[:HD]
        kt_ref[:, rows] = turned[HD:]
    vt_ref[HD:, :] = jnp.ones((VROWS - HD, WINDOW), bf16)
    kt_ref.send()
    acc_ref[...] = jnp.zeros(acc_ref.shape, f32)
    for g in range(2):
        spread_query(qt_ref, rs_ref, g)
    info_ref.ready()
    scal_ref.ready()
    parts = [slice(i * GRP, (i + 1) * GRP) for i in range(ROWS // GRP)]

    for g in range(2):

        def block(kb, carry, masked, g=g):
            k0 = pl.multiple_of(kb * BK_FORWARD, BK_FORWARD)
            keys = keys_ref[pl.ds(k0, BK_FORWARD), :]
            vt = vt_ref[:, pl.ds(k0, BK_FORWARD)]
            scores = [dot(keys, rs_ref[g, :, cols]) for cols in parts]
            new, products = [], []
            for s, cols, m_old in zip(scores, parts, carry, strict=True):
                if masked:
                    s = jnp.where(open_keys(s, k0, info_ref, g, cols), s, NEG)
                m_new = jnp.maximum(m_old, jnp.max(s, axis=0, keepdims=True))
                p = jnp.exp2(s - m_new)
                new.append(m_new)
                products.append((jnp.exp2(m_old - m_new), dot(vt, p.astype(bf16))))
            for cols, (alpha, product) in zip(parts, products, strict=True):
                acc_ref[g, :, cols] = acc_ref[g, :, cols] * alpha + product
            return tuple(new)

        start = tuple(jnp.full((1, GRP), NEG, f32) for _ in parts)
        done = over_blocks(scal_ref, g * 4, block, start)
        for cols, m in zip(parts, done, strict=True):
            total = acc_ref[g, HD : HD + 1, cols]
            ot_ref[g, :, cols] = acc_ref[g, :HD, cols] / total
            lse_ref[g, :, cols] = m + jnp.log2(total)
        att_ref[g * HT : (g + 1) * HT, :] = unpack(ot_ref[g]).astype(bf16)
    ot_ref.send()
    att_ref.send()
    hidden = x_ref[...].astype(f32) + dot(att_ref[...], wnat_ref[...]) + vec_ref[3:4]
    hid_ref[...] = hidden
    hid_ref.send()
    xhat, _ = normalize(hidden)
    mid_ref[...] = (xhat * vec_ref[4:5] + vec_ref[5:6]).astype(bf16)


def weights_kernel(att_ref, cols_ref, mm_ref, pm_ref, pu_ref, mo_ref, we_ref, ws_ref, apt_ref):
    for k in range(4):
        apt_ref[k] = dot_nt(hot_rows(cols_ref[:, k : k + 1]), att_ref[...]).astype(bf16)
    apt_ref.send()
    for out, perm, lo in ((we_ref, pm_ref, 0), (ws_ref, pu_ref, D)):
        cols = pl.ds(lo, D)
        out[...] = (
            dot(perm[:, :384], mm_ref[:, cols]) + dot(perm[:, 384:], mo_ref[:, cols])
        ).astype(bf16)
        out.send()


def mlp_kernel(
    n0, n1, n2, n3, we_ref, row_ref, u0, u1, u2, u3, ws_ref, c_ref,
    d0, d1, d2, d3, keep_ref, send_ref, act_ref, eb_ref, dp_ref, n_ref, u_ref,
):
    for k, (n, u) in enumerate(((n0, u0), (n1, u1), (n2, u2), (n3, u3))):
        u_ref[pl.ds(k * T, T), :] = u[...]
        n_ref[pl.ds(k * T, T), :] = n[...]
    c0 = math.sqrt(2.0 / math.pi)
    for lo in (0, 384):
        cols = pl.ds(lo, 384)
        pre = dot(n_ref[...], we_ref[:, cols]) + row_ref[0:1, cols]
        da = dot_nt(u_ref[...], ws_ref[cols, :])
        sq = pre * pre
        th = jnp.tanh(c0 * pre * (1.0 + 0.044715 * sq))
        up = 0.5 * (1.0 + th)
        act_ref[:, cols] = (pre * up).astype(bf16)
        slope = up + 0.5 * pre * (1.0 - th * th) * (c0 * (1.0 + 3 * 0.044715 * sq))
        dp_ref[:, cols] = (slope * da).astype(bf16)
    act_ref.send()
    eb_ref[...] = jnp.sum(dp_ref[...].astype(f32), axis=0, keepdims=True)
    eb_ref.send()
    dm = dot_nt(dp_ref[...], we_ref[...])
    for k, d in enumerate((d0, d1, d2, d3)):
        d[...] = dm[k * T : (k + 1) * T].astype(bf16)
        d.send()
    first = c_ref[0] == 0
    here, there = (keep_ref, send_ref), (send_ref, keep_ref)
    for when, (a, b) in ((first, here), (jnp.logical_not(first), there)):

        @pl.when(when)
        def _(a=a, b=b):
            a[:, :D] = n_ref[...]
            a[:, D:] = dp_ref[...]
            b[:, :D] = act_ref[...]
            b[:, D:] = u_ref[...]


def result_kernel(act_ref, ws_ref, r0, r1, r2, r3):
    for k, r in enumerate((r0, r1, r2, r3)):
        r[...] = dot(act_ref[k * T : (k + 1) * T, :], ws_ref[...]).astype(bf16)


def mlp_grads_kernel(perm_ref, keep_ref, got_ref, g_ref):
    rows = dot_nt(perm_ref[...], keep_ref[:, :D]).astype(bf16)
    own = dot(rows, keep_ref[:, D:])
    rows = dot_nt(perm_ref[...], got_ref[:, :D]).astype(bf16)
    g_ref[...] = (own + dot(rows, got_ref[:, D:])).astype(bf16)


def backward_kernel(
    hid_ref, d0, d1, d2, d3, up_ref, vec_ref, wnat_ref, ot_ref, qt_ref, lse_ref, kvs_ref, kt_ref, qr_ref, info_ref,
    scal_ref, dkv_ref, dq_ref, dhid_ref, dhl_ref, sums_ref,
    rs_ref, rd_ref, dor_ref, dkv_acc, dqt_ref, keys_ref,
):
    xhat, rstd = normalize(hid_ref[...])
    d_mid = (
        d0[...].astype(f32) + d1[...].astype(f32) + d2[...].astype(f32) + d3[...].astype(f32)
    )
    up = up_ref[...].astype(f32)
    d_hidden = up + norm_back(xhat, rstd, d_mid, vec_ref[4:5])
    dhid_ref[...] = d_hidden
    dhid_ref.send()
    d_low = d_hidden.astype(bf16)
    d_att = dot_nt(d_low, wnat_ref[...]).astype(bf16).astype(f32)
    dhl_ref[...] = d_low
    dhl_ref.send()
    sums_ref[...] = jnp.concatenate(
        [
            jnp.sum(d_hidden, axis=0, keepdims=True),
            jnp.sum(d_mid * xhat, axis=0, keepdims=True),
            jnp.sum(d_mid, axis=0, keepdims=True),
            jnp.sum(up, axis=0, keepdims=True),
            jnp.zeros((4, D), f32),
        ],
        axis=0,
    )
    d_att_t = d_att.T
    for g in range(2):
        cols = pack_cols(d_att_t, g)
        delta = jnp.sum(cols * ot_ref[g], axis=0, keepdims=True)
        rd_ref[g] = jnp.zeros((4 * HD, ROWS), bf16)
        rd_ref[g, HD : 2 * HD, :] = cols.astype(bf16)
        rd_ref[g, 3 * HD : 3 * HD + 16, :] = three_parts(-delta)
        spread_query(qt_ref, rs_ref, g)
        rs_ref[g, 3 * HD : 3 * HD + 16, :] = three_parts(-lse_ref[g])
        rows = pack_rows(d_att, g)
        dor_ref[g] = jnp.concatenate([jnp.zeros((ROWS, HD), f32), rows], axis=1).astype(bf16)
    dkv_acc[...] = jnp.zeros(dkv_acc.shape, f32)
    dqt_ref[...] = jnp.zeros(dqt_ref.shape, f32)
    spread_keys(kvs_ref, keys_ref)
    for ref in (kt_ref, qr_ref, info_ref, scal_ref):
        ref.ready()
    parts = [slice(i * GRP, (i + 1) * GRP) for i in range(ROWS // GRP)]

    for g in range(2):

        def block(kb, carry, masked, g=g):
            k0 = pl.multiple_of(kb * BK, BK)
            keys = keys_ref[pl.ds(k0, BK), :]
            kt = kt_ref[:, pl.ds(k0, BK)]
            acc = dkv_acc[pl.ds(k0, BK), :]
            pairs = [(dot(keys, rs_ref[g, :, cols]), dot(keys, rd_ref[g, :, cols])) for cols in parts]
            terms = []
            for (s, dp), cols in zip(pairs, parts, strict=True):
                p = jnp.exp2(s)
                if masked:
                    p = jnp.where(open_keys(s, k0, info_ref, g, cols), p, 0.0)
                terms.append((p.astype(bf16), (p * dp).astype(bf16)))
            products = []
            for (p, ds), cols in zip(terms, parts, strict=True):
                acc = acc + dot(p, dor_ref[g, cols, :]) + dot(ds, qr_ref[g, cols, :])
                products.append(dot(kt, ds))
            dkv_acc[pl.ds(k0, BK), :] = acc
            for product, cols in zip(products, parts, strict=True):
                dqt_ref[g, :, cols] += product
            return carry

        over_blocks(scal_ref, 8 + g * 4, block, 0)
    for i in range(NSEQ):
        dkv_ref[i, :HT, :] = dkv_acc[pl.ds(i * T, HT), :].astype(bf16)
        dkv_ref[NSEQ - 1 - i, HT:, :] = dkv_acc[pl.ds(i * T + HT, HT), :].astype(bf16)
    dkv_ref.send()
    for g in range(2):
        dq_ref[g * HT : (g + 1) * HT, :] = (unpack(dqt_ref[g]) * (1.0 / math.sqrt(HD))).astype(bf16)


def weight_grads_kernel(
    npt_ref, dq_ref, apt_ref, dhl_ref, mlp_ref, c_ref, m0, m1, m2, o0, o1, o2, keep_ref, send_ref
):
    later = dhl_ref[:, HALF:]
    for lo, outs in ((512, (o0, o1, o2)), (0, (m0, m1, m2))):
        rows = slice(lo, lo + 512)
        for k, out in enumerate(outs):
            cols = slice(k * HALF, (k + 1) * HALF)
            left, right = (npt_ref[rows, :], dq_ref[:, cols]) if k < 2 else (apt_ref[0, rows, :], dhl_ref[:, :HALF])
            left = jnp.concatenate([left, apt_ref[k + 1, rows, :]], axis=1)
            out[...] = dot(left, jnp.concatenate([right, later], axis=0)).astype(bf16)
            out.send()
    total = mlp_ref[0].astype(f32)
    for i in range(1, 16):
        total = total + mlp_ref[i].astype(f32)
    first = c_ref[0] == 0
    keep_ref[...] = jnp.where(first, total[:24], total[24:])
    send_ref[...] = jnp.where(first, total[24:], total[:24])


def last_kernel(
    x_ref, vec_ref, dq_ref, wq_ref, wkv_ref, got_ref, dhid_ref, sums_ref, eb_ref, npt_ref, cols_ref, keep_ref, far_ref,
    hid_ref, r0, r1, r2, r3, at_ref,
    res_ref, near_ref, both_ref, gm_ref, go_ref, shrink_ref, p0, p1, p2, p3, rows_ref,
):
    xhat, rstd = normalize(x_ref[...].astype(f32))
    total = got_ref[0].astype(f32)
    for i in range(1, NSEQ):
        total = total + got_ref[i].astype(f32)
    owned = total.astype(bf16)
    d_normed = dot_nt(dq_ref[...], wq_ref[...]) + dot_nt(owned, wkv_ref[...])
    grad = dhid_ref[...] + norm_back(xhat, rstd, d_normed, vec_ref[0:1])
    near_ref[...] = grad[:HT]
    both_ref[:, D:] = grad[HT:].astype(bf16)
    result = hid_ref[...] + vec_ref[6:7]
    for r in (r0, r1, r2, r3):
        result = result + r[...].astype(f32)
    res_ref[...] = result[:HT]
    both_ref[:, :D] = result[HT:].astype(bf16)
    for ref in (near_ref, res_ref, both_ref):
        ref.send()
    rows = jnp.concatenate(
        [
            jnp.sum(d_normed * xhat, axis=0, keepdims=True),
            jnp.sum(d_normed, axis=0, keepdims=True),
            jnp.sum(dq_ref[...].astype(f32), axis=0, keepdims=True),
            sums_ref[0:1],
            sums_ref[1:2],
            sums_ref[2:3],
            sums_ref[3:4],
            jnp.zeros((9, D), f32),
        ],
        axis=0,
    ).astype(bf16)
    places, bias_places = vector_places()
    lane = lax.broadcasted_iota(jnp.int32, (T, 16), 0)
    row = lax.broadcasted_iota(jnp.int32, (T, 16), 1)
    spread_rows = dot(((lane // 6 == row) & (lane < 48)).astype(bf16), rows)
    spread_rows = jnp.where(places, spread_rows, 0.0).astype(bf16)
    bias = jnp.where(bias_places, eb_ref[...], 0.0).astype(bf16)
    out = (
        dot(npt_ref[...], owned)
        + dot_nt(hot_rows(cols_ref[:, 4:5], 6), spread_rows)
        + dot_nt(hot_rows(cols_ref[:, 5:6], 24), bias)
    )
    sixth = lax.broadcasted_iota(jnp.int32, (1024, 1), 0) % 8 == 6
    out = jnp.where(sixth, jnp.sum(owned.astype(f32), axis=0, keepdims=True), out).astype(bf16)
    go_ref[...] = out[512:]
    go_ref.send()
    gm_ref[...] = out[:512]
    gm_ref.send()
    first = at_ref[0] == 0
    shrink_ref[...] = jnp.where(first, far_ref[...], keep_ref[...])
    rows = jnp.where(first, keep_ref[...], far_ref[...])
    for k in range(4):
        rows_ref[k] = jnp.concatenate([rows[6 * k : 6 * k + 6], jnp.zeros((2, D), f32)], axis=0)
    for k, p in enumerate((p0, p1, p2, p3)):
        p[...] = rows_ref[(at_ref[1] + k) % 4]


def shift(value, axis, by):
    size = lax.axis_size(axis)
    return lax.ppermute(value, axis, [(i, (i + by) % size) for i in range(size)])


def after(value, *others):
    return lax.optimization_barrier((value, *others))[0]


def spread(block, axis):
    return [block] + [shift(block, axis, k) for k in (1, 2, 3)]


def repeated(block, axes):
    count = math.prod(lax.axis_size(a) for a in axes)
    return jnp.broadcast_to(block[None], (count,) + block.shape)


def body(
    tokens,
    file_lengths,
    upstream,
    pre_gain,
    pre_shift,
    query_weight,
    query_bias,
    keyval_weight,
    value_bias,
    mixer_weight,
    mixer_bias,
    mid_gain,
    middle_norm_bias,
    expand_weight,
    expand_bias,
    shrink_weight,
    shrink_bias,
):
    z, c = lax.axis_index("z"), lax.axis_index("c")
    seq = lax.axis_index(SEQ)
    mirror = [(i, NSEQ - 1 - i) for i in range(NSEQ)]


    vectors = jnp.concatenate(
        [
            v.reshape(1, 6)
            for v in (
                pre_gain, pre_shift, query_bias, mixer_bias, mid_gain, middle_norm_bias, shrink_bias,
                jnp.zeros((6,), bf16),
            )
        ]
        + [expand_bias.reshape(4, 6)],
        axis=0,
    )
    vectors = jnp.pad(vectors.reshape(1, 72), ((1, 0), (0, T - 72)))
    block = jnp.concatenate(
        [
            jnp.concatenate([keyval_weight, query_weight, mixer_weight[:, :HALF]], axis=1),
            jnp.concatenate([vectors, mixer_weight[:, HALF:].reshape(2, 3 * HALF)], axis=1),
        ],
        axis=0,
    )
    block = repeated(block, CHIPS)

    tokens, upstream, expand_weight = lax.optimization_barrier(
        (tokens, upstream, expand_weight, block)
    )[:3]
    w_mine = lax.all_to_all(block, CHIPS, 0, 0, tiled=True).reshape(512, AW)
    both = jnp.concatenate([tokens[0], upstream[0]], axis=1)
    far = lax.ppermute(both[HT:], SEQ, mirror)
    x = jnp.concatenate([tokens[0, :HT], far[:, :D]], axis=0)
    up = jnp.concatenate([upstream[0, :HT], far[:, D:]], axis=0)

    columns = expand_weight.reshape(6, 4, D)
    rows6 = [lax.dynamic_index_in_dim(columns, (z + k) % 4, 1, keepdims=False)[None] for k in range(4)]
    rows6 = [rows6[0]] + [shift(rows6[k], "z", k) for k in (1, 2, 3)]
    rows24 = jnp.zeros((4, 6, D), bf16)
    for k in range(4):
        rows24 = lax.dynamic_update_slice_in_dim(rows24, rows6[k], (z - k) % 4, 0)
    m_all = repeated(jnp.concatenate([rows24.reshape(24, D), shrink_weight], axis=1), SLICE)

    at = jnp.stack([c, z]).astype(jnp.int32)

    feat = jnp.arange(D, dtype=jnp.int32)[:, None]
    e = jnp.arange(1024, dtype=jnp.int32)[None, :]
    chip, r = e % 512 // 8, e % 8
    dev = 2 * chip + jnp.where(e < 512, c, 1 - c)
    tgt = [jnp.where(r < 6, dev * 6 + r, -1)]
    tgt += [jnp.where(r == 6, dev * 6 + k, jnp.where(r == 7, dev * 6 + 3 + k, -1)) for k in range(3)]
    tgt += [jnp.where(r == 7, dev, -1), jnp.where((r == 7) & (dev // 32 == z), dev % 32, -1)]
    tgt = jnp.concatenate(tgt + [jnp.full((2, 1024), -1, jnp.int32)], axis=0)
    cols = tgt.T
    of = jnp.arange(D, dtype=jnp.int32)[None, :]
    rest = of % 384 // 24 * 2 + jnp.where(of < 384, c, 1 - c)
    pm = (feat == (of % 24 // 6 * 32 + rest) * 6 + of % 6).astype(bf16)
    pu = (feat == rest * 24 + of % 24).astype(bf16)
    rest = feat // 24
    perm = (
        of == jnp.where(c == 0, (feat % 24 // 6 * 32 + rest) * 6 + feat % 6, rest * 24 + feat % 24)
    ).astype(bf16)

    lengths = file_lengths[0]
    ends = jnp.cumsum(lengths)
    local = jnp.arange(HT, dtype=jnp.int32)
    pos = jnp.stack([seq * T + local, (NSEQ - 1 - seq) * T + HT + local])
    past = pos[:, :, None] >= ends
    start = jnp.where(
        jnp.all(past, axis=-1), pos, jnp.sum(jnp.where(past, lengths, 0), axis=-1)
    )
    info = jnp.tile(jnp.stack([pos, start], axis=1), (1, 1, H))
    base = pos[:, 0]
    scal = []
    for size in (BK_FORWARD, BK):
        lo = jnp.min(start, axis=1) // size
        end = (base + HT - 1) // size + 1
        u0 = jnp.clip((jnp.max(start, axis=1) + size - 1) // size, lo, end)
        u1 = jnp.clip((base + 1) // size, u0, end)
        scal.append(jnp.stack([lo, u0, u1, end], axis=1))
    scal = jnp.stack(scal).reshape(16).astype(jnp.int32)

    vb = jnp.concatenate([jnp.zeros((HD,), f32), value_bias.astype(f32)])[None]
    w_mine, x, m_all, tgt, cols, pm, pu, perm, info, scal, vb = lax.optimization_barrier(
        (w_mine, x, m_all, tgt, cols, pm, pu, perm, info, scal, vb)
    )
    w_kv = [w_mine[:, :Q0]]
    w_kv.append(shift(w_kv[0], "c", 1))
    kv_out, normed, wkv, vec, chunk = call(
        first_kernel,
        [
            ((NSEQ, T, 2 * HD), bf16),
            ((T, D), bf16),
            ((D, 2 * HD), bf16),
            ((8, D), f32),
            ((T, 1024), bf16),
        ],
        (x, *(Inside(w) for w in w_kv), tgt, vb),
    )
    kv_all = lax.all_to_all(kv_out, SEQ, 0, 0, tiled=True)
    w_qo = [after(w_mine, kv_out)[:, Q0:]]
    w_qo.append(shift(w_qo[0], "c", 1))
    qt, qr, wq, wnat, npt, eb_row = call(
        query_kernel,
        [
            ((2, 2 * HD, ROWS), bf16),
            ((2, ROWS, 2 * HD), bf16),
            ((D, D), bf16),
            ((D, D), bf16),
            ((1024, T), bf16),
            ((8, D), f32),
        ],
        (normed, Anywhere(w_qo[0]), Anywhere(w_qo[1]), tgt, cols, vec, chunk),
    )
    kv_all, wnat, qt, m_all, up = lax.optimization_barrier((kv_all, wnat, qt, m_all, up))
    m_all = lax.all_to_all(m_all, SLICE, 0, 0, tiled=True).reshape(384, D2)
    ups = spread(up, "z")

    ot, lse, att, hidden, mid, kvs, kt = call(
        forward_kernel,
        [
            ((2, HD, ROWS), f32),
            ((2, 1, ROWS), f32),
            ((T, D), bf16),
            ((T, D), f32),
            ((T, D), bf16),
            ((WINDOW, 2 * HD), bf16),
            ((HD, WINDOW), bf16),
        ],
        (Inside(kv_all), qt, info, x, wnat, vec),
        [scal],
        scratch=[
            pltpu.VMEM((WINDOW, 4 * HD), bf16),
            pltpu.VMEM((VROWS, WINDOW), bf16),
            pltpu.VMEM((2, 4 * HD, ROWS), bf16),
            pltpu.VMEM((2, VROWS, ROWS), f32),
        ],
    )
    m_all, mid, ups = lax.optimization_barrier((m_all, mid, ups))
    m_other = shift(m_all, "c", 1)
    mids = spread(mid, "z")
    we, ws, apt = call(
        weights_kernel,
        [((D, D), bf16, VMEM), ((D, D), bf16, VMEM), ((4, 1024, T), bf16)],
        (att, cols, Anywhere(m_all), pm, pu, Anywhere(m_other)),
    )
    *ds, keep, send, act, eb = call(
        mlp_kernel,
        [((T, D), bf16, VMEM)] * 4 + [((4 * T, D2), bf16, VMEM)] * 2 + [((4 * T, D), bf16), ((1, D), f32)],
        (*(Inside(n) for n in mids), Inside(we), eb_row, *(Inside(u) for u in ups), Inside(ws)),
        [at],
        scratch=[pltpu.VMEM((4 * T, D), bf16)] * 3,
    )
    back = [ds[0]] + [shift(ds[k], "z", -k) for k in (1, 2, 3)]
    got = shift(send, "c", 1)
    (g_mlp,) = call(
        mlp_grads_kernel,
        [((D, D), bf16)],
        (perm, Inside(keep), Inside(got)),
    )
    outs = call(result_kernel, [((T, D), bf16)] * 4, (act, Anywhere(ws)))
    back, g_mlp, outs = lax.optimization_barrier((back, g_mlp, outs))
    outs = [outs[0]] + [shift(outs[k], "z", -k) for k in (1, 2, 3)]
    g_mlp = lax.all_to_all(g_mlp.reshape(16, 48, D), SLICE, 0, 0, tiled=True)

    dkv, dq, d_hidden, dh_low, sums = call(
        backward_kernel,
        [((NSEQ, T, 2 * HD), bf16), ((T, D), bf16), ((T, D), f32), ((T, D), bf16, VMEM), ((8, D), f32)],
        (hidden, *(Inside(d) for d in back), up, vec, wnat, ot, qt, lse, kvs, kt, qr, info),
        [scal],
        scratch=[
            pltpu.VMEM((2, 4 * HD, ROWS), bf16),
            pltpu.VMEM((2, 4 * HD, ROWS), bf16),
            pltpu.VMEM((2, ROWS, 2 * HD), bf16),
            pltpu.VMEM((WINDOW, 2 * HD), f32),
            pltpu.VMEM((2, HD, ROWS), f32),
            pltpu.VMEM((WINDOW, 4 * HD), bf16),
        ],
    )
    dkv, dq, dh_low, g_mlp, outs = lax.optimization_barrier((dkv, dq, dh_low, g_mlp, outs))
    got = lax.all_to_all(dkv, SEQ, 0, 0, tiled=True)
    *g_qo, keep, send = call(
        weight_grads_kernel,
        [((512, HALF), bf16)] * 6 + [((24, D), f32)] * 2,
        (npt, dq, apt, Inside(dh_low), Anywhere(g_mlp)),
        [at],
    )
    other, far = [shift(g, "c", 1) for g in g_qo[3:]], shift(send, "c", 1)
    result, tokens_grad, both, g_kv, kv_other, shrink_grad, *pieces = call(
        last_kernel,
        [
            ((HT, D), f32),
            ((HT, D), f32),
            ((HT, D2), bf16),
            ((512, Q0), bf16, VMEM),
            ((512, Q0), bf16, VMEM),
            ((24, D), f32),
        ]
        + [((8, D), f32)] * 4,
        (x, vec, dq, wq, wkv, Inside(got), d_hidden, sums, eb, npt, cols, keep, far, hidden, *outs),
        [at],
        scratch=[pltpu.VMEM((4, 8, D), f32)],
    )
    pieces = [pieces[0]] + [shift(pieces[k], "z", k) for k in (1, 2, 3)]
    kv_other = shift(kv_other, "c", 1)
    g_all = jnp.concatenate([g_kv + kv_other] + [a + b for a, b in zip(g_qo, other)], axis=1)
    last = lax.all_to_all(g_all.reshape(64, 8, AW), CHIPS, 0, 0, tiled=True)
    last = jnp.sum(last.astype(f32), axis=0)
    expand_grad = jnp.zeros((6, 4 * D), f32)
    for k in range(4):
        expand_grad = lax.dynamic_update_slice_in_dim(expand_grad, pieces[k][:6], ((z - k) % 4) * D, 1)
    both = lax.ppermute(both, SEQ, mirror).astype(f32)
    result = jnp.concatenate([result, both[:, :D]], axis=0)
    tokens_grad = jnp.concatenate([tokens_grad, both[:, D:]], axis=0)

    mixer_grad = jnp.concatenate([last[:6, O0:], last[6:, Q0:].reshape(6, HALF)], axis=1)
    vecs = [last[7, 6 * k : 6 * k + 6] for k in range(7)]
    return (
        result[None],
        tokens_grad[None],
        vecs[0],
        vecs[1],
        last[:6, Q0:O0],
        vecs[2],
        last[:6, :Q0],
        last[6, HD:Q0],
        mixer_grad,
        vecs[3],
        vecs[4],
        vecs[5],
        expand_grad,
        last[7, 48:72],
        shrink_grad,
        vecs[6],
    )


def solution(mesh):
    grid = Mesh(mesh.devices.reshape(4, 2, 4, 2, 2), SEQ + WIN)
    every = SEQ + WIN
    rows, flat = P(every, None), P(every)
    tokens = P(WIN, SEQ, None)
    return jax.shard_map(
        body,
        mesh=grid,
        in_specs=(
            tokens, P(WIN, None), tokens, flat, flat, rows, flat, rows, P(), rows, flat, flat, flat, rows, flat, rows, flat,
        ),
        out_specs=(
            tokens, tokens, flat, flat, rows, flat, rows, P(), rows, flat, flat, flat, rows, flat, rows, flat,
        ),
        check_vma=False,
    )
```

```python
import functools
import math

import jax
import jax.numpy as jnp
from jax import lax
from jax.experimental import pallas as pl
from jax.experimental.pallas import tpu as pltpu
from jax.sharding import Mesh, PartitionSpec as P

bf16 = jnp.bfloat16
f32 = jnp.float32
D = 768
H = 12
HD = 64
T = 128
HT = 64
WINDOW = 4096
NSEQ = 32
ROWS = H * HT
BK_FORWARD = 512
BK = 256
VROWS = 80
GRP = 256
NEG = -1e30
EPS = 1e-5
SEQ = ("z", "yl", "x")
WIN = ("yh", "c")
ALL = SEQ + WIN
CHIPS = ("z", "yl", "x", "yh")
SLICE = ("yl", "x", "yh")
D2 = 2 * D
Q0, O0, AW = 128, 896, 1280
HALF = D // 2
HBM = pl.BlockSpec(memory_space=pltpu.HBM)
ANY = pl.BlockSpec(memory_space=pl.ANY)
VMEM = pl.BlockSpec(memory_space=pltpu.VMEM)


class Anywhere:
    def __init__(self, array):
        self.array = array


class Inside(Anywhere):
    pass


class Incoming:
    def __init__(self, source, ref, sem):
        self.ref, self.copy = ref, pltpu.make_async_copy(source, ref, sem)
        self.copy.start()

    def ready(self):
        if self.copy is not None:
            self.copy.wait()
            self.copy = None
        return self.ref

    def __getitem__(self, index):
        return self.ready()[index]


class Outgoing:
    def __init__(self, ref, target, sem):
        self.ref, self.copy, self.sent = ref, pltpu.make_async_copy(ref, target, sem), False

    def send(self):
        if not self.sent:
            self.copy.start()
            self.sent = True

    def __getitem__(self, index):
        return self.ref[index]

    def __setitem__(self, index, value):
        self.ref[index] = value


class Plain:
    def __init__(self, ref):
        self.ref = ref

    def ready(self):
        return self.ref

    def send(self):
        pass

    def __getitem__(self, index):
        return self.ref[index]

    def __setitem__(self, index, value):
        self.ref[index] = value


def call(kernel, outs, args, scalars=(), scratch=(), limit=20):
    kinds = [type(a) if isinstance(a, Anywhere) else None for a in args]
    parts = [a.array if isinstance(a, Anywhere) else a for a in args]
    parts = [a if isinstance(a, tuple) else (a, None, None) for a in parts]
    spaces = {None: pltpu.HBM, Inside: pltpu.VMEM}
    arrays = [
        p[0] if kind is Anywhere else pltpu.with_memory_space_constraint(p[0], spaces[kind])
        for p, kind in zip(parts, kinds, strict=True)
    ]
    inner = [len(o) == 3 for o in outs]
    n, m, k = len(arrays), len(outs), len(scalars)

    def shape(array, lo, hi):
        return array.shape if lo is None else array.shape[:-1] + (hi - lo,)

    moved = [i for i, kind in enumerate(kinds) if kind is not Inside]
    left = [i for i, here in enumerate(inner) if not here]

    def run(*refs):
        ins, small, results = refs[:n], refs[n : n + k], refs[n + k : n + k + m]
        rest = list(refs[n + k + m :])
        bufs = dict(zip(moved, rest, strict=False))
        out_bufs = dict(zip(left, rest[len(moved) :], strict=False))
        small_bufs = rest[len(moved) + len(left) :][:k]
        in_sem, out_sem, *extra = rest[len(moved) + len(left) + k :]
        small = [Incoming(r, b, in_sem.at[n + i]) for i, (r, b) in enumerate(zip(small, small_bufs, strict=True))]
        coming = []
        for i, (r, p) in enumerate(zip(ins, parts, strict=True)):
            if i in bufs:
                source = r if p[1] is None else r.at[..., pl.ds(p[1], p[2] - p[1])]
                coming.append(Incoming(source, bufs[i], in_sem.at[i]))
            else:
                coming.append(Plain(r))
        going = [
            Outgoing(out_bufs[i], r, out_sem.at[i]) if i in out_bufs else Plain(r)
            for i, r in enumerate(results)
        ]
        kernel(*coming, *small, *going, *extra)
        for c in coming + small:
            c.ready()
        for g in going:
            g.send()
        for g in going:
            if isinstance(g, Outgoing):
                g.copy.wait()

    specs = {None: HBM, Anywhere: ANY, Inside: VMEM}
    return pl.pallas_call(
        run,
        out_shape=[(pltpu.VMEM if here else pltpu.HBM)(*o[:2]) for o, here in zip(outs, inner, strict=True)],
        in_specs=[specs[kind] for kind in kinds] + [HBM] * k,
        out_specs=[VMEM if here else HBM for here in inner],
        scratch_shapes=[pltpu.VMEM(shape(*parts[i]), parts[i][0].dtype) for i in moved]
        + [pltpu.VMEM(*outs[i]) for i in left]
        + [pltpu.SMEM(a.shape, a.dtype) for a in scalars]
        + [pltpu.SemaphoreType.DMA((n + k,)), pltpu.SemaphoreType.DMA((m,))]
        + list(scratch),
        compiler_params=pltpu.CompilerParams(vmem_limit_bytes=limit * 1024 * 1024),
    )(*arrays, *(pltpu.with_memory_space_constraint(a, pltpu.HBM) for a in scalars))


def dot(a, b):
    return jnp.dot(a, b, preferred_element_type=f32)


def dot_nt(a, b):
    return lax.dot_general(a, b, (((1,), (1,)), ((), ())), preferred_element_type=f32)


def dot_tn(a, b):
    return lax.dot_general(a, b, (((0,), (0,)), ((), ())), preferred_element_type=f32)


def normalize(v):
    mean = jnp.mean(v, axis=-1, keepdims=True)
    centered = v - mean
    spread = jnp.mean(centered * centered, axis=-1, keepdims=True)
    rstd = lax.rsqrt(spread + EPS)
    return centered * rstd, rstd


def norm_back(xhat, rstd, d_out, gain):
    d_hat = d_out * gain
    return rstd * (
        d_hat
        - jnp.mean(d_hat, axis=-1, keepdims=True)
        - xhat * jnp.mean(d_hat * xhat, axis=-1, keepdims=True)
    )


def hot(target, group=1):
    return (lax.broadcasted_iota(jnp.int32, (D, 1), 0) // group == target).astype(bf16)


def hot_rows(target, group=1):
    return (lax.broadcasted_iota(jnp.int32, (1, D), 1) // group == target).astype(bf16)


def vector_places():
    lane = lax.broadcasted_iota(jnp.int32, (T, 1), 0)
    feat = lax.broadcasted_iota(jnp.int32, (1, D), 1)
    return (lane % 6 == feat % 6) & (lane < 48), lane == 48 + feat % 24


def first_kernel(x_ref, wm_ref, wo_ref, tgt_ref, vb_ref, kv_ref, normed_ref, wkv_ref, vec_ref, chunk_ref):
    xhat, _ = normalize(x_ref[...].astype(f32))
    chunk = jnp.concatenate([wm_ref[...].astype(f32).T, wo_ref[...].astype(f32).T], axis=1).astype(bf16)
    places, _ = vector_places()
    found = jnp.where(places, dot_nt(chunk, hot(tgt_ref[4:5, :], 6)), 0.0).astype(bf16)
    lane = lax.broadcasted_iota(jnp.int32, (16, T), 1)
    row = lax.broadcasted_iota(jnp.int32, (16, T), 0)
    vecs = dot(((lane // 6 == row) & (lane < 48)).astype(bf16), found)
    normed = (xhat * vecs[0:1] + vecs[1:2]).astype(bf16)
    wkv = dot(hot(tgt_ref[0:1, :512]), wm_ref[...]) + dot(hot(tgt_ref[0:1, 512:]), wo_ref[...])
    wkv = wkv.astype(bf16)
    kv = (dot(normed, wkv) + vb_ref[...]).astype(bf16)
    for i in range(NSEQ):
        kv_ref[i] = kv
    kv_ref.send()
    normed_ref[...] = normed
    wkv_ref[...] = wkv
    vec_ref[...] = vecs[0:8]
    chunk_ref[...] = chunk


def pack_cols(xt, g):
    return jnp.concatenate(
        [xt[h * HD : (h + 1) * HD, g * HT : (g + 1) * HT] for h in range(H)], axis=1
    )


def pack_rows(x, g):
    return jnp.concatenate(
        [x[g * HT : (g + 1) * HT, h * HD : (h + 1) * HD] for h in range(H)], axis=0
    )


def unpack(y):
    yt = y.T
    return jnp.concatenate([yt[h * HT : (h + 1) * HT] for h in range(H)], axis=1)


def query_kernel(
    normed_ref, wm_ref, wo_ref, tgt_ref, cols_ref, vec_ref, chunk_ref,
    qt_ref, qr_ref, wq_ref, wnat_ref, npt_ref, eb_ref,
):
    halves = ((wm_ref, slice(0, 512)), (wo_ref, slice(512, 1024)))
    picks = [hot(tgt_ref[0:1, at]) for _, at in halves]
    wq_ref[...] = sum(dot(p, w[:, :D]) for p, (w, _) in zip(picks, halves, strict=True)).astype(bf16)
    wq_ref.send()
    wnat_ref[:, :HALF] = sum(dot(p, w[:, D:]) for p, (w, _) in zip(picks, halves, strict=True)).astype(bf16)
    total = jnp.zeros((D, HALF), f32)
    for k in range(3):
        for w, at in halves:
            total = total + dot(hot(tgt_ref[1 + k : 2 + k, at]), w[:, k * HALF : (k + 1) * HALF])
    wnat_ref[:, HALF:] = total.astype(bf16)
    wnat_ref.send()
    q = (dot(normed_ref[...], wq_ref[...]) + vec_ref[2:3]).astype(bf16).astype(f32)
    qt = (q * (math.log2(math.e) / math.sqrt(HD))).T
    q = q * (1.0 / math.sqrt(HD))
    for g in range(2):
        cols = pack_cols(qt, g)
        high = cols.astype(bf16)
        qt_ref[g, :HD, :] = high
        qt_ref[g, HD:, :] = (cols - high.astype(f32)).astype(bf16)
        rows = pack_rows(q, g)
        qr_ref[g] = jnp.concatenate([rows, jnp.zeros((ROWS, HD), f32)], axis=1).astype(bf16)
    npt_ref[...] = dot_nt(hot_rows(cols_ref[:, 0:1]), normed_ref[...]).astype(bf16)
    _, places = vector_places()
    found = jnp.where(places, dot_nt(chunk_ref[...], hot(tgt_ref[5:6, :], 24)), 0.0)
    eb_ref[...] = jnp.broadcast_to(jnp.sum(found, axis=0, keepdims=True), (8, D))


def three_parts(row):
    first = row.astype(bf16)
    rest = row - first.astype(f32)
    second = rest.astype(bf16)
    third = (rest - second.astype(f32)).astype(bf16)
    at = lax.broadcasted_iota(jnp.int32, (16, row.shape[1]), 0)
    out = jnp.where(at == 0, first.astype(f32), 0.0)
    out = jnp.where(at == 1, second.astype(f32), out)
    return jnp.where(at == 2, third.astype(f32), out).astype(bf16)


def open_keys(s, k0, info_ref, g, cols):
    j = k0 + lax.broadcasted_iota(jnp.int32, s.shape, 0)
    return (j >= info_ref[g, 1:2, cols]) & (j <= info_ref[g, 0:1, cols])


def over_blocks(scal_ref, b, block, carry):
    lo, u0, u1, end = scal_ref[b], scal_ref[b + 1], scal_ref[b + 2], scal_ref[b + 3]
    for first, last, masked in ((lo, u0, True), (u0, u1, False), (u1, end, True)):
        carry = lax.fori_loop(
            first, last, lambda kb, value, masked=masked: block(kb, value, masked), carry
        )
    return carry


def spread_keys(kvs_ref, keys_ref):
    keys_ref[:, :T] = kvs_ref[...]
    lane = lax.broadcasted_iota(jnp.int32, (T, T), 1)
    for i in range(NSEQ):
        rows = pl.ds(i * T, T)
        keys_ref[rows, T:] = jnp.where(lane < HD, kvs_ref[rows, :].astype(f32), 1.0).astype(bf16)


def spread_query(qt_ref, rs_ref, g):
    rs_ref[g] = jnp.zeros((4 * HD, ROWS), bf16)
    rs_ref[g, :HD, :] = qt_ref[g, :HD, :]
    rs_ref[g, 2 * HD : 3 * HD, :] = qt_ref[g, HD:, :]


def forward_kernel(
    kv_ref, qt_ref, info_ref, x_ref, wnat_ref, vec_ref, scal_ref,
    ot_ref, lse_ref, att_ref, hid_ref, mid_ref, kvs_ref, kt_ref, keys_ref, vt_ref, rs_ref, acc_ref,
):
    for i in range(NSEQ):
        kvs_ref[pl.ds(i * T, T), :] = jnp.concatenate(
            [kv_ref[i, :HT], kv_ref[NSEQ - 1 - i, HT:]], axis=0
        )
    kvs_ref.send()
    spread_keys(kvs_ref, keys_ref)
    at = lax.broadcasted_iota(jnp.int32, (T, T), 0)
    lane = lax.broadcasted_iota(jnp.int32, (T, T), 1)
    pick = (lane == (at + HD) % T).astype(bf16)
    for i in range(NSEQ // 4):
        rows = pl.ds(i * 4 * T, 4 * T)
        turned = dot_nt(pick, kvs_ref[rows, :]).astype(bf16)
        vt_ref[:HD, rows] = turned[:HD]
        kt_ref[:, rows] = turned[HD:]
    vt_ref[HD:, :] = jnp.ones((VROWS - HD, WINDOW), bf16)
    kt_ref.send()
    acc_ref[...] = jnp.zeros(acc_ref.shape, f32)
    for g in range(2):
        spread_query(qt_ref, rs_ref, g)
    info_ref.ready()
    scal_ref.ready()
    parts = [slice(i * GRP, (i + 1) * GRP) for i in range(ROWS // GRP)]

    for g in range(2):

        def block(kb, carry, masked, g=g):
            k0 = pl.multiple_of(kb * BK_FORWARD, BK_FORWARD)
            keys = keys_ref[pl.ds(k0, BK_FORWARD), :]
            vt = vt_ref[:, pl.ds(k0, BK_FORWARD)]
            scores = [dot(keys, rs_ref[g, :, cols]) for cols in parts]
            new, products = [], []
            for s, cols, m_old in zip(scores, parts, carry, strict=True):
                if masked:
                    s = jnp.where(open_keys(s, k0, info_ref, g, cols), s, NEG)
                m_new = jnp.maximum(m_old, jnp.max(s, axis=0, keepdims=True))
                p = jnp.exp2(s - m_new)
                new.append(m_new)
                products.append((jnp.exp2(m_old - m_new), dot(vt, p.astype(bf16))))
            for cols, (alpha, product) in zip(parts, products, strict=True):
                acc_ref[g, :, cols] = acc_ref[g, :, cols] * alpha + product
            return tuple(new)

        start = tuple(jnp.full((1, GRP), NEG, f32) for _ in parts)
        done = over_blocks(scal_ref, g * 4, block, start)
        for cols, m in zip(parts, done, strict=True):
            total = acc_ref[g, HD : HD + 1, cols]
            ot_ref[g, :, cols] = acc_ref[g, :HD, cols] / total
            lse_ref[g, :, cols] = m + jnp.log2(total)
        att_ref[g * HT : (g + 1) * HT, :] = unpack(ot_ref[g]).astype(bf16)
    ot_ref.send()
    att_ref.send()
    hidden = x_ref[...].astype(f32) + dot(att_ref[...], wnat_ref[...]) + vec_ref[3:4]
    hid_ref[...] = hidden
    hid_ref.send()
    xhat, _ = normalize(hidden)
    mid_ref[...] = (xhat * vec_ref[4:5] + vec_ref[5:6]).astype(bf16)


def weights_kernel(mm_ref, pm_ref, pu_ref, mo_ref, we_ref, ws_ref):
    for out, perm, lo in ((we_ref, pm_ref, 0), (ws_ref, pu_ref, D)):
        cols = pl.ds(lo, D)
        out[...] = (
            dot(perm[:, :384], mm_ref[:, cols]) + dot(perm[:, 384:], mo_ref[:, cols])
        ).astype(bf16)
        out.send()


def mlp_kernel(
    n0, n1, n2, n3, we_ref, row_ref, u0, u1, u2, u3, ws_ref, c_ref,
    d0, d1, d2, d3, keep_ref, send_ref, act_ref, eb_ref, dp_ref, n_ref, u_ref,
):
    for k, (n, u) in enumerate(((n0, u0), (n1, u1), (n2, u2), (n3, u3))):
        u_ref[pl.ds(k * T, T), :] = u[...]
        n_ref[pl.ds(k * T, T), :] = n[...]
    c0 = math.sqrt(2.0 / math.pi)
    for lo in (0, 384):
        cols = pl.ds(lo, 384)
        pre = dot(n_ref[...], we_ref[:, cols]) + row_ref[0:1, cols]
        da = dot_nt(u_ref[...], ws_ref[cols, :])
        sq = pre * pre
        th = jnp.tanh(c0 * pre * (1.0 + 0.044715 * sq))
        up = 0.5 * (1.0 + th)
        act_ref[:, cols] = (pre * up).astype(bf16)
        slope = up + 0.5 * pre * (1.0 - th * th) * (c0 * (1.0 + 3 * 0.044715 * sq))
        dp_ref[:, cols] = (slope * da).astype(bf16)
    act_ref.send()
    eb_ref[...] = jnp.sum(dp_ref[...].astype(f32), axis=0, keepdims=True)
    eb_ref.send()
    dm = dot_nt(dp_ref[...], we_ref[...])
    for k, d in enumerate((d0, d1, d2, d3)):
        d[...] = dm[k * T : (k + 1) * T].astype(bf16)
        d.send()
    first = c_ref[0] == 0
    here, there = (keep_ref, send_ref), (send_ref, keep_ref)
    for when, (a, b) in ((first, here), (jnp.logical_not(first), there)):

        @pl.when(when)
        def _(a=a, b=b):
            a[:, :D] = n_ref[...]
            a[:, D:] = dp_ref[...]
            b[:, :D] = act_ref[...]
            b[:, D:] = u_ref[...]


def result_kernel(act_ref, ws_ref, r0, r1, r2, r3):
    for k, r in enumerate((r0, r1, r2, r3)):
        r[...] = dot(act_ref[k * T : (k + 1) * T, :], ws_ref[...]).astype(bf16)


def mlp_grads_kernel(perm_ref, keep_ref, got_ref, g_ref):
    rows = dot_nt(perm_ref[...], keep_ref[:, :D]).astype(bf16)
    own = dot(rows, keep_ref[:, D:])
    rows = dot_nt(perm_ref[...], got_ref[:, :D]).astype(bf16)
    g_ref[...] = (own + dot(rows, got_ref[:, D:])).astype(bf16)


def backward_kernel(
    hid_ref, d0, d1, d2, d3, up_ref, vec_ref, wnat_ref, ot_ref, qt_ref, lse_ref, kvs_ref, kt_ref, qr_ref, info_ref,
    scal_ref, dkv_ref, dq_ref, dhid_ref, dhl_ref, sums_ref,
    rs_ref, rd_ref, dor_ref, dkv_acc, dqt_ref, keys_ref,
):
    xhat, rstd = normalize(hid_ref[...])
    d_mid = (
        d0[...].astype(f32) + d1[...].astype(f32) + d2[...].astype(f32) + d3[...].astype(f32)
    )
    up = up_ref[...].astype(f32)
    d_hidden = up + norm_back(xhat, rstd, d_mid, vec_ref[4:5])
    dhid_ref[...] = d_hidden
    dhid_ref.send()
    d_low = d_hidden.astype(bf16)
    d_att = dot_nt(d_low, wnat_ref[...]).astype(bf16).astype(f32)
    dhl_ref[...] = d_low
    dhl_ref.send()
    sums_ref[...] = jnp.concatenate(
        [
            jnp.sum(d_hidden, axis=0, keepdims=True),
            jnp.sum(d_mid * xhat, axis=0, keepdims=True),
            jnp.sum(d_mid, axis=0, keepdims=True),
            jnp.sum(up, axis=0, keepdims=True),
            jnp.zeros((4, D), f32),
        ],
        axis=0,
    )
    d_att_t = d_att.T
    for g in range(2):
        cols = pack_cols(d_att_t, g)
        delta = jnp.sum(cols * ot_ref[g], axis=0, keepdims=True)
        rd_ref[g] = jnp.zeros((4 * HD, ROWS), bf16)
        rd_ref[g, HD : 2 * HD, :] = cols.astype(bf16)
        rd_ref[g, 3 * HD : 3 * HD + 16, :] = three_parts(-delta)
        spread_query(qt_ref, rs_ref, g)
        rs_ref[g, 3 * HD : 3 * HD + 16, :] = three_parts(-lse_ref[g])
        rows = pack_rows(d_att, g)
        dor_ref[g] = jnp.concatenate([jnp.zeros((ROWS, HD), f32), rows], axis=1).astype(bf16)
    dkv_acc[...] = jnp.zeros(dkv_acc.shape, f32)
    dqt_ref[...] = jnp.zeros(dqt_ref.shape, f32)
    spread_keys(kvs_ref, keys_ref)
    for ref in (kt_ref, qr_ref, info_ref, scal_ref):
        ref.ready()
    parts = [slice(i * GRP, (i + 1) * GRP) for i in range(ROWS // GRP)]

    for g in range(2):

        def block(kb, carry, masked, g=g):
            k0 = pl.multiple_of(kb * BK, BK)
            keys = keys_ref[pl.ds(k0, BK), :]
            kt = kt_ref[:, pl.ds(k0, BK)]
            acc = dkv_acc[pl.ds(k0, BK), :]
            pairs = [(dot(keys, rs_ref[g, :, cols]), dot(keys, rd_ref[g, :, cols])) for cols in parts]
            terms = []
            for (s, dp), cols in zip(pairs, parts, strict=True):
                p = jnp.exp2(s)
                if masked:
                    p = jnp.where(open_keys(s, k0, info_ref, g, cols), p, 0.0)
                terms.append((p.astype(bf16), (p * dp).astype(bf16)))
            products = []
            for (p, ds), cols in zip(terms, parts, strict=True):
                acc = acc + dot(p, dor_ref[g, cols, :]) + dot(ds, qr_ref[g, cols, :])
                products.append(dot(kt, ds))
            dkv_acc[pl.ds(k0, BK), :] = acc
            for product, cols in zip(products, parts, strict=True):
                dqt_ref[g, :, cols] += product
            return carry

        over_blocks(scal_ref, 8 + g * 4, block, 0)
    for i in range(NSEQ):
        dkv_ref[i, :HT, :] = dkv_acc[pl.ds(i * T, HT), :].astype(bf16)
        dkv_ref[NSEQ - 1 - i, HT:, :] = dkv_acc[pl.ds(i * T + HT, HT), :].astype(bf16)
    dkv_ref.send()
    for g in range(2):
        dq_ref[g * HT : (g + 1) * HT, :] = (unpack(dqt_ref[g]) * (1.0 / math.sqrt(HD))).astype(bf16)


def weight_grads_kernel(
    cols_ref, att_ref, npt_ref, dq_ref, dhl_ref, mlp_ref, c_ref, m0, m1, m2, o0, o1, o2, keep_ref, send_ref, apt_ref
):
    for k in range(4):
        apt_ref[k] = dot_nt(hot_rows(cols_ref[:, k : k + 1]), att_ref[...]).astype(bf16)
    later = dhl_ref[:, HALF:]
    for lo, outs in ((512, (o0, o1, o2)), (0, (m0, m1, m2))):
        rows = slice(lo, lo + 512)
        for k, out in enumerate(outs):
            cols = slice(k * HALF, (k + 1) * HALF)
            left, right = (npt_ref[rows, :], dq_ref[:, cols]) if k < 2 else (apt_ref[0, rows, :], dhl_ref[:, :HALF])
            left = jnp.concatenate([left, apt_ref[k + 1, rows, :]], axis=1)
            out[...] = dot(left, jnp.concatenate([right, later], axis=0)).astype(bf16)
            out.send()
    total = mlp_ref[0].astype(f32)
    for i in range(1, 16):
        total = total + mlp_ref[i].astype(f32)
    first = c_ref[0] == 0
    keep_ref[...] = jnp.where(first, total[:24], total[24:])
    send_ref[...] = jnp.where(first, total[24:], total[:24])


def last_kernel(
    x_ref, vec_ref, dq_ref, wq_ref, wkv_ref, got_ref, dhid_ref, sums_ref, eb_ref, npt_ref, cols_ref, keep_ref, far_ref,
    hid_ref, r0, r1, r2, r3, at_ref,
    res_ref, near_ref, both_ref, gm_ref, go_ref, shrink_ref, p0, p1, p2, p3, rows_ref,
):
    xhat, rstd = normalize(x_ref[...].astype(f32))
    total = got_ref[0].astype(f32)
    for i in range(1, NSEQ):
        total = total + got_ref[i].astype(f32)
    owned = total.astype(bf16)
    d_normed = dot_nt(dq_ref[...], wq_ref[...]) + dot_nt(owned, wkv_ref[...])
    grad = dhid_ref[...] + norm_back(xhat, rstd, d_normed, vec_ref[0:1])
    near_ref[...] = grad[:HT]
    both_ref[:, D:] = grad[HT:].astype(bf16)
    result = hid_ref[...] + vec_ref[6:7]
    for r in (r0, r1, r2, r3):
        result = result + r[...].astype(f32)
    res_ref[...] = result[:HT]
    both_ref[:, :D] = result[HT:].astype(bf16)
    for ref in (near_ref, res_ref, both_ref):
        ref.send()
    rows = jnp.concatenate(
        [
            jnp.sum(d_normed * xhat, axis=0, keepdims=True),
            jnp.sum(d_normed, axis=0, keepdims=True),
            jnp.sum(dq_ref[...].astype(f32), axis=0, keepdims=True),
            sums_ref[0:1],
            sums_ref[1:2],
            sums_ref[2:3],
            sums_ref[3:4],
            jnp.zeros((9, D), f32),
        ],
        axis=0,
    ).astype(bf16)
    places, bias_places = vector_places()
    lane = lax.broadcasted_iota(jnp.int32, (T, 16), 0)
    row = lax.broadcasted_iota(jnp.int32, (T, 16), 1)
    spread_rows = dot(((lane // 6 == row) & (lane < 48)).astype(bf16), rows)
    spread_rows = jnp.where(places, spread_rows, 0.0).astype(bf16)
    bias = jnp.where(bias_places, eb_ref[...], 0.0).astype(bf16)
    out = (
        dot(npt_ref[...], owned)
        + dot_nt(hot_rows(cols_ref[:, 4:5], 6), spread_rows)
        + dot_nt(hot_rows(cols_ref[:, 5:6], 24), bias)
    )
    sixth = lax.broadcasted_iota(jnp.int32, (1024, 1), 0) % 8 == 6
    out = jnp.where(sixth, jnp.sum(owned.astype(f32), axis=0, keepdims=True), out).astype(bf16)
    go_ref[...] = out[512:]
    go_ref.send()
    gm_ref[...] = out[:512]
    gm_ref.send()
    first = at_ref[0] == 0
    shrink_ref[...] = jnp.where(first, far_ref[...], keep_ref[...])
    rows = jnp.where(first, keep_ref[...], far_ref[...])
    for k in range(4):
        rows_ref[k] = jnp.concatenate([rows[6 * k : 6 * k + 6], jnp.zeros((2, D), f32)], axis=0)
    for k, p in enumerate((p0, p1, p2, p3)):
        p[...] = rows_ref[(at_ref[1] + k) % 4]


def shift(value, axis, by):
    size = lax.axis_size(axis)
    return lax.ppermute(value, axis, [(i, (i + by) % size) for i in range(size)])


def after(value, *others):
    return lax.optimization_barrier((value, *others))[0]


def spread(block, axis):
    return [block] + [shift(block, axis, k) for k in (1, 2, 3)]


def repeated(block, axes):
    count = math.prod(lax.axis_size(a) for a in axes)
    return jnp.broadcast_to(block[None], (count,) + block.shape)


def body(
    tokens,
    file_lengths,
    upstream,
    pre_gain,
    pre_shift,
    query_weight,
    query_bias,
    keyval_weight,
    value_bias,
    mixer_weight,
    mixer_bias,
    mid_gain,
    middle_norm_bias,
    expand_weight,
    expand_bias,
    shrink_weight,
    shrink_bias,
):
    z, c = lax.axis_index("z"), lax.axis_index("c")
    seq = lax.axis_index(SEQ)
    mirror = [(i, NSEQ - 1 - i) for i in range(NSEQ)]


    vectors = jnp.concatenate(
        [
            v.reshape(1, 6)
            for v in (
                pre_gain, pre_shift, query_bias, mixer_bias, mid_gain, middle_norm_bias, shrink_bias,
                jnp.zeros((6,), bf16),
            )
        ]
        + [expand_bias.reshape(4, 6)],
        axis=0,
    )
    vectors = jnp.pad(vectors.reshape(1, 72), ((1, 0), (0, T - 72)))
    block = jnp.concatenate(
        [
            jnp.concatenate([keyval_weight, query_weight, mixer_weight[:, :HALF]], axis=1),
            jnp.concatenate([vectors, mixer_weight[:, HALF:].reshape(2, 3 * HALF)], axis=1),
        ],
        axis=0,
    )
    block = repeated(block, CHIPS)

    tokens, upstream, expand_weight = lax.optimization_barrier(
        (tokens, upstream, expand_weight, block)
    )[:3]
    w_mine = lax.all_to_all(block, CHIPS, 0, 0, tiled=True).reshape(512, AW)
    both = jnp.concatenate([tokens[0], upstream[0]], axis=1)
    far = lax.ppermute(both[HT:], SEQ, mirror)
    x = jnp.concatenate([tokens[0, :HT], far[:, :D]], axis=0)
    up = jnp.concatenate([upstream[0, :HT], far[:, D:]], axis=0)

    columns = expand_weight.reshape(6, 4, D)
    rows6 = [lax.dynamic_index_in_dim(columns, (z + k) % 4, 1, keepdims=False)[None] for k in range(4)]
    rows6 = [rows6[0]] + [shift(rows6[k], "z", k) for k in (1, 2, 3)]
    rows24 = jnp.zeros((4, 6, D), bf16)
    for k in range(4):
        rows24 = lax.dynamic_update_slice_in_dim(rows24, rows6[k], (z - k) % 4, 0)
    m_all = jnp.concatenate([rows24.reshape(24, D), shrink_weight], axis=1)

    at = jnp.stack([c, z]).astype(jnp.int32)

    feat = jnp.arange(D, dtype=jnp.int32)[:, None]
    e = jnp.arange(1024, dtype=jnp.int32)[None, :]
    chip, r = e % 512 // 8, e % 8
    dev = 2 * chip + jnp.where(e < 512, c, 1 - c)
    tgt = [jnp.where(r < 6, dev * 6 + r, -1)]
    tgt += [jnp.where(r == 6, dev * 6 + k, jnp.where(r == 7, dev * 6 + 3 + k, -1)) for k in range(3)]
    tgt += [jnp.where(r == 7, dev, -1), jnp.where((r == 7) & (dev // 32 == z), dev % 32, -1)]
    tgt = jnp.concatenate(tgt + [jnp.full((2, 1024), -1, jnp.int32)], axis=0)
    cols = tgt.T
    of = jnp.arange(D, dtype=jnp.int32)[None, :]
    rest = of % 384 // 24 * 2 + jnp.where(of < 384, c, 1 - c)
    pm = (feat == (of % 24 // 6 * 32 + rest) * 6 + of % 6).astype(bf16)
    pu = (feat == rest * 24 + of % 24).astype(bf16)
    rest = feat // 24
    perm = (
        of == jnp.where(c == 0, (feat % 24 // 6 * 32 + rest) * 6 + feat % 6, rest * 24 + feat % 24)
    ).astype(bf16)

    lengths = file_lengths[0]
    ends = jnp.cumsum(lengths)
    local = jnp.arange(HT, dtype=jnp.int32)
    pos = jnp.stack([seq * T + local, (NSEQ - 1 - seq) * T + HT + local])
    past = pos[:, :, None] >= ends
    start = jnp.where(
        jnp.all(past, axis=-1), pos, jnp.sum(jnp.where(past, lengths, 0), axis=-1)
    )
    info = jnp.tile(jnp.stack([pos, start], axis=1), (1, 1, H))
    base = pos[:, 0]
    scal = []
    for size in (BK_FORWARD, BK):
        lo = jnp.min(start, axis=1) // size
        end = (base + HT - 1) // size + 1
        u0 = jnp.clip((jnp.max(start, axis=1) + size - 1) // size, lo, end)
        u1 = jnp.clip((base + 1) // size, u0, end)
        scal.append(jnp.stack([lo, u0, u1, end], axis=1))
    scal = jnp.stack(scal).reshape(16).astype(jnp.int32)

    vb = jnp.concatenate([jnp.zeros((HD,), f32), value_bias.astype(f32)])[None]
    w_mine, x, m_all, tgt, cols, pm, pu, perm, info, scal, vb = lax.optimization_barrier(
        (w_mine, x, m_all, tgt, cols, pm, pu, perm, info, scal, vb)
    )
    w_kv = [w_mine[:, :Q0]]
    w_kv.append(shift(w_kv[0], "c", 1))
    kv_out, normed, wkv, vec, chunk = call(
        first_kernel,
        [
            ((NSEQ, T, 2 * HD), bf16),
            ((T, D), bf16),
            ((D, 2 * HD), bf16),
            ((8, D), f32),
            ((T, 1024), bf16),
        ],
        (x, *(Inside(w) for w in w_kv), tgt, vb),
    )
    kv_all = lax.all_to_all(kv_out, SEQ, 0, 0, tiled=True)
    m_all = repeated(after(m_all, kv_out), SLICE)
    normed = after(normed, m_all)
    w_qo = [after(w_mine, kv_out)[:, Q0:]]
    w_qo.append(shift(w_qo[0], "c", 1))
    qt, qr, wq, wnat, npt, eb_row = call(
        query_kernel,
        [
            ((2, 2 * HD, ROWS), bf16),
            ((2, ROWS, 2 * HD), bf16),
            ((D, D), bf16),
            ((D, D), bf16),
            ((1024, T), bf16),
            ((8, D), f32),
        ],
        (normed, Anywhere(w_qo[0]), Anywhere(w_qo[1]), tgt, cols, vec, chunk),
    )
    kv_all, wnat, qt, m_all, up = lax.optimization_barrier((kv_all, wnat, qt, m_all, up))
    m_all = lax.all_to_all(m_all, SLICE, 0, 0, tiled=True).reshape(384, D2)
    ups = spread(up, "z")

    ot, lse, att, hidden, mid, kvs, kt = call(
        forward_kernel,
        [
            ((2, HD, ROWS), f32),
            ((2, 1, ROWS), f32),
            ((T, D), bf16),
            ((T, D), f32),
            ((T, D), bf16),
            ((WINDOW, 2 * HD), bf16),
            ((HD, WINDOW), bf16),
        ],
        (Inside(kv_all), qt, info, x, wnat, vec),
        [scal],
        scratch=[
            pltpu.VMEM((WINDOW, 4 * HD), bf16),
            pltpu.VMEM((VROWS, WINDOW), bf16),
            pltpu.VMEM((2, 4 * HD, ROWS), bf16),
            pltpu.VMEM((2, VROWS, ROWS), f32),
        ],
    )
    m_all, mid, ups = lax.optimization_barrier((m_all, mid, ups))
    m_other = shift(m_all, "c", 1)
    mids = spread(mid, "z")
    we, ws = call(
        weights_kernel,
        [((D, D), bf16, VMEM), ((D, D), bf16, VMEM)],
        (Anywhere(m_all), pm, pu, Anywhere(m_other)),
    )
    *ds, keep, send, act, eb = call(
        mlp_kernel,
        [((T, D), bf16, VMEM)] * 4 + [((4 * T, D2), bf16, VMEM)] * 2 + [((4 * T, D), bf16), ((1, D), f32)],
        (*(Inside(n) for n in mids), Inside(we), eb_row, *(Inside(u) for u in ups), Inside(ws)),
        [at],
        scratch=[pltpu.VMEM((4 * T, D), bf16)] * 3,
    )
    back = [ds[0]] + [shift(ds[k], "z", -k) for k in (1, 2, 3)]
    got = shift(send, "c", 1)
    (g_mlp,) = call(
        mlp_grads_kernel,
        [((D, D), bf16)],
        (perm, Inside(keep), Inside(got)),
    )
    outs = call(result_kernel, [((T, D), bf16)] * 4, (act, Anywhere(ws)))
    back, g_mlp, outs = lax.optimization_barrier((back, g_mlp, outs))
    outs = [outs[0]] + [shift(outs[k], "z", -k) for k in (1, 2, 3)]
    g_mlp = lax.all_to_all(g_mlp.reshape(16, 48, D), SLICE, 0, 0, tiled=True)

    dkv, dq, d_hidden, dh_low, sums = call(
        backward_kernel,
        [((NSEQ, T, 2 * HD), bf16), ((T, D), bf16), ((T, D), f32), ((T, D), bf16, VMEM), ((8, D), f32)],
        (hidden, *(Inside(d) for d in back), up, vec, wnat, ot, qt, lse, kvs, kt, qr, info),
        [scal],
        scratch=[
            pltpu.VMEM((2, 4 * HD, ROWS), bf16),
            pltpu.VMEM((2, 4 * HD, ROWS), bf16),
            pltpu.VMEM((2, ROWS, 2 * HD), bf16),
            pltpu.VMEM((WINDOW, 2 * HD), f32),
            pltpu.VMEM((2, HD, ROWS), f32),
            pltpu.VMEM((WINDOW, 4 * HD), bf16),
        ],
    )
    dkv, dq, dh_low, g_mlp, outs = lax.optimization_barrier((dkv, dq, dh_low, g_mlp, outs))
    got = lax.all_to_all(dkv, SEQ, 0, 0, tiled=True)
    *g_qo, keep, send = call(
        weight_grads_kernel,
        [((512, HALF), bf16)] * 6 + [((24, D), f32)] * 2,
        (cols, att, npt, dq, Inside(dh_low), Anywhere(g_mlp)),
        [at],
        scratch=[pltpu.VMEM((4, 1024, T), bf16)],
    )
    other, far = [shift(g, "c", 1) for g in g_qo[3:]], shift(send, "c", 1)
    result, tokens_grad, both, g_kv, kv_other, shrink_grad, *pieces = call(
        last_kernel,
        [
            ((HT, D), f32),
            ((HT, D), f32),
            ((HT, D2), bf16),
            ((512, Q0), bf16, VMEM),
            ((512, Q0), bf16, VMEM),
            ((24, D), f32),
        ]
        + [((8, D), f32)] * 4,
        (x, vec, dq, wq, wkv, Inside(got), d_hidden, sums, eb, npt, cols, keep, far, hidden, *outs),
        [at],
        scratch=[pltpu.VMEM((4, 8, D), f32)],
    )
    pieces = [pieces[0]] + [shift(pieces[k], "z", k) for k in (1, 2, 3)]
    kv_other = shift(kv_other, "c", 1)
    g_all = jnp.concatenate([g_kv + kv_other] + [a + b for a, b in zip(g_qo, other)], axis=1)
    last = lax.all_to_all(g_all.reshape(64, 8, AW), CHIPS, 0, 0, tiled=True)
    last = jnp.sum(last.astype(f32), axis=0)
    expand_grad = jnp.zeros((6, 4 * D), f32)
    for k in range(4):
        expand_grad = lax.dynamic_update_slice_in_dim(expand_grad, pieces[k][:6], ((z - k) % 4) * D, 1)
    both = lax.ppermute(both, SEQ, mirror).astype(f32)
    result = jnp.concatenate([result, both[:, :D]], axis=0)
    tokens_grad = jnp.concatenate([tokens_grad, both[:, D:]], axis=0)

    mixer_grad = jnp.concatenate([last[:6, O0:], last[6:, Q0:].reshape(6, HALF)], axis=1)
    vecs = [last[7, 6 * k : 6 * k + 6] for k in range(7)]
    return (
        result[None],
        tokens_grad[None],
        vecs[0],
        vecs[1],
        last[:6, Q0:O0],
        vecs[2],
        last[:6, :Q0],
        last[6, HD:Q0],
        mixer_grad,
        vecs[3],
        vecs[4],
        vecs[5],
        expand_grad,
        last[7, 48:72],
        shrink_grad,
        vecs[6],
    )


def solution(mesh):
    grid = Mesh(mesh.devices.reshape(4, 2, 4, 2, 2), SEQ + WIN)
    every = SEQ + WIN
    rows, flat = P(every, None), P(every)
    tokens = P(WIN, SEQ, None)
    return jax.shard_map(
        body,
        mesh=grid,
        in_specs=(
            tokens, P(WIN, None), tokens, flat, flat, rows, flat, rows, P(), rows, flat, flat, flat, rows, flat, rows, flat,
        ),
        out_specs=(
            tokens, tokens, flat, flat, rows, flat, rows, P(), rows, flat, flat, flat, rows, flat, rows, flat,
        ),
        check_vma=False,
    )
```

```python
import functools
import math

import jax
import jax.numpy as jnp
from jax import lax
from jax.experimental import pallas as pl
from jax.experimental.pallas import tpu as pltpu
from jax.sharding import Mesh, PartitionSpec as P

bf16 = jnp.bfloat16
f32 = jnp.float32
D = 768
H = 12
HD = 64
T = 128
HT = 64
WINDOW = 4096
NSEQ = 32
ROWS = H * HT
BK_FORWARD = 512
BK = 256
VROWS = 80
GRP = 256
NEG = -1e30
EPS = 1e-5
SEQ = ("z", "yl", "x")
WIN = ("yh", "c")
ALL = SEQ + WIN
CHIPS = ("z", "yl", "x", "yh")
SLICE = ("yl", "x", "yh")
D2 = 2 * D
Q0, O0, AW = 128, 896, 1280
HALF = D // 2
HBM = pl.BlockSpec(memory_space=pltpu.HBM)
ANY = pl.BlockSpec(memory_space=pl.ANY)
VMEM = pl.BlockSpec(memory_space=pltpu.VMEM)


class Anywhere:
    def __init__(self, array):
        self.array = array


class Inside(Anywhere):
    pass


class Incoming:
    def __init__(self, source, ref, sem):
        self.ref, self.copy = ref, pltpu.make_async_copy(source, ref, sem)
        self.copy.start()

    def ready(self):
        if self.copy is not None:
            self.copy.wait()
            self.copy = None
        return self.ref

    def __getitem__(self, index):
        return self.ready()[index]


class Outgoing:
    def __init__(self, ref, target, sem):
        self.ref, self.copy, self.sent = ref, pltpu.make_async_copy(ref, target, sem), False

    def send(self):
        if not self.sent:
            self.copy.start()
            self.sent = True

    def __getitem__(self, index):
        return self.ref[index]

    def __setitem__(self, index, value):
        self.ref[index] = value


class Plain:
    def __init__(self, ref):
        self.ref = ref

    def ready(self):
        return self.ref

    def send(self):
        pass

    def __getitem__(self, index):
        return self.ref[index]

    def __setitem__(self, index, value):
        self.ref[index] = value


def call(kernel, outs, args, scalars=(), scratch=(), limit=20):
    kinds = [type(a) if isinstance(a, Anywhere) else None for a in args]
    parts = [a.array if isinstance(a, Anywhere) else a for a in args]
    parts = [a if isinstance(a, tuple) else (a, None, None) for a in parts]
    spaces = {None: pltpu.HBM, Inside: pltpu.VMEM}
    arrays = [
        p[0] if kind is Anywhere else pltpu.with_memory_space_constraint(p[0], spaces[kind])
        for p, kind in zip(parts, kinds, strict=True)
    ]
    inner = [len(o) == 3 for o in outs]
    n, m, k = len(arrays), len(outs), len(scalars)

    def shape(array, lo, hi):
        return array.shape if lo is None else array.shape[:-1] + (hi - lo,)

    moved = [i for i, kind in enumerate(kinds) if kind is not Inside]
    left = [i for i, here in enumerate(inner) if not here]

    def run(*refs):
        ins, small, results = refs[:n], refs[n : n + k], refs[n + k : n + k + m]
        rest = list(refs[n + k + m :])
        bufs = dict(zip(moved, rest, strict=False))
        out_bufs = dict(zip(left, rest[len(moved) :], strict=False))
        small_bufs = rest[len(moved) + len(left) :][:k]
        in_sem, out_sem, *extra = rest[len(moved) + len(left) + k :]
        small = [Incoming(r, b, in_sem.at[n + i]) for i, (r, b) in enumerate(zip(small, small_bufs, strict=True))]
        coming = []
        for i, (r, p) in enumerate(zip(ins, parts, strict=True)):
            if i in bufs:
                source = r if p[1] is None else r.at[..., pl.ds(p[1], p[2] - p[1])]
                coming.append(Incoming(source, bufs[i], in_sem.at[i]))
            else:
                coming.append(Plain(r))
        going = [
            Outgoing(out_bufs[i], r, out_sem.at[i]) if i in out_bufs else Plain(r)
            for i, r in enumerate(results)
        ]
        kernel(*coming, *small, *going, *extra)
        for c in coming + small:
            c.ready()
        for g in going:
            g.send()
        for g in going:
            if isinstance(g, Outgoing):
                g.copy.wait()

    specs = {None: HBM, Anywhere: ANY, Inside: VMEM}
    return pl.pallas_call(
        run,
        out_shape=[(pltpu.VMEM if here else pltpu.HBM)(*o[:2]) for o, here in zip(outs, inner, strict=True)],
        in_specs=[specs[kind] for kind in kinds] + [HBM] * k,
        out_specs=[VMEM if here else HBM for here in inner],
        scratch_shapes=[pltpu.VMEM(shape(*parts[i]), parts[i][0].dtype) for i in moved]
        + [pltpu.VMEM(*outs[i]) for i in left]
        + [pltpu.SMEM(a.shape, a.dtype) for a in scalars]
        + [pltpu.SemaphoreType.DMA((n + k,)), pltpu.SemaphoreType.DMA((m,))]
        + list(scratch),
        compiler_params=pltpu.CompilerParams(vmem_limit_bytes=limit * 1024 * 1024),
    )(*arrays, *(pltpu.with_memory_space_constraint(a, pltpu.HBM) for a in scalars))


def dot(a, b):
    return jnp.dot(a, b, preferred_element_type=f32)


def dot_nt(a, b):
    return lax.dot_general(a, b, (((1,), (1,)), ((), ())), preferred_element_type=f32)


def dot_tn(a, b):
    return lax.dot_general(a, b, (((0,), (0,)), ((), ())), preferred_element_type=f32)


def normalize(v):
    mean = jnp.mean(v, axis=-1, keepdims=True)
    centered = v - mean
    spread = jnp.mean(centered * centered, axis=-1, keepdims=True)
    rstd = lax.rsqrt(spread + EPS)
    return centered * rstd, rstd


def norm_back(xhat, rstd, d_out, gain):
    d_hat = d_out * gain
    return rstd * (
        d_hat
        - jnp.mean(d_hat, axis=-1, keepdims=True)
        - xhat * jnp.mean(d_hat * xhat, axis=-1, keepdims=True)
    )


def hot(target, group=1):
    return (lax.broadcasted_iota(jnp.int32, (D, 1), 0) // group == target).astype(bf16)


def hot_rows(target, group=1):
    return (lax.broadcasted_iota(jnp.int32, (1, D), 1) // group == target).astype(bf16)


def vector_places():
    lane = lax.broadcasted_iota(jnp.int32, (T, 1), 0)
    feat = lax.broadcasted_iota(jnp.int32, (1, D), 1)
    return (lane % 6 == feat % 6) & (lane < 48), lane == 48 + feat % 24


def first_kernel(x_ref, wm_ref, wo_ref, tgt_ref, vb_ref, kv_ref, normed_ref, wkv_ref, vec_ref, chunk_ref):
    xhat, _ = normalize(x_ref[...].astype(f32))
    chunk = jnp.concatenate([wm_ref[...].astype(f32).T, wo_ref[...].astype(f32).T], axis=1).astype(bf16)
    places, _ = vector_places()
    found = jnp.where(places, dot_nt(chunk, hot(tgt_ref[4:5, :], 6)), 0.0).astype(bf16)
    lane = lax.broadcasted_iota(jnp.int32, (16, T), 1)
    row = lax.broadcasted_iota(jnp.int32, (16, T), 0)
    vecs = dot(((lane // 6 == row) & (lane < 48)).astype(bf16), found)
    normed = (xhat * vecs[0:1] + vecs[1:2]).astype(bf16)
    wkv = dot(hot(tgt_ref[0:1, :512]), wm_ref[...]) + dot(hot(tgt_ref[0:1, 512:]), wo_ref[...])
    wkv = wkv.astype(bf16)
    kv = (dot(normed, wkv) + vb_ref[...]).astype(bf16)
    for i in range(NSEQ):
        kv_ref[i] = kv
    kv_ref.send()
    normed_ref[...] = normed
    wkv_ref[...] = wkv
    vec_ref[...] = vecs[0:8]
    chunk_ref[...] = chunk


def pack_cols(xt, g):
    return jnp.concatenate(
        [xt[h * HD : (h + 1) * HD, g * HT : (g + 1) * HT] for h in range(H)], axis=1
    )


def pack_rows(x, g):
    return jnp.concatenate(
        [x[g * HT : (g + 1) * HT, h * HD : (h + 1) * HD] for h in range(H)], axis=0
    )


def unpack(y):
    yt = y.T
    return jnp.concatenate([yt[h * HT : (h + 1) * HT] for h in range(H)], axis=1)


def query_kernel(
    normed_ref, wm_ref, wo_ref, tgt_ref, cols_ref, vec_ref, chunk_ref,
    qt_ref, qr_ref, wq_ref, wnat_ref, npt_ref, eb_ref,
):
    halves = ((wm_ref, slice(0, 512)), (wo_ref, slice(512, 1024)))
    picks = [hot(tgt_ref[0:1, at]) for _, at in halves]
    wq_ref[...] = sum(dot(p, w[:, :D]) for p, (w, _) in zip(picks, halves, strict=True)).astype(bf16)
    wq_ref.send()
    wnat_ref[:, :HALF] = sum(dot(p, w[:, D:]) for p, (w, _) in zip(picks, halves, strict=True)).astype(bf16)
    total = jnp.zeros((D, HALF), f32)
    for k in range(3):
        for w, at in halves:
            total = total + dot(hot(tgt_ref[1 + k : 2 + k, at]), w[:, k * HALF : (k + 1) * HALF])
    wnat_ref[:, HALF:] = total.astype(bf16)
    wnat_ref.send()
    q = (dot(normed_ref[...], wq_ref[...]) + vec_ref[2:3]).astype(bf16).astype(f32)
    qt = (q * (math.log2(math.e) / math.sqrt(HD))).T
    q = q * (1.0 / math.sqrt(HD))
    for g in range(2):
        cols = pack_cols(qt, g)
        high = cols.astype(bf16)
        qt_ref[g, :HD, :] = high
        qt_ref[g, HD:, :] = (cols - high.astype(f32)).astype(bf16)
        rows = pack_rows(q, g)
        qr_ref[g] = jnp.concatenate([rows, jnp.zeros((ROWS, HD), f32)], axis=1).astype(bf16)
    npt_ref[...] = dot_nt(hot_rows(cols_ref[:, 0:1]), normed_ref[...]).astype(bf16)
    _, places = vector_places()
    found = jnp.where(places, dot_nt(chunk_ref[...], hot(tgt_ref[5:6, :], 24)), 0.0)
    eb_ref[...] = jnp.broadcast_to(jnp.sum(found, axis=0, keepdims=True), (8, D))


def three_parts(row):
    first = row.astype(bf16)
    rest = row - first.astype(f32)
    second = rest.astype(bf16)
    third = (rest - second.astype(f32)).astype(bf16)
    at = lax.broadcasted_iota(jnp.int32, (16, row.shape[1]), 0)
    out = jnp.where(at == 0, first.astype(f32), 0.0)
    out = jnp.where(at == 1, second.astype(f32), out)
    return jnp.where(at == 2, third.astype(f32), out).astype(bf16)


def open_keys(s, k0, info_ref, g, cols):
    start, pos = info_ref[g, 1:2, cols], info_ref[g, 0:1, cols]
    after_start = lax.broadcasted_iota(jnp.int32, s.shape, 0) - (start - k0)
    return after_start.astype(jnp.uint32) <= (pos - start).astype(jnp.uint32)


def over_blocks(scal_ref, b, block, carry):
    lo, u0, u1, end = scal_ref[b], scal_ref[b + 1], scal_ref[b + 2], scal_ref[b + 3]
    for first, last, masked in ((lo, u0, True), (u0, u1, False), (u1, end, True)):
        carry = lax.fori_loop(
            first, last, lambda kb, value, masked=masked: block(kb, value, masked), carry
        )
    return carry


def spread_keys(kvs_ref, keys_ref):
    keys_ref[:, :T] = kvs_ref[...]
    lane = lax.broadcasted_iota(jnp.int32, (T, T), 1)
    for i in range(NSEQ):
        rows = pl.ds(i * T, T)
        keys_ref[rows, T:] = jnp.where(lane < HD, kvs_ref[rows, :].astype(f32), 1.0).astype(bf16)


def spread_query(qt_ref, rs_ref, g):
    rs_ref[g] = jnp.zeros((4 * HD, ROWS), bf16)
    rs_ref[g, :HD, :] = qt_ref[g, :HD, :]
    rs_ref[g, 2 * HD : 3 * HD, :] = qt_ref[g, HD:, :]


def forward_kernel(
    kv_ref, qt_ref, info_ref, x_ref, wnat_ref, vec_ref, scal_ref,
    ot_ref, lse_ref, att_ref, hid_ref, mid_ref, kvs_ref, kt_ref, keys_ref, vt_ref, rs_ref, acc_ref,
):
    for i in range(NSEQ):
        kvs_ref[pl.ds(i * T, T), :] = jnp.concatenate(
            [kv_ref[i, :HT], kv_ref[NSEQ - 1 - i, HT:]], axis=0
        )
    kvs_ref.send()
    spread_keys(kvs_ref, keys_ref)
    at = lax.broadcasted_iota(jnp.int32, (T, T), 0)
    lane = lax.broadcasted_iota(jnp.int32, (T, T), 1)
    pick = (lane == (at + HD) % T).astype(bf16)
    for i in range(NSEQ // 4):
        rows = pl.ds(i * 4 * T, 4 * T)
        turned = dot_nt(pick, kvs_ref[rows, :]).astype(bf16)
        vt_ref[:HD, rows] = turned[:HD]
        kt_ref[:, rows] = turned[HD:]
    vt_ref[HD:, :] = jnp.ones((VROWS - HD, WINDOW), bf16)
    kt_ref.send()
    acc_ref[...] = jnp.zeros(acc_ref.shape, f32)
    for g in range(2):
        spread_query(qt_ref, rs_ref, g)
    info_ref.ready()
    scal_ref.ready()
    parts = [slice(i * GRP, (i + 1) * GRP) for i in range(ROWS // GRP)]

    for g in range(2):

        def block(kb, carry, masked, g=g):
            k0 = pl.multiple_of(kb * BK_FORWARD, BK_FORWARD)
            keys = keys_ref[pl.ds(k0, BK_FORWARD), :]
            vt = vt_ref[:, pl.ds(k0, BK_FORWARD)]
            scores = [dot(keys, rs_ref[g, :, cols]) for cols in parts]
            new, products = [], []
            for s, cols, m_old in zip(scores, parts, carry, strict=True):
                if masked:
                    s = jnp.where(open_keys(s, k0, info_ref, g, cols), s, NEG)
                m_new = jnp.maximum(m_old, jnp.max(s, axis=0, keepdims=True))
                p = jnp.exp2(s - m_new)
                new.append(m_new)
                products.append((jnp.exp2(m_old - m_new), dot(vt, p.astype(bf16))))
            for cols, (alpha, product) in zip(parts, products, strict=True):
                acc_ref[g, :, cols] = acc_ref[g, :, cols] * alpha + product
            return tuple(new)

        start = tuple(jnp.full((1, GRP), NEG, f32) for _ in parts)
        done = over_blocks(scal_ref, g * 4, block, start)
        for cols, m in zip(parts, done, strict=True):
            total = acc_ref[g, HD : HD + 1, cols]
            ot_ref[g, :, cols] = acc_ref[g, :HD, cols] / total
            lse_ref[g, :, cols] = m + jnp.log2(total)
        att_ref[g * HT : (g + 1) * HT, :] = unpack(ot_ref[g]).astype(bf16)
    ot_ref.send()
    att_ref.send()
    hidden = x_ref[...].astype(f32) + dot(att_ref[...], wnat_ref[...]) + vec_ref[3:4]
    hid_ref[...] = hidden
    hid_ref.send()
    xhat, _ = normalize(hidden)
    mid_ref[...] = (xhat * vec_ref[4:5] + vec_ref[5:6]).astype(bf16)


def weights_kernel(mm_ref, pm_ref, pu_ref, mo_ref, we_ref, ws_ref):
    for out, perm, lo in ((we_ref, pm_ref, 0), (ws_ref, pu_ref, D)):
        cols = pl.ds(lo, D)
        out[...] = (
            dot(perm[:, :384], mm_ref[:, cols]) + dot(perm[:, 384:], mo_ref[:, cols])
        ).astype(bf16)
        out.send()


def mlp_kernel(
    n0, n1, n2, n3, we_ref, row_ref, u0, u1, u2, u3, ws_ref, c_ref,
    d0, d1, d2, d3, keep_ref, send_ref, act_ref, eb_ref, dp_ref, n_ref, u_ref,
):
    for k, (n, u) in enumerate(((n0, u0), (n1, u1), (n2, u2), (n3, u3))):
        u_ref[pl.ds(k * T, T), :] = u[...]
        n_ref[pl.ds(k * T, T), :] = n[...]
    c0 = math.sqrt(2.0 / math.pi)
    for lo in (0, 384):
        cols = pl.ds(lo, 384)
        pre = dot(n_ref[...], we_ref[:, cols]) + row_ref[0:1, cols]
        da = dot_nt(u_ref[...], ws_ref[cols, :])
        sq = pre * pre
        th = jnp.tanh(c0 * pre * (1.0 + 0.044715 * sq))
        up = 0.5 * (1.0 + th)
        act_ref[:, cols] = (pre * up).astype(bf16)
        slope = up + 0.5 * pre * (1.0 - th * th) * (c0 * (1.0 + 3 * 0.044715 * sq))
        dp_ref[:, cols] = (slope * da).astype(bf16)
    act_ref.send()
    eb_ref[...] = jnp.sum(dp_ref[...].astype(f32), axis=0, keepdims=True)
    eb_ref.send()
    dm = dot_nt(dp_ref[...], we_ref[...])
    for k, d in enumerate((d0, d1, d2, d3)):
        d[...] = dm[k * T : (k + 1) * T].astype(bf16)
        d.send()
    first = c_ref[0] == 0
    here, there = (keep_ref, send_ref), (send_ref, keep_ref)
    for when, (a, b) in ((first, here), (jnp.logical_not(first), there)):

        @pl.when(when)
        def _(a=a, b=b):
            a[:, :D] = n_ref[...]
            a[:, D:] = dp_ref[...]
            b[:, :D] = act_ref[...]
            b[:, D:] = u_ref[...]


def result_kernel(act_ref, ws_ref, r0, r1, r2, r3):
    for k, r in enumerate((r0, r1, r2, r3)):
        r[...] = dot(act_ref[k * T : (k + 1) * T, :], ws_ref[...]).astype(bf16)


def mlp_grads_kernel(perm_ref, keep_ref, got_ref, g_ref):
    rows = dot_nt(perm_ref[...], keep_ref[:, :D]).astype(bf16)
    own = dot(rows, keep_ref[:, D:])
    rows = dot_nt(perm_ref[...], got_ref[:, :D]).astype(bf16)
    g_ref[...] = (own + dot(rows, got_ref[:, D:])).astype(bf16)


def backward_kernel(
    hid_ref, d0, d1, d2, d3, up_ref, vec_ref, wnat_ref, ot_ref, qt_ref, lse_ref, kvs_ref, kt_ref, qr_ref, info_ref,
    scal_ref, dkv_ref, dq_ref, dhid_ref, dhl_ref, sums_ref,
    rs_ref, rd_ref, dor_ref, dkv_acc, dqt_ref, keys_ref,
):
    xhat, rstd = normalize(hid_ref[...])
    d_mid = (
        d0[...].astype(f32) + d1[...].astype(f32) + d2[...].astype(f32) + d3[...].astype(f32)
    )
    up = up_ref[...].astype(f32)
    d_hidden = up + norm_back(xhat, rstd, d_mid, vec_ref[4:5])
    dhid_ref[...] = d_hidden
    dhid_ref.send()
    d_low = d_hidden.astype(bf16)
    d_att = dot_nt(d_low, wnat_ref[...]).astype(bf16).astype(f32)
    dhl_ref[...] = d_low
    dhl_ref.send()
    sums_ref[...] = jnp.concatenate(
        [
            jnp.sum(d_hidden, axis=0, keepdims=True),
            jnp.sum(d_mid * xhat, axis=0, keepdims=True),
            jnp.sum(d_mid, axis=0, keepdims=True),
            jnp.sum(up, axis=0, keepdims=True),
            jnp.zeros((4, D), f32),
        ],
        axis=0,
    )
    d_att_t = d_att.T
    for g in range(2):
        cols = pack_cols(d_att_t, g)
        delta = jnp.sum(cols * ot_ref[g], axis=0, keepdims=True)
        rd_ref[g] = jnp.zeros((4 * HD, ROWS), bf16)
        rd_ref[g, HD : 2 * HD, :] = cols.astype(bf16)
        rd_ref[g, 3 * HD : 3 * HD + 16, :] = three_parts(-delta)
        spread_query(qt_ref, rs_ref, g)
        rs_ref[g, 3 * HD : 3 * HD + 16, :] = three_parts(-lse_ref[g])
        rows = pack_rows(d_att, g)
        dor_ref[g] = jnp.concatenate([jnp.zeros((ROWS, HD), f32), rows], axis=1).astype(bf16)
    dkv_acc[...] = jnp.zeros(dkv_acc.shape, f32)
    dqt_ref[...] = jnp.zeros(dqt_ref.shape, f32)
    spread_keys(kvs_ref, keys_ref)
    for ref in (kt_ref, qr_ref, info_ref, scal_ref):
        ref.ready()
    parts = [slice(i * GRP, (i + 1) * GRP) for i in range(ROWS // GRP)]

    for g in range(2):

        def block(kb, carry, masked, g=g):
            k0 = pl.multiple_of(kb * BK, BK)
            keys = keys_ref[pl.ds(k0, BK), :]
            kt = kt_ref[:, pl.ds(k0, BK)]
            acc = dkv_acc[pl.ds(k0, BK), :]
            pairs = [(dot(keys, rs_ref[g, :, cols]), dot(keys, rd_ref[g, :, cols])) for cols in parts]
            terms = []
            for (s, dp), cols in zip(pairs, parts, strict=True):
                p = jnp.exp2(s)
                if masked:
                    p = jnp.where(open_keys(s, k0, info_ref, g, cols), p, 0.0)
                terms.append((p.astype(bf16), (p * dp).astype(bf16)))
            products = []
            for (p, ds), cols in zip(terms, parts, strict=True):
                acc = acc + dot(p, dor_ref[g, cols, :]) + dot(ds, qr_ref[g, cols, :])
                products.append(dot(kt, ds))
            dkv_acc[pl.ds(k0, BK), :] = acc
            for product, cols in zip(products, parts, strict=True):
                dqt_ref[g, :, cols] += product
            return carry

        over_blocks(scal_ref, 8 + g * 4, block, 0)
    for i in range(NSEQ):
        dkv_ref[i, :HT, :] = dkv_acc[pl.ds(i * T, HT), :].astype(bf16)
        dkv_ref[NSEQ - 1 - i, HT:, :] = dkv_acc[pl.ds(i * T + HT, HT), :].astype(bf16)
    dkv_ref.send()
    for g in range(2):
        dq_ref[g * HT : (g + 1) * HT, :] = (unpack(dqt_ref[g]) * (1.0 / math.sqrt(HD))).astype(bf16)


def weight_grads_kernel(
    cols_ref, att_ref, npt_ref, dq_ref, dhl_ref, mlp_ref, wq_ref, hid_ref, vec_ref, r0, r1, r2, r3, c_ref,
    m0, m1, m2, o0, o1, o2, keep_ref, send_ref, dn_ref, dqs_ref, near_ref, far_ref, apt_ref,
):
    for k in range(4):
        apt_ref[k] = dot_nt(hot_rows(cols_ref[:, k : k + 1]), att_ref[...]).astype(bf16)
    later = dhl_ref[:, HALF:]
    for lo, outs in ((512, (o0, o1, o2)), (0, (m0, m1, m2))):
        rows = slice(lo, lo + 512)
        for k, out in enumerate(outs):
            cols = slice(k * HALF, (k + 1) * HALF)
            left, right = (npt_ref[rows, :], dq_ref[:, cols]) if k < 2 else (apt_ref[0, rows, :], dhl_ref[:, :HALF])
            left = jnp.concatenate([left, apt_ref[k + 1, rows, :]], axis=1)
            out[...] = dot(left, jnp.concatenate([right, later], axis=0)).astype(bf16)
            out.send()
    total = mlp_ref[0].astype(f32)
    for i in range(1, 16):
        total = total + mlp_ref[i].astype(f32)
    first = c_ref[0] == 0
    send_ref[...] = jnp.where(first, total[24:], total[:24])
    send_ref.send()
    keep_ref[...] = jnp.where(first, total[:24], total[24:])
    dn_ref[...] = dot_nt(dq_ref[...], wq_ref[...])
    dqs_ref[...] = jnp.broadcast_to(jnp.sum(dq_ref[...].astype(f32), axis=0, keepdims=True), (8, D))
    result = hid_ref[...] + vec_ref[6:7]
    for r in (r0, r1, r2, r3):
        result = result + r[...].astype(f32)
    near_ref[...] = result[:HT]
    far_ref[...] = result[HT:].astype(bf16)


def last_kernel(
    x_ref, vec_ref, dn_ref, dqs_ref, wkv_ref, got_ref, dhid_ref, sums_ref, eb_ref, npt_ref, cols_ref, keep_ref, far_ref,
    res_ref, at_ref,
    near_ref, both_ref, gm_ref, go_ref, shrink_ref, p0, p1, p2, p3, rows_ref,
):
    xhat, rstd = normalize(x_ref[...].astype(f32))
    total = got_ref[0].astype(f32)
    for i in range(1, NSEQ):
        total = total + got_ref[i].astype(f32)
    owned = total.astype(bf16)
    d_normed = dn_ref[...] + dot_nt(owned, wkv_ref[...])
    grad = dhid_ref[...] + norm_back(xhat, rstd, d_normed, vec_ref[0:1])
    near_ref[...] = grad[:HT]
    both_ref[:, D:] = grad[HT:].astype(bf16)
    both_ref[:, :D] = res_ref[...]
    for ref in (near_ref, both_ref):
        ref.send()
    rows = jnp.concatenate(
        [
            jnp.sum(d_normed * xhat, axis=0, keepdims=True),
            jnp.sum(d_normed, axis=0, keepdims=True),
            dqs_ref[0:1],
            sums_ref[0:1],
            sums_ref[1:2],
            sums_ref[2:3],
            sums_ref[3:4],
            jnp.zeros((9, D), f32),
        ],
        axis=0,
    ).astype(bf16)
    places, bias_places = vector_places()
    lane = lax.broadcasted_iota(jnp.int32, (T, 16), 0)
    row = lax.broadcasted_iota(jnp.int32, (T, 16), 1)
    spread_rows = dot(((lane // 6 == row) & (lane < 48)).astype(bf16), rows)
    spread_rows = jnp.where(places, spread_rows, 0.0).astype(bf16)
    bias = jnp.where(bias_places, eb_ref[...], 0.0).astype(bf16)
    out = (
        dot(npt_ref[...], owned)
        + dot_nt(hot_rows(cols_ref[:, 4:5], 6), spread_rows)
        + dot_nt(hot_rows(cols_ref[:, 5:6], 24), bias)
    )
    sixth = lax.broadcasted_iota(jnp.int32, (1024, 1), 0) % 8 == 6
    out = jnp.where(sixth, jnp.sum(owned.astype(f32), axis=0, keepdims=True), out).astype(bf16)
    go_ref[...] = out[512:]
    go_ref.send()
    gm_ref[...] = out[:512]
    gm_ref.send()
    first = at_ref[0] == 0
    shrink_ref[...] = jnp.where(first, far_ref[...], keep_ref[...])
    rows = jnp.where(first, keep_ref[...], far_ref[...])
    for k in range(4):
        rows_ref[k] = jnp.concatenate([rows[6 * k : 6 * k + 6], jnp.zeros((2, D), f32)], axis=0)
    for k, p in enumerate((p0, p1, p2, p3)):
        p[...] = rows_ref[(at_ref[1] + k) % 4]


def shift(value, axis, by):
    size = lax.axis_size(axis)
    return lax.ppermute(value, axis, [(i, (i + by) % size) for i in range(size)])


def after(value, *others):
    return lax.optimization_barrier((value, *others))[0]


def spread(block, axis):
    return [block] + [shift(block, axis, k) for k in (1, 2, 3)]


def repeated(block, axes):
    count = math.prod(lax.axis_size(a) for a in axes)
    return jnp.broadcast_to(block[None], (count,) + block.shape)


def body(
    tokens,
    file_lengths,
    upstream,
    pre_gain,
    pre_shift,
    query_weight,
    query_bias,
    keyval_weight,
    value_bias,
    mixer_weight,
    mixer_bias,
    mid_gain,
    middle_norm_bias,
    expand_weight,
    expand_bias,
    shrink_weight,
    shrink_bias,
):
    z, c = lax.axis_index("z"), lax.axis_index("c")
    seq = lax.axis_index(SEQ)
    mirror = [(i, NSEQ - 1 - i) for i in range(NSEQ)]


    vectors = jnp.concatenate(
        [
            v.reshape(1, 6)
            for v in (
                pre_gain, pre_shift, query_bias, mixer_bias, mid_gain, middle_norm_bias, shrink_bias,
                jnp.zeros((6,), bf16),
            )
        ]
        + [expand_bias.reshape(4, 6)],
        axis=0,
    )
    vectors = jnp.pad(vectors.reshape(1, 72), ((1, 0), (0, T - 72)))
    block = jnp.concatenate(
        [
            jnp.concatenate([keyval_weight, query_weight, mixer_weight[:, :HALF]], axis=1),
            jnp.concatenate([vectors, mixer_weight[:, HALF:].reshape(2, 3 * HALF)], axis=1),
        ],
        axis=0,
    )
    block = repeated(block, CHIPS)

    tokens, upstream, expand_weight = lax.optimization_barrier(
        (tokens, upstream, expand_weight, block)
    )[:3]
    w_mine = lax.all_to_all(block, CHIPS, 0, 0, tiled=True).reshape(512, AW)
    both = jnp.concatenate([tokens[0], upstream[0]], axis=1)
    far = lax.ppermute(both[HT:], SEQ, mirror)
    x = jnp.concatenate([tokens[0, :HT], far[:, :D]], axis=0)
    up = jnp.concatenate([upstream[0, :HT], far[:, D:]], axis=0)

    columns = expand_weight.reshape(6, 4, D)
    rows6 = [lax.dynamic_index_in_dim(columns, (z + k) % 4, 1, keepdims=False)[None] for k in range(4)]
    rows6 = [rows6[0]] + [shift(rows6[k], "z", k) for k in (1, 2, 3)]
    rows24 = jnp.zeros((4, 6, D), bf16)
    for k in range(4):
        rows24 = lax.dynamic_update_slice_in_dim(rows24, rows6[k], (z - k) % 4, 0)
    m_all = jnp.concatenate([rows24.reshape(24, D), shrink_weight], axis=1)

    at = jnp.stack([c, z]).astype(jnp.int32)

    feat = jnp.arange(D, dtype=jnp.int32)[:, None]
    e = jnp.arange(1024, dtype=jnp.int32)[None, :]
    chip, r = e % 512 // 8, e % 8
    dev = 2 * chip + jnp.where(e < 512, c, 1 - c)
    tgt = [jnp.where(r < 6, dev * 6 + r, -1)]
    tgt += [jnp.where(r == 6, dev * 6 + k, jnp.where(r == 7, dev * 6 + 3 + k, -1)) for k in range(3)]
    tgt += [jnp.where(r == 7, dev, -1), jnp.where((r == 7) & (dev // 32 == z), dev % 32, -1)]
    tgt = jnp.concatenate(tgt + [jnp.full((2, 1024), -1, jnp.int32)], axis=0)
    cols = tgt.T
    of = jnp.arange(D, dtype=jnp.int32)[None, :]
    rest = of % 384 // 24 * 2 + jnp.where(of < 384, c, 1 - c)
    pm = (feat == (of % 24 // 6 * 32 + rest) * 6 + of % 6).astype(bf16)
    pu = (feat == rest * 24 + of % 24).astype(bf16)
    rest = feat // 24
    perm = (
        of == jnp.where(c == 0, (feat % 24 // 6 * 32 + rest) * 6 + feat % 6, rest * 24 + feat % 24)
    ).astype(bf16)

    lengths = file_lengths[0]
    ends = jnp.cumsum(lengths)
    local = jnp.arange(HT, dtype=jnp.int32)
    pos = jnp.stack([seq * T + local, (NSEQ - 1 - seq) * T + HT + local])
    past = pos[:, :, None] >= ends
    start = jnp.where(
        jnp.all(past, axis=-1), pos, jnp.sum(jnp.where(past, lengths, 0), axis=-1)
    )
    info = jnp.tile(jnp.stack([pos, start], axis=1), (1, 1, H))
    base = pos[:, 0]
    scal = []
    for size in (BK_FORWARD, BK):
        lo = jnp.min(start, axis=1) // size
        end = (base + HT - 1) // size + 1
        u0 = jnp.clip((jnp.max(start, axis=1) + size - 1) // size, lo, end)
        u1 = jnp.clip((base + 1) // size, u0, end)
        scal.append(jnp.stack([lo, u0, u1, end], axis=1))
    scal = jnp.stack(scal).reshape(16).astype(jnp.int32)

    vb = jnp.concatenate([jnp.zeros((HD,), f32), value_bias.astype(f32)])[None]
    w_mine, x, m_all, tgt, cols, pm, pu, perm, info, scal, vb = lax.optimization_barrier(
        (w_mine, x, m_all, tgt, cols, pm, pu, perm, info, scal, vb)
    )
    w_kv = [w_mine[:, :Q0]]
    w_kv.append(shift(w_kv[0], "c", 1))
    kv_out, normed, wkv, vec, chunk = call(
        first_kernel,
        [
            ((NSEQ, T, 2 * HD), bf16),
            ((T, D), bf16),
            ((D, 2 * HD), bf16),
            ((8, D), f32),
            ((T, 1024), bf16),
        ],
        (x, *(Inside(w) for w in w_kv), tgt, vb),
    )
    kv_all = lax.all_to_all(kv_out, SEQ, 0, 0, tiled=True)
    m_all = repeated(after(m_all, kv_out), SLICE)
    normed = after(normed, m_all)
    w_qo = [after(w_mine, kv_out)[:, Q0:]]
    w_qo.append(shift(w_qo[0], "c", 1))
    qt, qr, wq, wnat, npt, eb_row = call(
        query_kernel,
        [
            ((2, 2 * HD, ROWS), bf16),
            ((2, ROWS, 2 * HD), bf16),
            ((D, D), bf16),
            ((D, D), bf16),
            ((1024, T), bf16),
            ((8, D), f32),
        ],
        (normed, Anywhere(w_qo[0]), Anywhere(w_qo[1]), tgt, cols, vec, chunk),
    )
    kv_all, wnat, qt, m_all, up = lax.optimization_barrier((kv_all, wnat, qt, m_all, up))
    m_all = lax.all_to_all(m_all, SLICE, 0, 0, tiled=True).reshape(384, D2)
    ups = spread(up, "z")

    ot, lse, att, hidden, mid, kvs, kt = call(
        forward_kernel,
        [
            ((2, HD, ROWS), f32),
            ((2, 1, ROWS), f32),
            ((T, D), bf16),
            ((T, D), f32),
            ((T, D), bf16),
            ((WINDOW, 2 * HD), bf16),
            ((HD, WINDOW), bf16),
        ],
        (Inside(kv_all), qt, info, x, wnat, vec),
        [scal],
        scratch=[
            pltpu.VMEM((WINDOW, 4 * HD), bf16),
            pltpu.VMEM((VROWS, WINDOW), bf16),
            pltpu.VMEM((2, 4 * HD, ROWS), bf16),
            pltpu.VMEM((2, VROWS, ROWS), f32),
        ],
    )
    m_all, mid, ups = lax.optimization_barrier((m_all, mid, ups))
    m_other = shift(m_all, "c", 1)
    mids = spread(mid, "z")
    we, ws = call(
        weights_kernel,
        [((D, D), bf16, VMEM), ((D, D), bf16, VMEM)],
        (Anywhere(m_all), pm, pu, Anywhere(m_other)),
    )
    *ds, keep, send, act, eb = call(
        mlp_kernel,
        [((T, D), bf16, VMEM)] * 4 + [((4 * T, D2), bf16, VMEM)] * 2 + [((4 * T, D), bf16), ((1, D), f32)],
        (*(Inside(n) for n in mids), Inside(we), eb_row, *(Inside(u) for u in ups), Inside(ws)),
        [at],
        scratch=[pltpu.VMEM((4 * T, D), bf16)] * 3,
    )
    back = [ds[0]] + [shift(ds[k], "z", -k) for k in (1, 2, 3)]
    got = shift(send, "c", 1)
    (g_mlp,) = call(
        mlp_grads_kernel,
        [((D, D), bf16)],
        (perm, Inside(keep), Inside(got)),
    )
    outs = call(result_kernel, [((T, D), bf16)] * 4, (act, Anywhere(ws)))
    back, g_mlp, outs = lax.optimization_barrier((back, g_mlp, outs))
    outs = [outs[0]] + [shift(outs[k], "z", -k) for k in (1, 2, 3)]
    g_mlp = lax.all_to_all(g_mlp.reshape(16, 48, D), SLICE, 0, 0, tiled=True)

    dkv, dq, d_hidden, dh_low, sums = call(
        backward_kernel,
        [((NSEQ, T, 2 * HD), bf16), ((T, D), bf16), ((T, D), f32), ((T, D), bf16, VMEM), ((8, D), f32)],
        (hidden, *(Inside(d) for d in back), up, vec, wnat, ot, qt, lse, kvs, kt, qr, info),
        [scal],
        scratch=[
            pltpu.VMEM((2, 4 * HD, ROWS), bf16),
            pltpu.VMEM((2, 4 * HD, ROWS), bf16),
            pltpu.VMEM((2, ROWS, 2 * HD), bf16),
            pltpu.VMEM((WINDOW, 2 * HD), f32),
            pltpu.VMEM((2, HD, ROWS), f32),
            pltpu.VMEM((WINDOW, 4 * HD), bf16),
        ],
    )
    dkv, dq, dh_low, g_mlp, outs = lax.optimization_barrier((dkv, dq, dh_low, g_mlp, outs))
    got = lax.all_to_all(dkv, SEQ, 0, 0, tiled=True)
    *g_qo, keep, send, d_query, dq_sum, result, res_far = call(
        weight_grads_kernel,
        [((512, HALF), bf16)] * 6
        + [((24, D), f32)] * 2
        + [((T, D), f32), ((8, D), f32), ((HT, D), f32), ((HT, D), bf16)],
        (cols, att, npt, dq, Inside(dh_low), Anywhere(g_mlp), wq, hidden, vec, *outs),
        [at],
        scratch=[pltpu.VMEM((4, 1024, T), bf16)],
    )
    other, far = [shift(g, "c", 1) for g in g_qo[3:]], shift(send, "c", 1)
    g_qo = [a + b for a, b in zip(g_qo, other)]
    got, *g_qo = lax.optimization_barrier((got, *g_qo))
    tokens_grad, both, g_kv, kv_other, shrink_grad, *pieces = call(
        last_kernel,
        [
            ((HT, D), f32),
            ((HT, D2), bf16),
            ((512, Q0), bf16, VMEM),
            ((512, Q0), bf16, VMEM),
            ((24, D), f32),
        ]
        + [((8, D), f32)] * 4,
        (x, vec, d_query, dq_sum, wkv, Inside(got), d_hidden, sums, eb, npt, cols, keep, far, res_far),
        [at],
        scratch=[pltpu.VMEM((4, 8, D), f32)],
    )
    pieces = [pieces[0]] + [shift(pieces[k], "z", k) for k in (1, 2, 3)]
    kv_other = shift(kv_other, "c", 1)
    g_all = jnp.concatenate([g_kv + kv_other, *g_qo], axis=1)
    last = lax.all_to_all(g_all.reshape(64, 8, AW), CHIPS, 0, 0, tiled=True)
    last = jnp.sum(last.astype(f32), axis=0)
    expand_grad = jnp.zeros((6, 4 * D), f32)
    for k in range(4):
        expand_grad = lax.dynamic_update_slice_in_dim(expand_grad, pieces[k][:6], ((z - k) % 4) * D, 1)
    both = lax.ppermute(both, SEQ, mirror).astype(f32)
    result = jnp.concatenate([result, both[:, :D]], axis=0)
    tokens_grad = jnp.concatenate([tokens_grad, both[:, D:]], axis=0)

    mixer_grad = jnp.concatenate([last[:6, O0:], last[6:, Q0:].reshape(6, HALF)], axis=1)
    vecs = [last[7, 6 * k : 6 * k + 6] for k in range(7)]
    return (
        result[None],
        tokens_grad[None],
        vecs[0],
        vecs[1],
        last[:6, Q0:O0],
        vecs[2],
        last[:6, :Q0],
        last[6, HD:Q0],
        mixer_grad,
        vecs[3],
        vecs[4],
        vecs[5],
        expand_grad,
        last[7, 48:72],
        shrink_grad,
        vecs[6],
    )


def solution(mesh):
    grid = Mesh(mesh.devices.reshape(4, 2, 4, 2, 2), SEQ + WIN)
    every = SEQ + WIN
    rows, flat = P(every, None), P(every)
    tokens = P(WIN, SEQ, None)
    return jax.shard_map(
        body,
        mesh=grid,
        in_specs=(
            tokens, P(WIN, None), tokens, flat, flat, rows, flat, rows, P(), rows, flat, flat, flat, rows, flat, rows, flat,
        ),
        out_specs=(
            tokens, tokens, flat, flat, rows, flat, rows, P(), rows, flat, flat, flat, rows, flat, rows, flat,
        ),
        check_vma=False,
    )
```

```python
import functools
import math

import jax
import jax.numpy as jnp
from jax import lax
from jax.experimental import pallas as pl
from jax.experimental.pallas import tpu as pltpu
from jax.sharding import Mesh, PartitionSpec as P

bf16 = jnp.bfloat16
f32 = jnp.float32
D = 768
H = 12
HD = 64
T = 128
HT = 64
WINDOW = 4096
NSEQ = 32
ROWS = H * HT
BK_FORWARD = 512
BK = 256
VROWS = 80
GRP = 256
NEG = -1e30
EPS = 1e-5
SEQ = ("z", "yl", "x")
WIN = ("yh", "c")
ALL = SEQ + WIN
CHIPS = ("yh", "yl", "x", "z")
SLICE = ("x", "yh", "yl")
WINDOW_ORDER = ("yl", "x", "z")
D2 = 2 * D
Q0, O0, AW = 128, 896, 1280
HALF = D // 2
HBM = pl.BlockSpec(memory_space=pltpu.HBM)
ANY = pl.BlockSpec(memory_space=pl.ANY)
VMEM = pl.BlockSpec(memory_space=pltpu.VMEM)


class Anywhere:
    def __init__(self, array):
        self.array = array


class Inside(Anywhere):
    pass


class Incoming:
    def __init__(self, source, ref, sem):
        self.ref, self.copy = ref, pltpu.make_async_copy(source, ref, sem)
        self.copy.start()

    def ready(self):
        if self.copy is not None:
            self.copy.wait()
            self.copy = None
        return self.ref

    def __getitem__(self, index):
        return self.ready()[index]


class Outgoing:
    def __init__(self, ref, target, sem):
        self.ref, self.copy, self.sent = ref, pltpu.make_async_copy(ref, target, sem), False

    def send(self):
        if not self.sent:
            self.copy.start()
            self.sent = True

    def __getitem__(self, index):
        return self.ref[index]

    def __setitem__(self, index, value):
        self.ref[index] = value


class Plain:
    def __init__(self, ref):
        self.ref = ref

    def ready(self):
        return self.ref

    def send(self):
        pass

    def __getitem__(self, index):
        return self.ref[index]

    def __setitem__(self, index, value):
        self.ref[index] = value


def call(kernel, outs, args, scalars=(), scratch=(), limit=20):
    kinds = [type(a) if isinstance(a, Anywhere) else None for a in args]
    parts = [a.array if isinstance(a, Anywhere) else a for a in args]
    parts = [a if isinstance(a, tuple) else (a, None, None) for a in parts]
    spaces = {None: pltpu.HBM, Inside: pltpu.VMEM}
    arrays = [
        p[0] if kind is Anywhere else pltpu.with_memory_space_constraint(p[0], spaces[kind])
        for p, kind in zip(parts, kinds, strict=True)
    ]
    inner = [len(o) == 3 for o in outs]
    n, m, k = len(arrays), len(outs), len(scalars)

    def shape(array, lo, hi):
        return array.shape if lo is None else array.shape[:-1] + (hi - lo,)

    moved = [i for i, kind in enumerate(kinds) if kind is not Inside]
    left = [i for i, here in enumerate(inner) if not here]

    def run(*refs):
        ins, small, results = refs[:n], refs[n : n + k], refs[n + k : n + k + m]
        rest = list(refs[n + k + m :])
        bufs = dict(zip(moved, rest, strict=False))
        out_bufs = dict(zip(left, rest[len(moved) :], strict=False))
        small_bufs = rest[len(moved) + len(left) :][:k]
        in_sem, out_sem, *extra = rest[len(moved) + len(left) + k :]
        small = [Incoming(r, b, in_sem.at[n + i]) for i, (r, b) in enumerate(zip(small, small_bufs, strict=True))]
        coming = []
        for i, (r, p) in enumerate(zip(ins, parts, strict=True)):
            if i in bufs:
                source = r if p[1] is None else r.at[..., pl.ds(p[1], p[2] - p[1])]
                coming.append(Incoming(source, bufs[i], in_sem.at[i]))
            else:
                coming.append(Plain(r))
        going = [
            Outgoing(out_bufs[i], r, out_sem.at[i]) if i in out_bufs else Plain(r)
            for i, r in enumerate(results)
        ]
        kernel(*coming, *small, *going, *extra)
        for c in coming + small:
            c.ready()
        for g in going:
            g.send()
        for g in going:
            if isinstance(g, Outgoing):
                g.copy.wait()

    specs = {None: HBM, Anywhere: ANY, Inside: VMEM}
    return pl.pallas_call(
        run,
        out_shape=[(pltpu.VMEM if here else pltpu.HBM)(*o[:2]) for o, here in zip(outs, inner, strict=True)],
        in_specs=[specs[kind] for kind in kinds] + [HBM] * k,
        out_specs=[VMEM if here else HBM for here in inner],
        scratch_shapes=[pltpu.VMEM(shape(*parts[i]), parts[i][0].dtype) for i in moved]
        + [pltpu.VMEM(*outs[i]) for i in left]
        + [pltpu.SMEM(a.shape, a.dtype) for a in scalars]
        + [pltpu.SemaphoreType.DMA((n + k,)), pltpu.SemaphoreType.DMA((m,))]
        + list(scratch),
        compiler_params=pltpu.CompilerParams(vmem_limit_bytes=limit * 1024 * 1024),
    )(*arrays, *(pltpu.with_memory_space_constraint(a, pltpu.HBM) for a in scalars))


def chip_of(place):
    return place % 4 * 16 + place // 16 % 2 * 8 + place // 4 % 4 * 2 + place // 32


def rest_of(place):
    return place % 2 * 8 + place // 4 * 2 + place // 2 % 2


def place_of(seq):
    return seq // 4 % 2 * 16 + seq % 4 * 4 + seq // 8


def dot(a, b):
    return jnp.dot(a, b, preferred_element_type=f32)


def dot_nt(a, b):
    return lax.dot_general(a, b, (((1,), (1,)), ((), ())), preferred_element_type=f32)


def dot_tn(a, b):
    return lax.dot_general(a, b, (((0,), (0,)), ((), ())), preferred_element_type=f32)


def normalize(v):
    mean = jnp.mean(v, axis=-1, keepdims=True)
    centered = v - mean
    spread = jnp.mean(centered * centered, axis=-1, keepdims=True)
    rstd = lax.rsqrt(spread + EPS)
    return centered * rstd, rstd


def norm_back(xhat, rstd, d_out, gain):
    d_hat = d_out * gain
    return rstd * (
        d_hat
        - jnp.mean(d_hat, axis=-1, keepdims=True)
        - xhat * jnp.mean(d_hat * xhat, axis=-1, keepdims=True)
    )


def hot(target, group=1):
    return (lax.broadcasted_iota(jnp.int32, (D, 1), 0) // group == target).astype(bf16)


def hot_rows(target, group=1):
    return (lax.broadcasted_iota(jnp.int32, (1, D), 1) // group == target).astype(bf16)


def vector_places():
    lane = lax.broadcasted_iota(jnp.int32, (T, 1), 0)
    feat = lax.broadcasted_iota(jnp.int32, (1, D), 1)
    return (lane % 6 == feat % 6) & (lane < 48), lane == 48 + feat % 24


def first_kernel(x_ref, wm_ref, wo_ref, tgt_ref, vb_ref, kv_ref, normed_ref, wkv_ref, vec_ref, chunk_ref):
    xhat, _ = normalize(x_ref[...].astype(f32))
    chunk = jnp.concatenate([wm_ref[...].astype(f32).T, wo_ref[...].astype(f32).T], axis=1).astype(bf16)
    places, _ = vector_places()
    found = jnp.where(places, dot_nt(chunk, hot(tgt_ref[4:5, :], 6)), 0.0).astype(bf16)
    lane = lax.broadcasted_iota(jnp.int32, (16, T), 1)
    row = lax.broadcasted_iota(jnp.int32, (16, T), 0)
    vecs = dot(((lane // 6 == row) & (lane < 48)).astype(bf16), found)
    normed = (xhat * vecs[0:1] + vecs[1:2]).astype(bf16)
    wkv = dot(hot(tgt_ref[0:1, :512]), wm_ref[...]) + dot(hot(tgt_ref[0:1, 512:]), wo_ref[...])
    wkv = wkv.astype(bf16)
    kv = (dot(normed, wkv) + vb_ref[...]).astype(bf16)
    for i in range(NSEQ):
        kv_ref[i] = kv
    kv_ref.send()
    normed_ref[...] = normed
    wkv_ref[...] = wkv
    vec_ref[...] = vecs[0:8]
    chunk_ref[...] = chunk


def pack_cols(xt, g):
    return jnp.concatenate(
        [xt[h * HD : (h + 1) * HD, g * HT : (g + 1) * HT] for h in range(H)], axis=1
    )


def pack_rows(x, g):
    return jnp.concatenate(
        [x[g * HT : (g + 1) * HT, h * HD : (h + 1) * HD] for h in range(H)], axis=0
    )


def unpack(y):
    yt = y.T
    return jnp.concatenate([yt[h * HT : (h + 1) * HT] for h in range(H)], axis=1)


def query_kernel(
    normed_ref, wm_ref, wo_ref, tgt_ref, cols_ref, vec_ref, chunk_ref,
    qt_ref, qr_ref, wq_ref, wnat_ref, npt_ref, eb_ref,
):
    halves = ((wm_ref, slice(0, 512)), (wo_ref, slice(512, 1024)))
    picks = [hot(tgt_ref[0:1, at]) for _, at in halves]
    wq_ref[...] = sum(dot(p, w[:, :D]) for p, (w, _) in zip(picks, halves, strict=True)).astype(bf16)
    wq_ref.send()
    wnat_ref[:, :HALF] = sum(dot(p, w[:, D:]) for p, (w, _) in zip(picks, halves, strict=True)).astype(bf16)
    total = jnp.zeros((D, HALF), f32)
    for k in range(3):
        for w, at in halves:
            total = total + dot(hot(tgt_ref[1 + k : 2 + k, at]), w[:, k * HALF : (k + 1) * HALF])
    wnat_ref[:, HALF:] = total.astype(bf16)
    wnat_ref.send()
    q = (dot(normed_ref[...], wq_ref[...]) + vec_ref[2:3]).astype(bf16).astype(f32)
    qt = (q * (math.log2(math.e) / math.sqrt(HD))).T
    q = q * (1.0 / math.sqrt(HD))
    for g in range(2):
        cols = pack_cols(qt, g)
        high = cols.astype(bf16)
        qt_ref[g, :HD, :] = high
        qt_ref[g, HD:, :] = (cols - high.astype(f32)).astype(bf16)
        rows = pack_rows(q, g)
        qr_ref[g] = jnp.concatenate([rows, jnp.zeros((ROWS, HD), f32)], axis=1).astype(bf16)
    npt_ref[...] = dot_nt(hot_rows(cols_ref[:, 0:1]), normed_ref[...]).astype(bf16)
    _, places = vector_places()
    found = jnp.where(places, dot_nt(chunk_ref[...], hot(tgt_ref[5:6, :], 24)), 0.0)
    eb_ref[...] = jnp.broadcast_to(jnp.sum(found, axis=0, keepdims=True), (8, D))


def three_parts(row):
    first = row.astype(bf16)
    rest = row - first.astype(f32)
    second = rest.astype(bf16)
    third = (rest - second.astype(f32)).astype(bf16)
    at = lax.broadcasted_iota(jnp.int32, (16, row.shape[1]), 0)
    out = jnp.where(at == 0, first.astype(f32), 0.0)
    out = jnp.where(at == 1, second.astype(f32), out)
    return jnp.where(at == 2, third.astype(f32), out).astype(bf16)


def open_keys(s, k0, info_ref, g, cols):
    start, pos = info_ref[g, 1:2, cols], info_ref[g, 0:1, cols]
    after_start = lax.broadcasted_iota(jnp.int32, s.shape, 0) - (start - k0)
    return after_start.astype(jnp.uint32) <= (pos - start).astype(jnp.uint32)


def over_blocks(scal_ref, b, block, carry):
    lo, u0, u1, end = scal_ref[b], scal_ref[b + 1], scal_ref[b + 2], scal_ref[b + 3]
    for first, last, masked in ((lo, u0, True), (u0, u1, False), (u1, end, True)):
        carry = lax.fori_loop(
            first, last, lambda kb, value, masked=masked: block(kb, value, masked), carry
        )
    return carry


def spread_keys(kvs_ref, keys_ref):
    keys_ref[:, :T] = kvs_ref[...]
    lane = lax.broadcasted_iota(jnp.int32, (T, T), 1)
    for i in range(NSEQ):
        rows = pl.ds(i * T, T)
        keys_ref[rows, T:] = jnp.where(lane < HD, kvs_ref[rows, :].astype(f32), 1.0).astype(bf16)


def spread_query(qt_ref, rs_ref, g):
    rs_ref[g] = jnp.zeros((4 * HD, ROWS), bf16)
    rs_ref[g, :HD, :] = qt_ref[g, :HD, :]
    rs_ref[g, 2 * HD : 3 * HD, :] = qt_ref[g, HD:, :]


def forward_kernel(
    kv_ref, qt_ref, info_ref, x_ref, wnat_ref, vec_ref, scal_ref,
    ot_ref, lse_ref, att_ref, hid_ref, mid_ref, kvs_ref, kt_ref, keys_ref, vt_ref, rs_ref, acc_ref,
):
    for i in range(NSEQ):
        kvs_ref[pl.ds(i * T, T), :] = jnp.concatenate(
            [kv_ref[place_of(i), :HT], kv_ref[place_of(NSEQ - 1 - i), HT:]], axis=0
        )
    kvs_ref.send()
    spread_keys(kvs_ref, keys_ref)
    at = lax.broadcasted_iota(jnp.int32, (T, T), 0)
    lane = lax.broadcasted_iota(jnp.int32, (T, T), 1)
    pick = (lane == (at + HD) % T).astype(bf16)
    for i in range(NSEQ // 4):
        rows = pl.ds(i * 4 * T, 4 * T)
        turned = dot_nt(pick, kvs_ref[rows, :]).astype(bf16)
        vt_ref[:HD, rows] = turned[:HD]
        kt_ref[:, rows] = turned[HD:]
    vt_ref[HD:, :] = jnp.ones((VROWS - HD, WINDOW), bf16)
    kt_ref.send()
    acc_ref[...] = jnp.zeros(acc_ref.shape, f32)
    for g in range(2):
        spread_query(qt_ref, rs_ref, g)
    info_ref.ready()
    scal_ref.ready()
    parts = [slice(i * GRP, (i + 1) * GRP) for i in range(ROWS // GRP)]

    for g in range(2):

        def block(kb, carry, masked, g=g):
            k0 = pl.multiple_of(kb * BK_FORWARD, BK_FORWARD)
            keys = keys_ref[pl.ds(k0, BK_FORWARD), :]
            vt = vt_ref[:, pl.ds(k0, BK_FORWARD)]
            scores = [dot(keys, rs_ref[g, :, cols]) for cols in parts]
            new, products = [], []
            for s, cols, m_old in zip(scores, parts, carry, strict=True):
                if masked:
                    s = jnp.where(open_keys(s, k0, info_ref, g, cols), s, NEG)
                m_new = jnp.maximum(m_old, jnp.max(s, axis=0, keepdims=True))
                p = jnp.exp2(s - m_new)
                new.append(m_new)
                products.append((jnp.exp2(m_old - m_new), dot(vt, p.astype(bf16))))
            for cols, (alpha, product) in zip(parts, products, strict=True):
                acc_ref[g, :, cols] = acc_ref[g, :, cols] * alpha + product
            return tuple(new)

        start = tuple(jnp.full((1, GRP), NEG, f32) for _ in parts)
        done = over_blocks(scal_ref, g * 4, block, start)
        for cols, m in zip(parts, done, strict=True):
            total = acc_ref[g, HD : HD + 1, cols]
            ot_ref[g, :, cols] = acc_ref[g, :HD, cols] / total
            lse_ref[g, :, cols] = m + jnp.log2(total)
        att_ref[g * HT : (g + 1) * HT, :] = unpack(ot_ref[g]).astype(bf16)
    ot_ref.send()
    att_ref.send()
    hidden = x_ref[...].astype(f32) + dot(att_ref[...], wnat_ref[...]) + vec_ref[3:4]
    hid_ref[...] = hidden
    hid_ref.send()
    xhat, _ = normalize(hidden)
    mid_ref[...] = (xhat * vec_ref[4:5] + vec_ref[5:6]).astype(bf16)


def weights_kernel(mm_ref, pm_ref, pu_ref, mo_ref, we_ref, ws_ref):
    for out, perm, lo in ((we_ref, pm_ref, 0), (ws_ref, pu_ref, D)):
        cols = pl.ds(lo, D)
        out[...] = (
            dot(perm[:, :384], mm_ref[:, cols]) + dot(perm[:, 384:], mo_ref[:, cols])
        ).astype(bf16)
        out.send()


def mlp_kernel(
    n0, n1, n2, n3, we_ref, row_ref, u0, u1, u2, u3, ws_ref, c_ref,
    d0, d1, d2, d3, keep_ref, send_ref, act_ref, eb_ref, dp_ref, n_ref, u_ref,
):
    for k, (n, u) in enumerate(((n0, u0), (n1, u1), (n2, u2), (n3, u3))):
        u_ref[pl.ds(k * T, T), :] = u[...]
        n_ref[pl.ds(k * T, T), :] = n[...]
    c0 = math.sqrt(2.0 / math.pi)
    for lo in (0, 384):
        cols = pl.ds(lo, 384)
        pre = dot(n_ref[...], we_ref[:, cols]) + row_ref[0:1, cols]
        da = dot_nt(u_ref[...], ws_ref[cols, :])
        sq = pre * pre
        th = jnp.tanh(c0 * pre * (1.0 + 0.044715 * sq))
        up = 0.5 * (1.0 + th)
        act_ref[:, cols] = (pre * up).astype(bf16)
        slope = up + 0.5 * pre * (1.0 - th * th) * (c0 * (1.0 + 3 * 0.044715 * sq))
        dp_ref[:, cols] = (slope * da).astype(bf16)
    act_ref.send()
    eb_ref[...] = jnp.sum(dp_ref[...].astype(f32), axis=0, keepdims=True)
    eb_ref.send()
    dm = dot_nt(dp_ref[...], we_ref[...])
    for k, d in enumerate((d0, d1, d2, d3)):
        d[...] = dm[k * T : (k + 1) * T].astype(bf16)
        d.send()
    first = c_ref[0] == 0
    here, there = (keep_ref, send_ref), (send_ref, keep_ref)
    for when, (a, b) in ((first, here), (jnp.logical_not(first), there)):

        @pl.when(when)
        def _(a=a, b=b):
            a[:, :D] = n_ref[...]
            a[:, D:] = dp_ref[...]
            b[:, :D] = act_ref[...]
            b[:, D:] = u_ref[...]


def result_kernel(act_ref, ws_ref, r0, r1, r2, r3):
    for k, r in enumerate((r0, r1, r2, r3)):
        r[...] = dot(act_ref[k * T : (k + 1) * T, :], ws_ref[...]).astype(bf16)


def mlp_grads_kernel(perm_ref, keep_ref, got_ref, g_ref):
    rows = dot_nt(perm_ref[...], keep_ref[:, :D]).astype(bf16)
    own = dot(rows, keep_ref[:, D:])
    rows = dot_nt(perm_ref[...], got_ref[:, :D]).astype(bf16)
    g_ref[...] = (own + dot(rows, got_ref[:, D:])).astype(bf16)


def backward_kernel(
    hid_ref, d0, d1, d2, d3, up_ref, vec_ref, wnat_ref, ot_ref, qt_ref, lse_ref, kvs_ref, kt_ref, qr_ref, info_ref,
    scal_ref, dkv_ref, dq_ref, dhid_ref, dhl_ref, sums_ref,
    rs_ref, rd_ref, dor_ref, dkv_acc, dqt_ref, keys_ref,
):
    xhat, rstd = normalize(hid_ref[...])
    d_mid = (
        d0[...].astype(f32) + d1[...].astype(f32) + d2[...].astype(f32) + d3[...].astype(f32)
    )
    up = up_ref[...].astype(f32)
    d_hidden = up + norm_back(xhat, rstd, d_mid, vec_ref[4:5])
    dhid_ref[...] = d_hidden
    dhid_ref.send()
    d_low = d_hidden.astype(bf16)
    d_att = dot_nt(d_low, wnat_ref[...]).astype(bf16).astype(f32)
    dhl_ref[...] = d_low
    dhl_ref.send()
    sums_ref[...] = jnp.concatenate(
        [
            jnp.sum(d_hidden, axis=0, keepdims=True),
            jnp.sum(d_mid * xhat, axis=0, keepdims=True),
            jnp.sum(d_mid, axis=0, keepdims=True),
            jnp.sum(up, axis=0, keepdims=True),
            jnp.zeros((4, D), f32),
        ],
        axis=0,
    )
    d_att_t = d_att.T
    for g in range(2):
        cols = pack_cols(d_att_t, g)
        delta = jnp.sum(cols * ot_ref[g], axis=0, keepdims=True)
        rd_ref[g] = jnp.zeros((4 * HD, ROWS), bf16)
        rd_ref[g, HD : 2 * HD, :] = cols.astype(bf16)
        rd_ref[g, 3 * HD : 3 * HD + 16, :] = three_parts(-delta)
        spread_query(qt_ref, rs_ref, g)
        rs_ref[g, 3 * HD : 3 * HD + 16, :] = three_parts(-lse_ref[g])
        rows = pack_rows(d_att, g)
        dor_ref[g] = jnp.concatenate([jnp.zeros((ROWS, HD), f32), rows], axis=1).astype(bf16)
    dkv_acc[...] = jnp.zeros(dkv_acc.shape, f32)
    dqt_ref[...] = jnp.zeros(dqt_ref.shape, f32)
    spread_keys(kvs_ref, keys_ref)
    for ref in (kt_ref, qr_ref, info_ref, scal_ref):
        ref.ready()
    parts = [slice(i * GRP, (i + 1) * GRP) for i in range(ROWS // GRP)]

    for g in range(2):

        def block(kb, carry, masked, g=g):
            k0 = pl.multiple_of(kb * BK, BK)
            keys = keys_ref[pl.ds(k0, BK), :]
            kt = kt_ref[:, pl.ds(k0, BK)]
            acc = dkv_acc[pl.ds(k0, BK), :]
            pairs = [(dot(keys, rs_ref[g, :, cols]), dot(keys, rd_ref[g, :, cols])) for cols in parts]
            terms = []
            for (s, dp), cols in zip(pairs, parts, strict=True):
                p = jnp.exp2(s)
                if masked:
                    p = jnp.where(open_keys(s, k0, info_ref, g, cols), p, 0.0)
                terms.append((p.astype(bf16), (p * dp).astype(bf16)))
            products = []
            for (p, ds), cols in zip(terms, parts, strict=True):
                acc = acc + dot(p, dor_ref[g, cols, :]) + dot(ds, qr_ref[g, cols, :])
                products.append(dot(kt, ds))
            dkv_acc[pl.ds(k0, BK), :] = acc
            for product, cols in zip(products, parts, strict=True):
                dqt_ref[g, :, cols] += product
            return carry

        over_blocks(scal_ref, 8 + g * 4, block, 0)
    for i in range(NSEQ):
        dkv_ref[place_of(i), :HT, :] = dkv_acc[pl.ds(i * T, HT), :].astype(bf16)
        dkv_ref[place_of(NSEQ - 1 - i), HT:, :] = dkv_acc[pl.ds(i * T + HT, HT), :].astype(bf16)
    dkv_ref.send()
    for g in range(2):
        dq_ref[g * HT : (g + 1) * HT, :] = (unpack(dqt_ref[g]) * (1.0 / math.sqrt(HD))).astype(bf16)


def weight_grads_kernel(
    cols_ref, att_ref, npt_ref, dq_ref, dhl_ref, mlp_ref, wq_ref, hid_ref, vec_ref, r0, r1, r2, r3, c_ref,
    m0, m1, m2, o0, o1, o2, keep_ref, send_ref, dn_ref, dqs_ref, near_ref, far_ref, apt_ref,
):
    for k in range(4):
        apt_ref[k] = dot_nt(hot_rows(cols_ref[:, k : k + 1]), att_ref[...]).astype(bf16)
    later = dhl_ref[:, HALF:]
    for lo, outs in ((512, (o0, o1, o2)), (0, (m0, m1, m2))):
        rows = slice(lo, lo + 512)
        for k, out in enumerate(outs):
            cols = slice(k * HALF, (k + 1) * HALF)
            left, right = (npt_ref[rows, :], dq_ref[:, cols]) if k < 2 else (apt_ref[0, rows, :], dhl_ref[:, :HALF])
            left = jnp.concatenate([left, apt_ref[k + 1, rows, :]], axis=1)
            out[...] = dot(left, jnp.concatenate([right, later], axis=0)).astype(bf16)
            out.send()
    total = mlp_ref[0].astype(f32)
    for i in range(1, 16):
        total = total + mlp_ref[i].astype(f32)
    first = c_ref[0] == 0
    send_ref[...] = jnp.where(first, total[24:], total[:24])
    send_ref.send()
    keep_ref[...] = jnp.where(first, total[:24], total[24:])
    dn_ref[...] = dot_nt(dq_ref[...], wq_ref[...])
    dqs_ref[...] = jnp.broadcast_to(jnp.sum(dq_ref[...].astype(f32), axis=0, keepdims=True), (8, D))
    result = hid_ref[...] + vec_ref[6:7]
    for r in (r0, r1, r2, r3):
        result = result + r[...].astype(f32)
    near_ref[...] = result[:HT]
    far_ref[...] = result[HT:].astype(bf16)


def last_kernel(
    x_ref, vec_ref, dn_ref, dqs_ref, wkv_ref, got_ref, dhid_ref, sums_ref, eb_ref, npt_ref, cols_ref, keep_ref, far_ref,
    res_ref, at_ref,
    near_ref, both_ref, gm_ref, go_ref, shrink_ref, p0, p1, p2, p3, rows_ref,
):
    xhat, rstd = normalize(x_ref[...].astype(f32))
    total = got_ref[0].astype(f32)
    for i in range(1, NSEQ):
        total = total + got_ref[i].astype(f32)
    owned = total.astype(bf16)
    d_normed = dn_ref[...] + dot_nt(owned, wkv_ref[...])
    grad = dhid_ref[...] + norm_back(xhat, rstd, d_normed, vec_ref[0:1])
    near_ref[...] = grad[:HT]
    both_ref[:, D:] = grad[HT:].astype(bf16)
    both_ref[:, :D] = res_ref[...]
    for ref in (near_ref, both_ref):
        ref.send()
    rows = jnp.concatenate(
        [
            jnp.sum(d_normed * xhat, axis=0, keepdims=True),
            jnp.sum(d_normed, axis=0, keepdims=True),
            dqs_ref[0:1],
            sums_ref[0:1],
            sums_ref[1:2],
            sums_ref[2:3],
            sums_ref[3:4],
            jnp.zeros((9, D), f32),
        ],
        axis=0,
    ).astype(bf16)
    places, bias_places = vector_places()
    lane = lax.broadcasted_iota(jnp.int32, (T, 16), 0)
    row = lax.broadcasted_iota(jnp.int32, (T, 16), 1)
    spread_rows = dot(((lane // 6 == row) & (lane < 48)).astype(bf16), rows)
    spread_rows = jnp.where(places, spread_rows, 0.0).astype(bf16)
    bias = jnp.where(bias_places, eb_ref[...], 0.0).astype(bf16)
    out = (
        dot(npt_ref[...], owned)
        + dot_nt(hot_rows(cols_ref[:, 4:5], 6), spread_rows)
        + dot_nt(hot_rows(cols_ref[:, 5:6], 24), bias)
    )
    sixth = lax.broadcasted_iota(jnp.int32, (1024, 1), 0) % 8 == 6
    out = jnp.where(sixth, jnp.sum(owned.astype(f32), axis=0, keepdims=True), out).astype(bf16)
    go_ref[...] = out[512:]
    go_ref.send()
    gm_ref[...] = out[:512]
    gm_ref.send()
    first = at_ref[0] == 0
    shrink_ref[...] = jnp.where(first, far_ref[...], keep_ref[...])
    rows = jnp.where(first, keep_ref[...], far_ref[...])
    for k in range(4):
        rows_ref[k] = jnp.concatenate([rows[6 * k : 6 * k + 6], jnp.zeros((2, D), f32)], axis=0)
    for k, p in enumerate((p0, p1, p2, p3)):
        p[...] = rows_ref[(at_ref[1] + k) % 4]


def shift(value, axis, by):
    size = lax.axis_size(axis)
    return lax.ppermute(value, axis, [(i, (i + by) % size) for i in range(size)])


def after(value, *others):
    return lax.optimization_barrier((value, *others))[0]


def spread(block, axis):
    return [block] + [shift(block, axis, k) for k in (1, 2, 3)]


def repeated(block, axes):
    count = math.prod(lax.axis_size(a) for a in axes)
    return jnp.broadcast_to(block[None], (count,) + block.shape)


def body(
    tokens,
    file_lengths,
    upstream,
    pre_gain,
    pre_shift,
    query_weight,
    query_bias,
    keyval_weight,
    value_bias,
    mixer_weight,
    mixer_bias,
    mid_gain,
    middle_norm_bias,
    expand_weight,
    expand_bias,
    shrink_weight,
    shrink_bias,
):
    z, c = lax.axis_index("z"), lax.axis_index("c")
    seq = lax.axis_index(SEQ)
    mirror = [(i, NSEQ - 1 - i) for i in range(NSEQ)]


    vectors = jnp.concatenate(
        [
            v.reshape(1, 6)
            for v in (
                pre_gain, pre_shift, query_bias, mixer_bias, mid_gain, middle_norm_bias, shrink_bias,
                jnp.zeros((6,), bf16),
            )
        ]
        + [expand_bias.reshape(4, 6)],
        axis=0,
    )
    vectors = jnp.pad(vectors.reshape(1, 72), ((1, 0), (0, T - 72)))
    block = jnp.concatenate(
        [
            jnp.concatenate([keyval_weight, query_weight, mixer_weight[:, :HALF]], axis=1),
            jnp.concatenate([vectors, mixer_weight[:, HALF:].reshape(2, 3 * HALF)], axis=1),
        ],
        axis=0,
    )
    block = repeated(block, CHIPS)

    tokens, upstream, expand_weight = lax.optimization_barrier(
        (tokens, upstream, expand_weight, block)
    )[:3]
    w_mine = lax.all_to_all(block, CHIPS, 0, 0, tiled=True).reshape(512, AW)
    both = jnp.concatenate([tokens[0], upstream[0]], axis=1)
    far = lax.ppermute(both[HT:], SEQ, mirror)
    x = jnp.concatenate([tokens[0, :HT], far[:, :D]], axis=0)
    up = jnp.concatenate([upstream[0, :HT], far[:, D:]], axis=0)

    columns = expand_weight.reshape(6, 4, D)
    rows6 = [lax.dynamic_index_in_dim(columns, (z + k) % 4, 1, keepdims=False)[None] for k in range(4)]
    rows6 = [rows6[0]] + [shift(rows6[k], "z", k) for k in (1, 2, 3)]
    rows24 = jnp.zeros((4, 6, D), bf16)
    for k in range(4):
        rows24 = lax.dynamic_update_slice_in_dim(rows24, rows6[k], (z - k) % 4, 0)
    m_all = jnp.concatenate([rows24.reshape(24, D), shrink_weight], axis=1)

    at = jnp.stack([c, z]).astype(jnp.int32)

    feat = jnp.arange(D, dtype=jnp.int32)[:, None]
    e = jnp.arange(1024, dtype=jnp.int32)[None, :]
    chip, r = chip_of(e % 512 // 8), e % 8
    dev = 2 * chip + jnp.where(e < 512, c, 1 - c)
    tgt = [jnp.where(r < 6, dev * 6 + r, -1)]
    tgt += [jnp.where(r == 6, dev * 6 + k, jnp.where(r == 7, dev * 6 + 3 + k, -1)) for k in range(3)]
    tgt += [jnp.where(r == 7, dev, -1), jnp.where((r == 7) & (dev // 32 == z), dev % 32, -1)]
    tgt = jnp.concatenate(tgt + [jnp.full((2, 1024), -1, jnp.int32)], axis=0)
    cols = tgt.T
    of = jnp.arange(D, dtype=jnp.int32)[None, :]
    rest = rest_of(of % 384 // 24) * 2 + jnp.where(of < 384, c, 1 - c)
    pm = (feat == (of % 24 // 6 * 32 + rest) * 6 + of % 6).astype(bf16)
    pu = (feat == rest * 24 + of % 24).astype(bf16)
    rest = rest_of(feat // 48) * 2 + feat % 48 // 24
    perm = (
        of == jnp.where(c == 0, (feat % 24 // 6 * 32 + rest) * 6 + feat % 6, rest * 24 + feat % 24)
    ).astype(bf16)

    lengths = file_lengths[0]
    ends = jnp.cumsum(lengths)
    local = jnp.arange(HT, dtype=jnp.int32)
    pos = jnp.stack([seq * T + local, (NSEQ - 1 - seq) * T + HT + local])
    past = pos[:, :, None] >= ends
    start = jnp.where(
        jnp.all(past, axis=-1), pos, jnp.sum(jnp.where(past, lengths, 0), axis=-1)
    )
    info = jnp.tile(jnp.stack([pos, start], axis=1), (1, 1, H))
    base = pos[:, 0]
    scal = []
    for size in (BK_FORWARD, BK):
        lo = jnp.min(start, axis=1) // size
        end = (base + HT - 1) // size + 1
        u0 = jnp.clip((jnp.max(start, axis=1) + size - 1) // size, lo, end)
        u1 = jnp.clip((base + 1) // size, u0, end)
        scal.append(jnp.stack([lo, u0, u1, end], axis=1))
    scal = jnp.stack(scal).reshape(16).astype(jnp.int32)

    vb = jnp.concatenate([jnp.zeros((HD,), f32), value_bias.astype(f32)])[None]
    w_mine, x, m_all, tgt, cols, pm, pu, perm, info, scal, vb = lax.optimization_barrier(
        (w_mine, x, m_all, tgt, cols, pm, pu, perm, info, scal, vb)
    )
    w_kv = [w_mine[:, :Q0]]
    w_kv.append(shift(w_kv[0], "c", 1))
    kv_out, normed, wkv, vec, chunk = call(
        first_kernel,
        [
            ((NSEQ, T, 2 * HD), bf16),
            ((T, D), bf16),
            ((D, 2 * HD), bf16),
            ((8, D), f32),
            ((T, 1024), bf16),
        ],
        (x, *(Inside(w) for w in w_kv), tgt, vb),
    )
    kv_all = lax.all_to_all(kv_out, WINDOW_ORDER, 0, 0, tiled=True)
    m_all = repeated(after(m_all, kv_out), SLICE)
    normed = after(normed, m_all)
    w_qo = [after(w_mine, kv_out)[:, Q0:]]
    w_qo.append(shift(w_qo[0], "c", 1))
    qt, qr, wq, wnat, npt, eb_row = call(
        query_kernel,
        [
            ((2, 2 * HD, ROWS), bf16),
            ((2, ROWS, 2 * HD), bf16),
            ((D, D), bf16),
            ((D, D), bf16),
            ((1024, T), bf16),
            ((8, D), f32),
        ],
        (normed, Anywhere(w_qo[0]), Anywhere(w_qo[1]), tgt, cols, vec, chunk),
    )
    kv_all, wnat, qt, m_all, up = lax.optimization_barrier((kv_all, wnat, qt, m_all, up))
    m_all = lax.all_to_all(m_all, SLICE, 0, 0, tiled=True).reshape(384, D2)
    ups = spread(up, "z")

    ot, lse, att, hidden, mid, kvs, kt = call(
        forward_kernel,
        [
            ((2, HD, ROWS), f32),
            ((2, 1, ROWS), f32),
            ((T, D), bf16),
            ((T, D), f32),
            ((T, D), bf16),
            ((WINDOW, 2 * HD), bf16),
            ((HD, WINDOW), bf16),
        ],
        (Inside(kv_all), qt, info, x, wnat, vec),
        [scal],
        scratch=[
            pltpu.VMEM((WINDOW, 4 * HD), bf16),
            pltpu.VMEM((VROWS, WINDOW), bf16),
            pltpu.VMEM((2, 4 * HD, ROWS), bf16),
            pltpu.VMEM((2, VROWS, ROWS), f32),
        ],
    )
    m_all, mid, ups = lax.optimization_barrier((m_all, mid, ups))
    m_other = shift(m_all, "c", 1)
    mids = spread(mid, "z")
    we, ws = call(
        weights_kernel,
        [((D, D), bf16, VMEM), ((D, D), bf16, VMEM)],
        (Anywhere(m_all), pm, pu, Anywhere(m_other)),
    )
    *ds, keep, send, act, eb = call(
        mlp_kernel,
        [((T, D), bf16, VMEM)] * 4 + [((4 * T, D2), bf16, VMEM)] * 2 + [((4 * T, D), bf16), ((1, D), f32)],
        (*(Inside(n) for n in mids), Inside(we), eb_row, *(Inside(u) for u in ups), Inside(ws)),
        [at],
        scratch=[pltpu.VMEM((4 * T, D), bf16)] * 3,
    )
    back = [ds[0]] + [shift(ds[k], "z", -k) for k in (1, 2, 3)]
    got = shift(send, "c", 1)
    (g_mlp,) = call(
        mlp_grads_kernel,
        [((D, D), bf16)],
        (perm, Inside(keep), Inside(got)),
    )
    outs = call(result_kernel, [((T, D), bf16)] * 4, (act, Anywhere(ws)))
    back, g_mlp, outs = lax.optimization_barrier((back, g_mlp, outs))
    outs = [outs[0]] + [shift(outs[k], "z", -k) for k in (1, 2, 3)]
    g_mlp = lax.all_to_all(g_mlp.reshape(16, 48, D), SLICE, 0, 0, tiled=True)

    dkv, dq, d_hidden, dh_low, sums = call(
        backward_kernel,
        [((NSEQ, T, 2 * HD), bf16), ((T, D), bf16), ((T, D), f32), ((T, D), bf16, VMEM), ((8, D), f32)],
        (hidden, *(Inside(d) for d in back), up, vec, wnat, ot, qt, lse, kvs, kt, qr, info),
        [scal],
        scratch=[
            pltpu.VMEM((2, 4 * HD, ROWS), bf16),
            pltpu.VMEM((2, 4 * HD, ROWS), bf16),
            pltpu.VMEM((2, ROWS, 2 * HD), bf16),
            pltpu.VMEM((WINDOW, 2 * HD), f32),
            pltpu.VMEM((2, HD, ROWS), f32),
            pltpu.VMEM((WINDOW, 4 * HD), bf16),
        ],
    )
    dkv, dq, dh_low, g_mlp, outs = lax.optimization_barrier((dkv, dq, dh_low, g_mlp, outs))
    got = lax.all_to_all(dkv, WINDOW_ORDER, 0, 0, tiled=True)
    *g_qo, keep, send, d_query, dq_sum, result, res_far = call(
        weight_grads_kernel,
        [((512, HALF), bf16)] * 6
        + [((24, D), f32)] * 2
        + [((T, D), f32), ((8, D), f32), ((HT, D), f32), ((HT, D), bf16)],
        (cols, att, npt, dq, Inside(dh_low), Anywhere(g_mlp), wq, hidden, vec, *outs),
        [at],
        scratch=[pltpu.VMEM((4, 1024, T), bf16)],
    )
    other, far = [shift(g, "c", 1) for g in g_qo[3:]], shift(send, "c", 1)
    g_qo = [a + b for a, b in zip(g_qo, other)]
    got, *g_qo = lax.optimization_barrier((got, *g_qo))
    tokens_grad, both, g_kv, kv_other, shrink_grad, *pieces = call(
        last_kernel,
        [
            ((HT, D), f32),
            ((HT, D2), bf16),
            ((512, Q0), bf16, VMEM),
            ((512, Q0), bf16, VMEM),
            ((24, D), f32),
        ]
        + [((8, D), f32)] * 4,
        (x, vec, d_query, dq_sum, wkv, Inside(got), d_hidden, sums, eb, npt, cols, keep, far, res_far),
        [at],
        scratch=[pltpu.VMEM((4, 8, D), f32)],
    )
    pieces = [pieces[0]] + [shift(pieces[k], "z", k) for k in (1, 2, 3)]
    kv_other = shift(kv_other, "c", 1)
    g_all = jnp.concatenate([g_kv + kv_other, *g_qo], axis=1)
    last = lax.all_to_all(g_all.reshape(64, 8, AW), CHIPS, 0, 0, tiled=True)
    last = jnp.sum(last.astype(f32), axis=0)
    expand_grad = jnp.zeros((6, 4 * D), f32)
    for k in range(4):
        expand_grad = lax.dynamic_update_slice_in_dim(expand_grad, pieces[k][:6], ((z - k) % 4) * D, 1)
    both = lax.ppermute(both, SEQ, mirror).astype(f32)
    result = jnp.concatenate([result, both[:, :D]], axis=0)
    tokens_grad = jnp.concatenate([tokens_grad, both[:, D:]], axis=0)

    mixer_grad = jnp.concatenate([last[:6, O0:], last[6:, Q0:].reshape(6, HALF)], axis=1)
    vecs = [last[7, 6 * k : 6 * k + 6] for k in range(7)]
    return (
        result[None],
        tokens_grad[None],
        vecs[0],
        vecs[1],
        last[:6, Q0:O0],
        vecs[2],
        last[:6, :Q0],
        last[6, HD:Q0],
        mixer_grad,
        vecs[3],
        vecs[4],
        vecs[5],
        expand_grad,
        last[7, 48:72],
        shrink_grad,
        vecs[6],
    )


def solution(mesh):
    grid = Mesh(mesh.devices.reshape(4, 2, 4, 2, 2), SEQ + WIN)
    every = SEQ + WIN
    rows, flat = P(every, None), P(every)
    tokens = P(WIN, SEQ, None)
    return jax.shard_map(
        body,
        mesh=grid,
        in_specs=(
            tokens, P(WIN, None), tokens, flat, flat, rows, flat, rows, P(), rows, flat, flat, flat, rows, flat, rows, flat,
        ),
        out_specs=(
            tokens, tokens, flat, flat, rows, flat, rows, P(), rows, flat, flat, flat, rows, flat, rows, flat,
        ),
        check_vma=False,
    )
```

```python
import functools
import math

import jax
import jax.numpy as jnp
from jax import lax
from jax.experimental import pallas as pl
from jax.experimental.pallas import tpu as pltpu
from jax.sharding import Mesh, PartitionSpec as P

bf16 = jnp.bfloat16
f32 = jnp.float32
D = 768
H = 12
HD = 64
T = 128
HT = 64
WINDOW = 4096
NSEQ = 32
ROWS = H * HT
BK_FORWARD = 512
BK = 256
VROWS = 80
GRP = 256
NEG = -1e30
EPS = 1e-5
SEQ = ("z", "yl", "x")
WIN = ("yh", "c")
ALL = SEQ + WIN
CHIPS = ("yh", "yl", "x", "z")
SLICE = ("x", "yh", "yl")
WINDOW_ORDER = ("yl", "x", "z")
D2 = 2 * D
Q0, O0, AW = 128, 896, 1280
HALF = D // 2
HBM = pl.BlockSpec(memory_space=pltpu.HBM)
ANY = pl.BlockSpec(memory_space=pl.ANY)
VMEM = pl.BlockSpec(memory_space=pltpu.VMEM)


class Anywhere:
    def __init__(self, array):
        self.array = array


class Inside(Anywhere):
    pass


class Incoming:
    def __init__(self, source, ref, sem):
        self.ref, self.copy = ref, pltpu.make_async_copy(source, ref, sem)
        self.copy.start()

    def ready(self):
        if self.copy is not None:
            self.copy.wait()
            self.copy = None
        return self.ref

    def __getitem__(self, index):
        return self.ready()[index]


class Outgoing:
    def __init__(self, ref, target, sem):
        self.ref, self.copy, self.sent = ref, pltpu.make_async_copy(ref, target, sem), False

    def send(self):
        if not self.sent:
            self.copy.start()
            self.sent = True

    def __getitem__(self, index):
        return self.ref[index]

    def __setitem__(self, index, value):
        self.ref[index] = value


class Plain:
    def __init__(self, ref):
        self.ref = ref

    def ready(self):
        return self.ref

    def send(self):
        pass

    def __getitem__(self, index):
        return self.ref[index]

    def __setitem__(self, index, value):
        self.ref[index] = value


def call(kernel, outs, args, scalars=(), scratch=(), limit=20):
    kinds = [type(a) if isinstance(a, Anywhere) else None for a in args]
    parts = [a.array if isinstance(a, Anywhere) else a for a in args]
    parts = [a if isinstance(a, tuple) else (a, None, None) for a in parts]
    spaces = {None: pltpu.HBM, Inside: pltpu.VMEM}
    arrays = [
        p[0] if kind is Anywhere else pltpu.with_memory_space_constraint(p[0], spaces[kind])
        for p, kind in zip(parts, kinds, strict=True)
    ]
    inner = [len(o) == 3 for o in outs]
    n, m, k = len(arrays), len(outs), len(scalars)

    def shape(array, lo, hi):
        return array.shape if lo is None else array.shape[:-1] + (hi - lo,)

    moved = [i for i, kind in enumerate(kinds) if kind is not Inside]
    left = [i for i, here in enumerate(inner) if not here]

    def run(*refs):
        ins, small, results = refs[:n], refs[n : n + k], refs[n + k : n + k + m]
        rest = list(refs[n + k + m :])
        bufs = dict(zip(moved, rest, strict=False))
        out_bufs = dict(zip(left, rest[len(moved) :], strict=False))
        small_bufs = rest[len(moved) + len(left) :][:k]
        in_sem, out_sem, *extra = rest[len(moved) + len(left) + k :]
        small = [Incoming(r, b, in_sem.at[n + i]) for i, (r, b) in enumerate(zip(small, small_bufs, strict=True))]
        coming = []
        for i, (r, p) in enumerate(zip(ins, parts, strict=True)):
            if i in bufs:
                source = r if p[1] is None else r.at[..., pl.ds(p[1], p[2] - p[1])]
                coming.append(Incoming(source, bufs[i], in_sem.at[i]))
            else:
                coming.append(Plain(r))
        going = [
            Outgoing(out_bufs[i], r, out_sem.at[i]) if i in out_bufs else Plain(r)
            for i, r in enumerate(results)
        ]
        kernel(*coming, *small, *going, *extra)
        for c in coming + small:
            c.ready()
        for g in going:
            g.send()
        for g in going:
            if isinstance(g, Outgoing):
                g.copy.wait()

    specs = {None: HBM, Anywhere: ANY, Inside: VMEM}
    return pl.pallas_call(
        run,
        out_shape=[(pltpu.VMEM if here else pltpu.HBM)(*o[:2]) for o, here in zip(outs, inner, strict=True)],
        in_specs=[specs[kind] for kind in kinds] + [HBM] * k,
        out_specs=[VMEM if here else HBM for here in inner],
        scratch_shapes=[pltpu.VMEM(shape(*parts[i]), parts[i][0].dtype) for i in moved]
        + [pltpu.VMEM(*outs[i]) for i in left]
        + [pltpu.SMEM(a.shape, a.dtype) for a in scalars]
        + [pltpu.SemaphoreType.DMA((n + k,)), pltpu.SemaphoreType.DMA((m,))]
        + list(scratch),
        compiler_params=pltpu.CompilerParams(vmem_limit_bytes=limit * 1024 * 1024),
    )(*arrays, *(pltpu.with_memory_space_constraint(a, pltpu.HBM) for a in scalars))


def chip_of(place):
    return place % 4 * 16 + place // 16 % 2 * 8 + place // 4 % 4 * 2 + place // 32


def rest_of(place):
    return place % 2 * 8 + place // 4 * 2 + place // 2 % 2


def place_of(seq):
    return seq // 4 % 2 * 16 + seq % 4 * 4 + seq // 8


def dot(a, b):
    return jnp.dot(a, b, preferred_element_type=f32)


def dot_nt(a, b):
    return lax.dot_general(a, b, (((1,), (1,)), ((), ())), preferred_element_type=f32)


def dot_tn(a, b):
    return lax.dot_general(a, b, (((0,), (0,)), ((), ())), preferred_element_type=f32)


def normalize(v):
    mean = jnp.mean(v, axis=-1, keepdims=True)
    centered = v - mean
    spread = jnp.mean(centered * centered, axis=-1, keepdims=True)
    rstd = lax.rsqrt(spread + EPS)
    return centered * rstd, rstd


def norm_back(xhat, rstd, d_out, gain):
    d_hat = d_out * gain
    return rstd * (
        d_hat
        - jnp.mean(d_hat, axis=-1, keepdims=True)
        - xhat * jnp.mean(d_hat * xhat, axis=-1, keepdims=True)
    )


def hot(target, group=1):
    return (lax.broadcasted_iota(jnp.int32, (D, 1), 0) // group == target).astype(bf16)


def hot_rows(target, group=1):
    return (lax.broadcasted_iota(jnp.int32, (1, D), 1) // group == target).astype(bf16)


def vector_places():
    lane = lax.broadcasted_iota(jnp.int32, (T, 1), 0)
    feat = lax.broadcasted_iota(jnp.int32, (1, D), 1)
    return (lane % 6 == feat % 6) & (lane < 48), lane == 48 + feat % 24


def first_kernel(x_ref, wm_ref, wo_ref, tgt_ref, vb_ref, kv_ref, normed_ref, wkv_ref, vec_ref, chunk_ref):
    xhat, _ = normalize(x_ref[...].astype(f32))
    chunk = jnp.concatenate([wm_ref[...].astype(f32).T, wo_ref[...].astype(f32).T], axis=1).astype(bf16)
    places, _ = vector_places()
    found = jnp.where(places, dot_nt(chunk, hot(tgt_ref[4:5, :], 6)), 0.0).astype(bf16)
    lane = lax.broadcasted_iota(jnp.int32, (16, T), 1)
    row = lax.broadcasted_iota(jnp.int32, (16, T), 0)
    vecs = dot(((lane // 6 == row) & (lane < 48)).astype(bf16), found)
    normed = (xhat * vecs[0:1] + vecs[1:2]).astype(bf16)
    wkv = dot(hot(tgt_ref[0:1, :512]), wm_ref[...]) + dot(hot(tgt_ref[0:1, 512:]), wo_ref[...])
    wkv = wkv.astype(bf16)
    kv = (dot(normed, wkv) + vb_ref[...]).astype(bf16)
    for i in range(NSEQ):
        kv_ref[i] = kv
    kv_ref.send()
    normed_ref[...] = normed
    wkv_ref[...] = wkv
    vec_ref[...] = vecs[0:8]
    chunk_ref[...] = chunk


def pack_cols(xt, g):
    return jnp.concatenate(
        [xt[h * HD : (h + 1) * HD, g * HT : (g + 1) * HT] for h in range(H)], axis=1
    )


def pack_rows(x, g):
    return jnp.concatenate(
        [x[g * HT : (g + 1) * HT, h * HD : (h + 1) * HD] for h in range(H)], axis=0
    )


def unpack(y):
    yt = y.T
    return jnp.concatenate([yt[h * HT : (h + 1) * HT] for h in range(H)], axis=1)


def query_kernel(
    normed_ref, wm_ref, wo_ref, tgt_ref, cols_ref, vec_ref, chunk_ref,
    qt_ref, qr_ref, wq_ref, wnat_ref, npt_ref, eb_ref,
):
    halves = ((wm_ref, slice(0, 512)), (wo_ref, slice(512, 1024)))
    picks = [hot(tgt_ref[0:1, at]) for _, at in halves]
    wq_ref[...] = sum(dot(p, w[:, :D]) for p, (w, _) in zip(picks, halves, strict=True)).astype(bf16)
    wq_ref.send()
    wnat_ref[:, :HALF] = sum(dot(p, w[:, D:]) for p, (w, _) in zip(picks, halves, strict=True)).astype(bf16)
    total = jnp.zeros((D, HALF), f32)
    for k in range(3):
        for w, at in halves:
            total = total + dot(hot(tgt_ref[1 + k : 2 + k, at]), w[:, k * HALF : (k + 1) * HALF])
    wnat_ref[:, HALF:] = total.astype(bf16)
    wnat_ref.send()
    q = (dot(normed_ref[...], wq_ref[...]) + vec_ref[2:3]).astype(bf16).astype(f32)
    qt = (q * (math.log2(math.e) / math.sqrt(HD))).T
    q = q * (1.0 / math.sqrt(HD))
    for g in range(2):
        cols = pack_cols(qt, g)
        high = cols.astype(bf16)
        qt_ref[g, :HD, :] = high
        qt_ref[g, HD:, :] = (cols - high.astype(f32)).astype(bf16)
        rows = pack_rows(q, g)
        qr_ref[g] = jnp.concatenate([rows, jnp.zeros((ROWS, HD), f32)], axis=1).astype(bf16)
    npt_ref[...] = dot_nt(hot_rows(cols_ref[:, 0:1]), normed_ref[...]).astype(bf16)
    _, places = vector_places()
    found = jnp.where(places, dot_nt(chunk_ref[...], hot(tgt_ref[5:6, :], 24)), 0.0)
    eb_ref[...] = jnp.broadcast_to(jnp.sum(found, axis=0, keepdims=True), (8, D))


def three_parts(row):
    first = row.astype(bf16)
    rest = row - first.astype(f32)
    second = rest.astype(bf16)
    third = (rest - second.astype(f32)).astype(bf16)
    at = lax.broadcasted_iota(jnp.int32, (16, row.shape[1]), 0)
    out = jnp.where(at == 0, first.astype(f32), 0.0)
    out = jnp.where(at == 1, second.astype(f32), out)
    return jnp.where(at == 2, third.astype(f32), out).astype(bf16)


def open_keys(s, k0, info_ref, g, cols):
    start, pos = info_ref[g, 1:2, cols], info_ref[g, 0:1, cols]
    after_start = lax.broadcasted_iota(jnp.int32, s.shape, 0) - (start - k0)
    return after_start.astype(jnp.uint32) <= (pos - start).astype(jnp.uint32)


def over_blocks(scal_ref, b, block, carry):
    lo, u0, u1, end = scal_ref[b], scal_ref[b + 1], scal_ref[b + 2], scal_ref[b + 3]
    for first, last, masked in ((lo, u0, True), (u0, u1, False), (u1, end, True)):
        carry = lax.fori_loop(
            first, last, lambda kb, value, masked=masked: block(kb, value, masked), carry
        )
    return carry


def spread_keys(kvs_ref, keys_ref):
    keys_ref[:, :T] = kvs_ref[...]
    lane = lax.broadcasted_iota(jnp.int32, (T, T), 1)
    for i in range(NSEQ):
        rows = pl.ds(i * T, T)
        keys_ref[rows, T:] = jnp.where(lane < HD, kvs_ref[rows, :].astype(f32), 1.0).astype(bf16)


def spread_query(qt_ref, rs_ref, g):
    rs_ref[g] = jnp.zeros((4 * HD, ROWS), bf16)
    rs_ref[g, :HD, :] = qt_ref[g, :HD, :]
    rs_ref[g, 2 * HD : 3 * HD, :] = qt_ref[g, HD:, :]


def forward_kernel(
    kv_ref, qt_ref, info_ref, x_ref, wnat_ref, vec_ref, scal_ref,
    ot_ref, lse_ref, att_ref, hid_ref, mid_ref, kvs_ref, kt_ref, keys_ref, vt_ref, rs_ref, acc_ref,
):
    for i in range(NSEQ):
        kvs_ref[pl.ds(i * T, T), :] = jnp.concatenate(
            [kv_ref[place_of(i), :HT], kv_ref[place_of(NSEQ - 1 - i), HT:]], axis=0
        )
    kvs_ref.send()
    spread_keys(kvs_ref, keys_ref)
    at = lax.broadcasted_iota(jnp.int32, (T, T), 0)
    lane = lax.broadcasted_iota(jnp.int32, (T, T), 1)
    pick = (lane == (at + HD) % T).astype(bf16)
    for i in range(NSEQ // 4):
        rows = pl.ds(i * 4 * T, 4 * T)
        turned = dot_nt(pick, kvs_ref[rows, :]).astype(bf16)
        vt_ref[:HD, rows] = turned[:HD]
        kt_ref[:, rows] = turned[HD:]
    vt_ref[HD:, :] = jnp.ones((VROWS - HD, WINDOW), bf16)
    kt_ref.send()
    acc_ref[...] = jnp.zeros(acc_ref.shape, f32)
    for g in range(2):
        spread_query(qt_ref, rs_ref, g)
    info_ref.ready()
    scal_ref.ready()
    parts = [slice(i * GRP, (i + 1) * GRP) for i in range(ROWS // GRP)]

    for g in range(2):

        def block(kb, carry, masked, g=g):
            k0 = pl.multiple_of(kb * BK_FORWARD, BK_FORWARD)
            keys = keys_ref[pl.ds(k0, BK_FORWARD), :]
            vt = vt_ref[:, pl.ds(k0, BK_FORWARD)]
            scores = [dot(keys, rs_ref[g, :, cols]) for cols in parts]
            new, products = [], []
            for s, cols, m_old in zip(scores, parts, carry, strict=True):
                if masked:
                    s = jnp.where(open_keys(s, k0, info_ref, g, cols), s, NEG)
                m_new = jnp.maximum(m_old, jnp.max(s, axis=0, keepdims=True))
                p = jnp.exp2(s - m_new)
                new.append(m_new)
                products.append((jnp.exp2(m_old - m_new), dot(vt, p.astype(bf16))))
            for cols, (alpha, product) in zip(parts, products, strict=True):
                acc_ref[g, :, cols] = acc_ref[g, :, cols] * alpha + product
            return tuple(new)

        start = tuple(jnp.full((1, GRP), NEG, f32) for _ in parts)
        done = over_blocks(scal_ref, g * 4, block, start)
        for cols, m in zip(parts, done, strict=True):
            total = acc_ref[g, HD : HD + 1, cols]
            ot_ref[g, :, cols] = acc_ref[g, :HD, cols] / total
            lse_ref[g, :, cols] = m + jnp.log2(total)
        att_ref[g * HT : (g + 1) * HT, :] = unpack(ot_ref[g]).astype(bf16)
    ot_ref.send()
    att_ref.send()
    hidden = x_ref[...].astype(f32) + dot(att_ref[...], wnat_ref[...]) + vec_ref[3:4]
    hid_ref[...] = hidden
    hid_ref.send()
    xhat, _ = normalize(hidden)
    mid_ref[...] = (xhat * vec_ref[4:5] + vec_ref[5:6]).astype(bf16)


def weights_kernel(mm_ref, pm_ref, pu_ref, mo_ref, we_ref, ws_ref):
    for out, perm, lo in ((we_ref, pm_ref, 0), (ws_ref, pu_ref, D)):
        cols = pl.ds(lo, D)
        out[...] = (
            dot(perm[:, :384], mm_ref[:, cols]) + dot(perm[:, 384:], mo_ref[:, cols])
        ).astype(bf16)
        out.send()


def mlp_kernel(
    n0, n1, n2, n3, we_ref, row_ref, u0, u1, u2, u3, ws_ref, c_ref,
    d0, d1, d2, d3, keep_ref, send_ref, act_ref, eb_ref, dp_ref, n_ref, u_ref,
):
    for k, (n, u) in enumerate(((n0, u0), (n1, u1), (n2, u2), (n3, u3))):
        u_ref[pl.ds(k * T, T), :] = u[...]
        n_ref[pl.ds(k * T, T), :] = n[...]
    c0 = math.sqrt(2.0 / math.pi)
    for lo in (0, 384):
        cols = pl.ds(lo, 384)
        pre = dot(n_ref[...], we_ref[:, cols]) + row_ref[0:1, cols]
        da = dot_nt(u_ref[...], ws_ref[cols, :])
        sq = pre * pre
        th = jnp.tanh(c0 * pre * (1.0 + 0.044715 * sq))
        up = 0.5 * (1.0 + th)
        act_ref[:, cols] = (pre * up).astype(bf16)
        slope = up + 0.5 * pre * (1.0 - th * th) * (c0 * (1.0 + 3 * 0.044715 * sq))
        dp_ref[:, cols] = (slope * da).astype(bf16)
    act_ref.send()
    eb_ref[...] = jnp.sum(dp_ref[...].astype(f32), axis=0, keepdims=True)
    eb_ref.send()
    dm = dot_nt(dp_ref[...], we_ref[...])
    for k, d in enumerate((d0, d1, d2, d3)):
        d[...] = dm[k * T : (k + 1) * T].astype(bf16)
        d.send()
    first = c_ref[0] == 0
    here, there = (keep_ref, send_ref), (send_ref, keep_ref)
    for when, (a, b) in ((first, here), (jnp.logical_not(first), there)):

        @pl.when(when)
        def _(a=a, b=b):
            a[:, :D] = n_ref[...]
            a[:, D:] = dp_ref[...]
            b[:, :D] = act_ref[...]
            b[:, D:] = u_ref[...]


def result_kernel(act_ref, ws_ref, r0, r1, r2, r3):
    for k, r in enumerate((r0, r1, r2, r3)):
        r[...] = dot(act_ref[k * T : (k + 1) * T, :], ws_ref[...]).astype(bf16)


def mlp_grads_kernel(perm_ref, keep_ref, got_ref, g_ref):
    rows = dot_nt(perm_ref[...], keep_ref[:, :D]).astype(bf16)
    own = dot(rows, keep_ref[:, D:])
    rows = dot_nt(perm_ref[...], got_ref[:, :D]).astype(bf16)
    g_ref[...] = (own + dot(rows, got_ref[:, D:])).astype(bf16)


def backward_kernel(
    hid_ref, d0, d1, d2, d3, up_ref, vec_ref, wnat_ref, ot_ref, qt_ref, lse_ref, kvs_ref, kt_ref, qr_ref, info_ref,
    scal_ref, dkv_ref, dq_ref, dhid_ref, dhl_ref, sums_ref,
    rs_ref, rd_ref, dor_ref, dkv_acc, dqt_ref, keys_ref,
):
    xhat, rstd = normalize(hid_ref[...])
    d_mid = (
        d0[...].astype(f32) + d1[...].astype(f32) + d2[...].astype(f32) + d3[...].astype(f32)
    )
    up = up_ref[...].astype(f32)
    d_hidden = up + norm_back(xhat, rstd, d_mid, vec_ref[4:5])
    dhid_ref[...] = d_hidden
    dhid_ref.send()
    d_low = d_hidden.astype(bf16)
    d_att = dot_nt(d_low, wnat_ref[...]).astype(bf16).astype(f32)
    dhl_ref[...] = d_low
    dhl_ref.send()
    sums_ref[...] = jnp.concatenate(
        [
            jnp.sum(d_hidden, axis=0, keepdims=True),
            jnp.sum(d_mid * xhat, axis=0, keepdims=True),
            jnp.sum(d_mid, axis=0, keepdims=True),
            jnp.sum(up, axis=0, keepdims=True),
            jnp.zeros((4, D), f32),
        ],
        axis=0,
    )
    d_att_t = d_att.T
    for g in range(2):
        cols = pack_cols(d_att_t, g)
        delta = jnp.sum(cols * ot_ref[g], axis=0, keepdims=True)
        rd_ref[g] = jnp.zeros((4 * HD, ROWS), bf16)
        rd_ref[g, HD : 2 * HD, :] = cols.astype(bf16)
        rd_ref[g, 3 * HD : 3 * HD + 16, :] = three_parts(-delta)
        spread_query(qt_ref, rs_ref, g)
        rs_ref[g, 3 * HD : 3 * HD + 16, :] = three_parts(-lse_ref[g])
        rows = pack_rows(d_att, g)
        dor_ref[g] = jnp.concatenate([jnp.zeros((ROWS, HD), f32), rows], axis=1).astype(bf16)
    dkv_acc[...] = jnp.zeros(dkv_acc.shape, f32)
    dqt_ref[...] = jnp.zeros(dqt_ref.shape, f32)
    spread_keys(kvs_ref, keys_ref)
    for ref in (kt_ref, qr_ref, info_ref, scal_ref):
        ref.ready()
    parts = [slice(i * GRP, (i + 1) * GRP) for i in range(ROWS // GRP)]

    for g in range(2):

        def block(kb, carry, masked, g=g):
            k0 = pl.multiple_of(kb * BK, BK)
            keys = keys_ref[pl.ds(k0, BK), :]
            kt = kt_ref[:, pl.ds(k0, BK)]
            acc = dkv_acc[pl.ds(k0, BK), :]
            pairs = [(dot(keys, rs_ref[g, :, cols]), dot(keys, rd_ref[g, :, cols])) for cols in parts]
            terms = []
            for (s, dp), cols in zip(pairs, parts, strict=True):
                p = jnp.exp2(s)
                if masked:
                    p = jnp.where(open_keys(s, k0, info_ref, g, cols), p, 0.0)
                terms.append((p.astype(bf16), (p * dp).astype(bf16)))
            products = []
            for (p, ds), cols in zip(terms, parts, strict=True):
                acc = acc + dot(p, dor_ref[g, cols, :]) + dot(ds, qr_ref[g, cols, :])
                products.append(dot(kt, ds))
            dkv_acc[pl.ds(k0, BK), :] = acc
            for product, cols in zip(products, parts, strict=True):
                dqt_ref[g, :, cols] += product
            return carry

        over_blocks(scal_ref, 8 + g * 4, block, 0)
    for i in range(NSEQ):
        dkv_ref[place_of(i), :HT, :] = dkv_acc[pl.ds(i * T, HT), :].astype(bf16)
        dkv_ref[place_of(NSEQ - 1 - i), HT:, :] = dkv_acc[pl.ds(i * T + HT, HT), :].astype(bf16)
    dkv_ref.send()
    for g in range(2):
        dq_ref[g * HT : (g + 1) * HT, :] = (unpack(dqt_ref[g]) * (1.0 / math.sqrt(HD))).astype(bf16)


def weight_grads_kernel(
    cols_ref, att_ref, npt_ref, dq_ref, dhl_ref, mlp_ref, wq_ref, hid_ref, vec_ref, r0, r1, r2, r3, c_ref,
    m0, m1, m2, o0, o1, o2, keep_ref, send_ref, dn_ref, dqs_ref, near_ref, far_ref, apt_ref,
):
    for k in range(4):
        apt_ref[k] = dot_nt(hot_rows(cols_ref[:, k : k + 1]), att_ref[...]).astype(bf16)
    later = dhl_ref[:, HALF:]
    for lo, outs in ((512, (o0, o1, o2)), (0, (m0, m1, m2))):
        rows = slice(lo, lo + 512)
        for k, out in enumerate(outs):
            cols = slice(k * HALF, (k + 1) * HALF)
            left, right = (npt_ref[rows, :], dq_ref[:, cols]) if k < 2 else (apt_ref[0, rows, :], dhl_ref[:, :HALF])
            left = jnp.concatenate([left, apt_ref[k + 1, rows, :]], axis=1)
            out[...] = dot(left, jnp.concatenate([right, later], axis=0)).astype(bf16)
            out.send()
    total = mlp_ref[0].astype(f32)
    for i in range(1, 16):
        total = total + mlp_ref[i].astype(f32)
    first = c_ref[0] == 0
    send_ref[...] = jnp.where(first, total[24:], total[:24])
    send_ref.send()
    keep_ref[...] = jnp.where(first, total[:24], total[24:])
    dn_ref[...] = dot_nt(dq_ref[...], wq_ref[...])
    dqs_ref[...] = jnp.broadcast_to(jnp.sum(dq_ref[...].astype(f32), axis=0, keepdims=True), (8, D))
    result = hid_ref[...] + vec_ref[6:7]
    for r in (r0, r1, r2, r3):
        result = result + r[...].astype(f32)
    near_ref[...] = result[:HT]
    far_ref[...] = result[HT:].astype(bf16)


def last_kernel(
    x_ref, vec_ref, dn_ref, dqs_ref, wkv_ref, got_ref, dhid_ref, sums_ref, eb_ref, npt_ref, cols_ref, keep_ref, far_ref,
    res_ref, at_ref,
    near_ref, both_ref, gm_ref, go_ref, shrink_ref, p0, p1, p2, p3, rows_ref,
):
    xhat, rstd = normalize(x_ref[...].astype(f32))
    total = got_ref[0].astype(f32)
    for i in range(1, NSEQ):
        total = total + got_ref[i].astype(f32)
    owned = total.astype(bf16)
    d_normed = dn_ref[...] + dot_nt(owned, wkv_ref[...])
    grad = dhid_ref[...] + norm_back(xhat, rstd, d_normed, vec_ref[0:1])
    near_ref[...] = grad[:HT]
    both_ref[:, D:] = grad[HT:].astype(bf16)
    both_ref[:, :D] = res_ref[...]
    for ref in (near_ref, both_ref):
        ref.send()
    rows = jnp.concatenate(
        [
            jnp.sum(d_normed * xhat, axis=0, keepdims=True),
            jnp.sum(d_normed, axis=0, keepdims=True),
            dqs_ref[0:1],
            sums_ref[0:1],
            sums_ref[1:2],
            sums_ref[2:3],
            sums_ref[3:4],
            jnp.zeros((9, D), f32),
        ],
        axis=0,
    ).astype(bf16)
    places, bias_places = vector_places()
    lane = lax.broadcasted_iota(jnp.int32, (T, 16), 0)
    row = lax.broadcasted_iota(jnp.int32, (T, 16), 1)
    spread_rows = dot(((lane // 6 == row) & (lane < 48)).astype(bf16), rows)
    spread_rows = jnp.where(places, spread_rows, 0.0).astype(bf16)
    bias = jnp.where(bias_places, eb_ref[...], 0.0).astype(bf16)
    out = (
        dot(npt_ref[...], owned)
        + dot_nt(hot_rows(cols_ref[:, 4:5], 6), spread_rows)
        + dot_nt(hot_rows(cols_ref[:, 5:6], 24), bias)
    )
    sixth = lax.broadcasted_iota(jnp.int32, (1024, 1), 0) % 8 == 6
    out = jnp.where(sixth, jnp.sum(owned.astype(f32), axis=0, keepdims=True), out).astype(bf16)
    go_ref[...] = out[512:]
    go_ref.send()
    gm_ref[...] = out[:512]
    gm_ref.send()
    first = at_ref[0] == 0
    shrink_ref[...] = jnp.where(first, far_ref[...], keep_ref[...])
    rows = jnp.where(first, keep_ref[...], far_ref[...])
    for k in range(4):
        rows_ref[k] = jnp.concatenate([rows[6 * k : 6 * k + 6], jnp.zeros((2, D), f32)], axis=0)
    for k, p in enumerate((p0, p1, p2, p3)):
        p[...] = rows_ref[(at_ref[1] + k) % 4]


def shift(value, axis, by):
    size = lax.axis_size(axis)
    return lax.ppermute(value, axis, [(i, (i + by) % size) for i in range(size)])


def after(value, *others):
    return lax.optimization_barrier((value, *others))[0]


def spread(block, axis):
    return [block] + [shift(block, axis, k) for k in (1, 2, 3)]


def repeated(block, axes):
    count = math.prod(lax.axis_size(a) for a in axes)
    return jnp.broadcast_to(block[None], (count,) + block.shape)


def body(
    tokens,
    file_lengths,
    upstream,
    pre_gain,
    pre_shift,
    query_weight,
    query_bias,
    keyval_weight,
    value_bias,
    mixer_weight,
    mixer_bias,
    mid_gain,
    middle_norm_bias,
    expand_weight,
    expand_bias,
    shrink_weight,
    shrink_bias,
):
    z, c = lax.axis_index("z"), lax.axis_index("c")
    seq = lax.axis_index(SEQ)
    mirror = [(i, NSEQ - 1 - i) for i in range(NSEQ)]


    vectors = sum(
        jnp.pad(v, (6 * k, T - 6 * k - v.shape[0]))
        for k, v in (
            (0, pre_gain), (1, pre_shift), (2, query_bias), (3, mixer_bias), (4, mid_gain), (5, middle_norm_bias),
            (6, shrink_bias), (8, expand_bias),
        )
    )
    vectors = jnp.pad(vectors.reshape(1, T), ((1, 0), (0, 0)))
    block = jnp.concatenate(
        [
            jnp.concatenate([keyval_weight, query_weight, mixer_weight[:, :HALF]], axis=1),
            jnp.concatenate([vectors, mixer_weight[:, HALF:].reshape(2, 3 * HALF)], axis=1),
        ],
        axis=0,
    )
    block = repeated(block, CHIPS)

    tokens, upstream, expand_weight = lax.optimization_barrier(
        (tokens, upstream, expand_weight, block)
    )[:3]
    w_mine = lax.all_to_all(block, CHIPS, 0, 0, tiled=True).reshape(512, AW)
    both = jnp.concatenate([tokens[0], upstream[0]], axis=1)
    far = lax.ppermute(both[HT:], SEQ, mirror)
    x = jnp.concatenate([tokens[0, :HT], far[:, :D]], axis=0)
    up = jnp.concatenate([upstream[0, :HT], far[:, D:]], axis=0)

    columns = expand_weight.reshape(6, 4, D)
    rows6 = [lax.dynamic_index_in_dim(columns, (z + k) % 4, 1, keepdims=False)[None] for k in range(4)]
    rows6 = [rows6[0]] + [shift(rows6[k], "z", k) for k in (1, 2, 3)]
    rows24 = jnp.zeros((4, 6, D), bf16)
    for k in range(4):
        rows24 = lax.dynamic_update_slice_in_dim(rows24, rows6[k], (z - k) % 4, 0)
    m_all = jnp.concatenate([rows24.reshape(24, D), shrink_weight], axis=1)

    at = jnp.stack([c, z]).astype(jnp.int32)

    feat = jnp.arange(D, dtype=jnp.int32)[:, None]
    e = jnp.arange(1024, dtype=jnp.int32)[None, :]
    chip, r = chip_of(e % 512 // 8), e % 8
    dev = 2 * chip + jnp.where(e < 512, c, 1 - c)
    tgt = [jnp.where(r < 6, dev * 6 + r, -1)]
    tgt += [jnp.where(r == 6, dev * 6 + k, jnp.where(r == 7, dev * 6 + 3 + k, -1)) for k in range(3)]
    tgt += [jnp.where(r == 7, dev, -1), jnp.where((r == 7) & (dev // 32 == z), dev % 32, -1)]
    tgt = jnp.concatenate(tgt + [jnp.full((2, 1024), -1, jnp.int32)], axis=0)
    cols = tgt.T
    of = jnp.arange(D, dtype=jnp.int32)[None, :]
    rest = rest_of(of % 384 // 24) * 2 + jnp.where(of < 384, c, 1 - c)
    pm = (feat == (of % 24 // 6 * 32 + rest) * 6 + of % 6).astype(bf16)
    pu = (feat == rest * 24 + of % 24).astype(bf16)
    rest = rest_of(feat // 48) * 2 + feat % 48 // 24
    perm = (
        of == jnp.where(c == 0, (feat % 24 // 6 * 32 + rest) * 6 + feat % 6, rest * 24 + feat % 24)
    ).astype(bf16)

    lengths = file_lengths[0]
    ends = jnp.cumsum(lengths)
    local = jnp.arange(HT, dtype=jnp.int32)
    pos = jnp.stack([seq * T + local, (NSEQ - 1 - seq) * T + HT + local])
    past = pos[:, :, None] >= ends
    start = jnp.where(
        jnp.all(past, axis=-1), pos, jnp.sum(jnp.where(past, lengths, 0), axis=-1)
    )
    info = jnp.tile(jnp.stack([pos, start], axis=1), (1, 1, H))
    base = pos[:, 0]
    scal = []
    for size in (BK_FORWARD, BK):
        lo = jnp.min(start, axis=1) // size
        end = (base + HT - 1) // size + 1
        u0 = jnp.clip((jnp.max(start, axis=1) + size - 1) // size, lo, end)
        u1 = jnp.clip((base + 1) // size, u0, end)
        scal.append(jnp.stack([lo, u0, u1, end], axis=1))
    scal = jnp.stack(scal).reshape(16).astype(jnp.int32)

    vb = jnp.concatenate([jnp.zeros((HD,), f32), value_bias.astype(f32)])[None]
    w_mine, x, m_all, tgt, cols, pm, pu, perm, info, scal, vb = lax.optimization_barrier(
        (w_mine, x, m_all, tgt, cols, pm, pu, perm, info, scal, vb)
    )
    w_kv = [w_mine[:, :Q0]]
    w_kv.append(shift(w_kv[0], "c", 1))
    kv_out, normed, wkv, vec, chunk = call(
        first_kernel,
        [
            ((NSEQ, T, 2 * HD), bf16),
            ((T, D), bf16),
            ((D, 2 * HD), bf16),
            ((8, D), f32),
            ((T, 1024), bf16),
        ],
        (x, *(Inside(w) for w in w_kv), tgt, vb),
    )
    kv_all = lax.all_to_all(kv_out, WINDOW_ORDER, 0, 0, tiled=True)
    m_all = repeated(after(m_all, kv_out), SLICE)
    normed = after(normed, m_all)
    w_qo = [after(w_mine, kv_out)[:, Q0:]]
    w_qo.append(shift(w_qo[0], "c", 1))
    qt, qr, wq, wnat, npt, eb_row = call(
        query_kernel,
        [
            ((2, 2 * HD, ROWS), bf16),
            ((2, ROWS, 2 * HD), bf16),
            ((D, D), bf16),
            ((D, D), bf16),
            ((1024, T), bf16),
            ((8, D), f32),
        ],
        (normed, Anywhere(w_qo[0]), Anywhere(w_qo[1]), tgt, cols, vec, chunk),
    )
    kv_all, wnat, qt, m_all, up = lax.optimization_barrier((kv_all, wnat, qt, m_all, up))
    m_all = lax.all_to_all(m_all, SLICE, 0, 0, tiled=True).reshape(384, D2)
    ups = spread(up, "z")

    ot, lse, att, hidden, mid, kvs, kt = call(
        forward_kernel,
        [
            ((2, HD, ROWS), f32),
            ((2, 1, ROWS), f32),
            ((T, D), bf16),
            ((T, D), f32),
            ((T, D), bf16),
            ((WINDOW, 2 * HD), bf16),
            ((HD, WINDOW), bf16),
        ],
        (Inside(kv_all), qt, info, x, wnat, vec),
        [scal],
        scratch=[
            pltpu.VMEM((WINDOW, 4 * HD), bf16),
            pltpu.VMEM((VROWS, WINDOW), bf16),
            pltpu.VMEM((2, 4 * HD, ROWS), bf16),
            pltpu.VMEM((2, VROWS, ROWS), f32),
        ],
    )
    m_all, mid, ups = lax.optimization_barrier((m_all, mid, ups))
    m_other = shift(m_all, "c", 1)
    mids = spread(mid, "z")
    we, ws = call(
        weights_kernel,
        [((D, D), bf16, VMEM), ((D, D), bf16, VMEM)],
        (Anywhere(m_all), pm, pu, Anywhere(m_other)),
    )
    *ds, keep, send, act, eb = call(
        mlp_kernel,
        [((T, D), bf16, VMEM)] * 4 + [((4 * T, D2), bf16, VMEM)] * 2 + [((4 * T, D), bf16), ((1, D), f32)],
        (*(Inside(n) for n in mids), Inside(we), eb_row, *(Inside(u) for u in ups), Inside(ws)),
        [at],
        scratch=[pltpu.VMEM((4 * T, D), bf16)] * 3,
    )
    back = [ds[0]] + [shift(ds[k], "z", -k) for k in (1, 2, 3)]
    got = shift(send, "c", 1)
    (g_mlp,) = call(
        mlp_grads_kernel,
        [((D, D), bf16)],
        (perm, Inside(keep), Inside(got)),
    )
    outs = call(result_kernel, [((T, D), bf16)] * 4, (act, Anywhere(ws)))
    back, g_mlp, outs = lax.optimization_barrier((back, g_mlp, outs))
    outs = [outs[0]] + [shift(outs[k], "z", -k) for k in (1, 2, 3)]
    g_mlp = lax.all_to_all(g_mlp.reshape(16, 48, D), SLICE, 0, 0, tiled=True)

    dkv, dq, d_hidden, dh_low, sums = call(
        backward_kernel,
        [((NSEQ, T, 2 * HD), bf16), ((T, D), bf16), ((T, D), f32), ((T, D), bf16, VMEM), ((8, D), f32)],
        (hidden, *(Inside(d) for d in back), up, vec, wnat, ot, qt, lse, kvs, kt, qr, info),
        [scal],
        scratch=[
            pltpu.VMEM((2, 4 * HD, ROWS), bf16),
            pltpu.VMEM((2, 4 * HD, ROWS), bf16),
            pltpu.VMEM((2, ROWS, 2 * HD), bf16),
            pltpu.VMEM((WINDOW, 2 * HD), f32),
            pltpu.VMEM((2, HD, ROWS), f32),
            pltpu.VMEM((WINDOW, 4 * HD), bf16),
        ],
    )
    dkv, dq, dh_low, g_mlp, outs = lax.optimization_barrier((dkv, dq, dh_low, g_mlp, outs))
    got = lax.all_to_all(dkv, WINDOW_ORDER, 0, 0, tiled=True)
    *g_qo, keep, send, d_query, dq_sum, result, res_far = call(
        weight_grads_kernel,
        [((512, HALF), bf16)] * 6
        + [((24, D), f32)] * 2
        + [((T, D), f32), ((8, D), f32), ((HT, D), f32), ((HT, D), bf16)],
        (cols, att, npt, dq, Inside(dh_low), Anywhere(g_mlp), wq, hidden, vec, *outs),
        [at],
        scratch=[pltpu.VMEM((4, 1024, T), bf16)],
    )
    other, far = [shift(g, "c", 1) for g in g_qo[3:]], shift(send, "c", 1)
    g_qo = [a + b for a, b in zip(g_qo, other)]
    got, *g_qo = lax.optimization_barrier((got, *g_qo))
    tokens_grad, both, g_kv, kv_other, shrink_grad, *pieces = call(
        last_kernel,
        [
            ((HT, D), f32),
            ((HT, D2), bf16),
            ((512, Q0), bf16, VMEM),
            ((512, Q0), bf16, VMEM),
            ((24, D), f32),
        ]
        + [((8, D), f32)] * 4,
        (x, vec, d_query, dq_sum, wkv, Inside(got), d_hidden, sums, eb, npt, cols, keep, far, res_far),
        [at],
        scratch=[pltpu.VMEM((4, 8, D), f32)],
    )
    pieces = [pieces[0]] + [shift(pieces[k], "z", k) for k in (1, 2, 3)]
    kv_other = shift(kv_other, "c", 1)
    g_all = jnp.concatenate([g_kv + kv_other, *g_qo], axis=1)
    last = lax.all_to_all(g_all.reshape(64, 8, AW), CHIPS, 0, 0, tiled=True)
    last = jnp.sum(last.astype(f32), axis=0)
    expand_grad = jnp.zeros((6, 4 * D), f32)
    for k in range(4):
        expand_grad = lax.dynamic_update_slice_in_dim(expand_grad, pieces[k][:6], ((z - k) % 4) * D, 1)
    both = lax.ppermute(both, SEQ, mirror).astype(f32)
    result = jnp.concatenate([result, both[:, :D]], axis=0)
    tokens_grad = jnp.concatenate([tokens_grad, both[:, D:]], axis=0)

    mixer_grad = jnp.concatenate([last[:6, O0:], last[6:, Q0:].reshape(6, HALF)], axis=1)
    vecs = [last[7, 6 * k : 6 * k + 6] for k in range(7)]
    return (
        result[None],
        tokens_grad[None],
        vecs[0],
        vecs[1],
        last[:6, Q0:O0],
        vecs[2],
        last[:6, :Q0],
        last[6, HD:Q0],
        mixer_grad,
        vecs[3],
        vecs[4],
        vecs[5],
        expand_grad,
        last[7, 48:72],
        shrink_grad,
        vecs[6],
    )


def solution(mesh):
    grid = Mesh(mesh.devices.reshape(4, 2, 4, 2, 2), SEQ + WIN)
    every = SEQ + WIN
    rows, flat = P(every, None), P(every)
    tokens = P(WIN, SEQ, None)
    return jax.shard_map(
        body,
        mesh=grid,
        in_specs=(
            tokens, P(WIN, None), tokens, flat, flat, rows, flat, rows, P(), rows, flat, flat, flat, rows, flat, rows, flat,
        ),
        out_specs=(
            tokens, tokens, flat, flat, rows, flat, rows, P(), rows, flat, flat, flat, rows, flat, rows, flat,
        ),
        check_vma=False,
    )
```
